128 devices in a mesh: dp: 8 (over y_hi, x), seq: 16 (over y_lo, z, core).
Axes of the slice: x: 4, y: 4 (y_hi: 2, y_lo: 2; y = y_hi * 2 + y_lo), z: 4, core: 2. Of those that a mesh axis runs over, the one named last changes fastest.
Arguments:
- latents: bfloat16 [8, 16, 256, 1152], P('dp', 'seq'), may hold values from -6 to 6
- cotangent: bfloat16 [8, 16, 256, 1152], P('dp', 'seq'), may hold values from -6 to 6
- modulation: float32 [8, 6, 1152], P('dp'), may hold values from -0.6 to 0.6
- spatial_qkv: bfloat16 [1152, 1728], replicated, may hold values from -0.1875 to 0.1875
- spatial_out: bfloat16 [1152, 576], replicated, may hold values from -0.25 to 0.25
- temporal_qkv: bfloat16 [1152, 1728], replicated, may hold values from -0.1875 to 0.1875
- temporal_out: bfloat16 [1152, 576], replicated, may hold values from -0.25 to 0.25
Outputs:
- grad_latents: bfloat16 [8, 16, 256, 1152], P('dp', 'seq')
- grad_modulation: float32 [8, 6, 1152], P('dp')
- spatial_dqkv: float32 [1152, 1728], P(('dp', 'seq'))
- spatial_dout: float32 [1152, 576], P(('dp', 'seq'))
- temporal_dqkv: float32 [1152, 1728], P(('dp', 'seq'))
- temporal_dout: float32 [1152, 576], P(('dp', 'seq'))
The draws below stay inside these ranges and needn't reach their ends.
All inputs are finite; a program needn't handle non-finite values.
Results may differ from the reference program's by a relative error of at most 0.018.
Values may be sent and summed in bfloat16 or wider, within the bound.
A program may use at most 128 MiB of HBM per device.

```python
from functools import partial
import jax
import jax.numpy as jnp
from jax import lax

D = 1152
HEADS = 8
HEAD_DIM = 72
FRAMES = 16
POS = 256
HE = 576
CLIPS_ALL = 8


def shard_levels(key, extent, cuts, low, high):
    factor_of = 1.0
    for axis_at, parts in cuts:
        heights = jax.random.uniform(jax.random.fold_in(jax.random.fold_in(key, 6), axis_at), (parts,), jnp.float32, low / len(cuts), high / len(cuts))
        factor_of = factor_of * jnp.repeat(jnp.exp(heights), extent[axis_at] // parts).reshape((-1,) + (1,) * (len(extent) - 1 - axis_at))
    return factor_of


def scatter_about(key, dims, scale, bound, cuts=(), dtype=jnp.bfloat16):
    entries = scale * jax.random.normal(key, dims, jnp.float32)
    if cuts:
        entries = entries * shard_levels(key, dims, cuts, -0.22, 0.18)
    return jnp.clip(entries, -bound, bound).astype(dtype)


def setup_inputs(seed: int = 0) -> dict:
    arg_keys = jax.random.split(jax.random.key(seed), 8)
    return {
        "latents": scatter_about(arg_keys[0], (CLIPS_ALL, FRAMES, POS, D), 1.0, 6.0, ((0, 8), (1, 16))),
        "cotangent": scatter_about(arg_keys[1], (CLIPS_ALL, FRAMES, POS, D), 1.0, 6.0, ((0, 8), (1, 16))),
        "modulation": jnp.clip(jax.random.uniform(arg_keys[2], (CLIPS_ALL, 6, D), jnp.float32, -0.6, 0.6) * shard_levels(arg_keys[2], (CLIPS_ALL, 6, D), ((0, 8),), -0.4, 0.0), -0.6, 0.6),
        "spatial_qkv": scatter_about(arg_keys[3], (D, 3 * HE), D ** -0.5, 0.1875),
        "spatial_out": scatter_about(arg_keys[4], (D, HE), HE ** -0.5, 0.25),
        "temporal_qkv": scatter_about(arg_keys[5], (D, 3 * HE), D ** -0.5, 0.1875),
        "temporal_out": scatter_about(arg_keys[6], (D, HE), HE ** -0.5, 0.25),
    }


EPSILON = 1e-06

def norm_modulate(signal, offset, stretch):
    average = lax.optimization_barrier(jnp.mean(signal, axis=-1, keepdims=True))
    centred = signal - average
    spread = lax.optimization_barrier(jnp.mean(centred * centred, axis=-1, keepdims=True))
    normed = centred * lax.rsqrt(spread + EPSILON)
    return (normed * (1.0 + stretch) + offset).astype(jnp.bfloat16)

def matmul(former, latter):
    return jnp.dot(former, latter, preferred_element_type=jnp.float32)

def matmul_nt(former, latter):
    return jnp.dot(former, latter.T, preferred_element_type=jnp.float32)

def matmul_tn(former, latter):
    return jnp.dot(former.T, latter, preferred_element_type=jnp.float32)

def attend(packed, over_frames):
    leading = packed.shape[:3]
    stacked = packed.reshape(leading + (3, HEADS, HEAD_DIM)).astype(jnp.float32)
    query_rows = stacked[:, :, :, 0]
    key_rows = stacked[:, :, :, 1]
    value_rows = stacked[:, :, :, 2]
    factor = HEAD_DIM ** (-0.5)
    if over_frames:
        scores = jnp.einsum('cfphe,cgphe->cphfg', query_rows, key_rows)
    else:
        scores = jnp.einsum('cfphe,cfqhe->cfhpq', query_rows, key_rows)
    raised = jnp.exp(scores * factor)
    weights = (raised / lax.optimization_barrier(jnp.sum(raised, axis=-1, keepdims=True))).astype(jnp.bfloat16)
    if over_frames:
        attended = jnp.einsum('cphfg,cgphe->cfphe', weights.astype(jnp.float32), value_rows)
    else:
        attended = jnp.einsum('cfhpq,cfqhe->cfphe', weights.astype(jnp.float32), value_rows)
    return attended.reshape(leading + (HEADS * HEAD_DIM,)).astype(jnp.bfloat16)

def sublayer_forward(signal, offset, stretch, gating, qkv_weight, out_weight, over_frames):
    widened = signal.astype(jnp.float32)
    modulated, norm_back = jax.vjp(norm_modulate, widened, offset, stretch)
    channels = signal.shape[-1]
    flattened = modulated.reshape(-1, channels)
    packed = matmul(flattened, qkv_weight).astype(jnp.bfloat16).reshape(signal.shape[:3] + (-1,))
    attended, core_back = jax.vjp(partial(attend, over_frames=over_frames), packed)
    branch = matmul_nt(attended.reshape(-1, attended.shape[-1]), out_weight)
    result = (widened + gating * branch.reshape(signal.shape)).astype(jnp.bfloat16)
    return (result, (flattened, attended, branch, norm_back, core_back))

def sublayer_backward(stashed, cotangent, gating, qkv_weight, out_weight):
    flattened, attended, branch, norm_back, core_back = stashed
    upstream = cotangent.astype(jnp.float32)
    clips_here = upstream.shape[0]
    channels = upstream.shape[-1]
    d_gate = lax.optimization_barrier(jnp.sum((upstream.reshape(-1, channels) * branch).reshape(clips_here, -1, channels), axis=1))
    d_branch = (gating * upstream).astype(jnp.bfloat16).reshape(-1, channels)
    d_mixed = matmul(d_branch, out_weight).astype(jnp.bfloat16).reshape(attended.shape)
    d_packed, = core_back(d_mixed)
    d_rows = d_packed.reshape(-1, d_packed.shape[-1])
    d_modulated = matmul_nt(d_rows, qkv_weight).astype(jnp.bfloat16).reshape(upstream.shape)
    d_signal, d_offset, d_stretch = norm_back(d_modulated)
    moments = jnp.stack([d_offset.reshape(clips_here, channels), d_stretch.reshape(clips_here, channels), d_gate], axis=1)
    grad_terms = (flattened, d_rows, d_branch, attended.reshape(-1, attended.shape[-1]))
    return (upstream + d_signal, moments, grad_terms)

def reference(latents, cotangent, modulation, spatial_qkv, spatial_out, temporal_qkv, temporal_out):
    channels = latents.shape[-1]

    def one_clip(totals, inputs):
        signal, upstream, settings = inputs
        pieces = settings.reshape(1, 6, 1, 1, channels)
        hidden, spatial_saved = sublayer_forward(signal[None], pieces[:, 0], pieces[:, 1], pieces[:, 2], spatial_qkv, spatial_out, False)
        unused_out, temporal_saved = sublayer_forward(hidden, pieces[:, 3], pieces[:, 4], pieces[:, 5], temporal_qkv, temporal_out, True)
        grad_hidden, temporal_moments, temporal_terms = sublayer_backward(temporal_saved, upstream[None], pieces[:, 5], temporal_qkv, temporal_out)
        grad_field, spatial_moments, spatial_terms = sublayer_backward(spatial_saved, grad_hidden.astype(jnp.bfloat16), pieces[:, 2], spatial_qkv, spatial_out)
        new_totals = (totals[0] + matmul_tn(spatial_terms[0], spatial_terms[1]), totals[1] + matmul_tn(spatial_terms[2], spatial_terms[3]), totals[2] + matmul_tn(temporal_terms[0], temporal_terms[1]), totals[3] + matmul_tn(temporal_terms[2], temporal_terms[3]))
        moments = jnp.concatenate([spatial_moments, temporal_moments], axis=1)[0]
        return (new_totals, (grad_field[0].astype(jnp.bfloat16), moments))
    initial = (jnp.zeros(spatial_qkv.shape, jnp.float32), jnp.zeros(spatial_out.shape, jnp.float32), jnp.zeros(temporal_qkv.shape, jnp.float32), jnp.zeros(temporal_out.shape, jnp.float32))
    totals, outputs = lax.scan(one_clip, initial, (latents, cotangent, modulation))
    grad_latents, grad_modulation = outputs
    return (grad_latents, grad_modulation, totals[0] / CLIPS_ALL, totals[1] / CLIPS_ALL, totals[2] / CLIPS_ALL, totals[3] / CLIPS_ALL)
```

```python
import functools

import jax
import jax.numpy as jnp
from jax import lax
from jax.experimental import pallas as pl
from jax.experimental.pallas import tpu as pltpu
from jax.sharding import PartitionSpec as P

HEADS = 8
HEAD_DIM = 72
HE = HEADS * HEAD_DIM
PACKED = 3 * HE
D = 1152
TOKENS = 256
SEQ = 16
EPSILON = 1e-06
FACTOR = HEAD_DIM**-0.5
MESH = pl.DeviceIdType.MESH
F32 = jnp.float32
BF16 = jnp.bfloat16

NN = (((1,), (0,)), ((), ()))
NT = (((1,), (1,)), ((), ()))
TN = (((0,), (0,)), ((), ()))


def dot(a, b, dims=NN):
    return lax.dot_general(a, b, dims, preferred_element_type=F32)


def rows_of(i, size):
    return pl.ds(pl.multiple_of(i * size, size), size)


def normalise(source, mod, row, normed, scale, modulated):
    offset = mod[row : row + 1, :]
    stretch = 1.0 + mod[row + 1 : row + 2, :]

    def body(i, _):
        rows = rows_of(i, 32)
        x = source[rows, :].astype(F32)
        centred = x - jnp.mean(x, axis=-1, keepdims=True)
        spread = jnp.mean(centred * centred, axis=-1, keepdims=True)
        inverse = lax.rsqrt(spread + EPSILON)
        n = centred * inverse
        normed[rows, :] = n
        scale[rows, :] = inverse
        modulated[rows, :] = (n * stretch + offset).astype(BF16)
        return 0

    lax.fori_loop(0, TOKENS // 32, body, 0)


def project(modulated, weight, packed):
    def body(i, _):
        cols = rows_of(i, 256)
        packed[:, cols] = dot(modulated[...], weight[:, cols]).astype(BF16)
        return 0

    lax.fori_loop(0, 6, body, 0)
    packed[:, 1536:PACKED] = dot(modulated[...], weight[:, 1536:PACKED]).astype(BF16)


def project_back(rows_in, weight, out, width):
    def body(i, _):
        cols = rows_of(i, 384)
        out[:, cols] = dot(rows_in[...], weight[cols, :], NT).astype(out.dtype)
        return 0

    lax.fori_loop(0, width // 384, body, 0)


def head(ref, h, section=0):
    lane = section * HE + h * HEAD_DIM
    return ref[:, lane : lane + HEAD_DIM]


def probabilities(packed, h, mask):
    scores = dot(head(packed, h, 0), head(packed, h, 1), NT)
    raised = jnp.exp(scores * FACTOR)
    if mask is not None:
        raised = jnp.where(mask, raised, 0.0)
    return raised / jnp.sum(raised, axis=-1, keepdims=True)


def head_backward(probs, weights, packed, d_attended, h, d_packed):
    d_head = head(d_attended, h)
    d_weights = dot(d_head, head(packed, h, 2), NT)
    carried = jnp.sum(d_weights * probs, axis=-1, keepdims=True)
    d_scores = (probs * (d_weights - carried) * FACTOR).astype(BF16)
    lane = h * HEAD_DIM
    d_packed[:, lane : lane + HEAD_DIM] = dot(d_scores, head(packed, h, 1)).astype(BF16)
    d_packed[:, HE + lane : HE + lane + HEAD_DIM] = dot(d_scores, head(packed, h, 0), TN).astype(BF16)
    d_packed[:, 2 * HE + lane : 2 * HE + lane + HEAD_DIM] = dot(weights, d_head, TN).astype(BF16)


def fold(x):
    return sum(x[8 * i : 8 * i + 8] for i in range(x.shape[0] // 8))


def gated(source, mod, row, out):
    gate = mod[row : row + 1, :]

    def body(i, _):
        rows = rows_of(i, 32)
        out[rows, :] = (source[rows, :].astype(F32) * gate).astype(BF16)
        return 0

    lax.fori_loop(0, TOKENS // 32, body, 0)


def gate_sum(upstream, branch):
    def body(i, total):
        rows = rows_of(i, 32)
        return total + fold(upstream[rows, :].astype(F32) * branch[rows, :])

    total = lax.fori_loop(0, TOKENS // 32, body, jnp.zeros((8, D), F32))
    return jnp.sum(total, axis=0, keepdims=True)


def normalise_back(d_modulated, normed, scale, mod, row, upstream, out, after):
    stretch = 1.0 + mod[row + 1 : row + 2, :]

    def body(i, totals):
        rows = rows_of(i, 16)
        g = d_modulated[rows, :].astype(F32)
        n = normed[rows, :]
        dn = g * stretch
        gn = g * n
        first = jnp.mean(dn, axis=-1, keepdims=True)
        second = jnp.mean(dn * n, axis=-1, keepdims=True)
        dx = scale[rows, :] * (dn - first - n * second)
        out[rows, :] = (upstream[rows, :].astype(F32) + dx).astype(BF16)
        after(i)
        return totals[0] + fold(g), totals[1] + fold(gn)

    zero = jnp.zeros((8, D), F32)
    totals = lax.fori_loop(0, TOKENS // 16, body, (zero, zero))
    return tuple(jnp.sum(t, axis=0, keepdims=True) for t in totals)


def weight_gradient(left, right, flipped, out, width):
    def turn(i, _):
        cols = rows_of(i, 128)
        flipped[cols, :] = left[:, cols].T
        return 0

    lax.fori_loop(0, D // 128, turn, 0)

    def body(i, _):
        rows = rows_of(i, 128)
        out[rows, :] = dot(flipped[rows, :], right[...]).astype(BF16)
        return 0

    lax.fori_loop(0, D // 128, body, 0)


class Exchange:
    def __init__(self, source, target, send, recv):
        self.source, self.target, self.send, self.recv = source, target, send, recv
        self.me = lax.axis_index("seq")

    def to(self, j):
        peer = lax.rem(self.me + j, SEQ)
        return pltpu.make_async_remote_copy(
            src_ref=self.source.at[rows_of(peer, 16)],
            dst_ref=self.target.at[rows_of(self.me, 16)],
            send_sem=self.send.at[j],
            recv_sem=self.recv.at[j],
            device_id={"seq": peer},
            device_id_type=MESH,
        )

    def start(self, j):
        self.to(j).start()

    def wait_recv(self):
        def body(j, _):
            sender = lax.rem(self.me + SEQ - j, SEQ)
            pltpu.make_async_remote_copy(
                src_ref=self.source.at[rows_of(sender, 16)],
                dst_ref=self.target.at[rows_of(sender, 16)],
                send_sem=self.send.at[j],
                recv_sem=self.recv.at[j],
                device_id={"seq": sender},
                device_id_type=MESH,
            ).wait_recv()
            return 0

        lax.fori_loop(1, SEQ, body, 0)

    def wait_send(self):
        def body(j, _):
            self.to(j).wait_send()
            return 0

        lax.fori_loop(1, SEQ, body, 0)


def kernel(
    lat_hbm, cot_hbm, mod_hbm, wqs_hbm, wos_hbm, wqt_hbm, wot_hbm,
    grad_latents, moments, dqkv_s, dout_s, dqkv_t, dout_t,
    lat, cot, mod, wqs, wos, wqt, wot,
    normed_s, scale_s, modulated_s, packed_s, probs_s, attended_s, branch_s,
    normed_t, scale_t, modulated_t, packed_t, attended_t, branch_t,
    hidden_out, hidden, grad_out, grad_hidden,
    d_branch_s, d_branch_t, d_attended, d_packed_s, d_packed_t, d_modulated, flipped,
    load_sem, send_sem, recv_sem,
):
    me = lax.axis_index("seq")
    loads = [
        pltpu.make_async_copy(src, dst, load_sem.at[i])
        for i, (src, dst) in enumerate(
            [
                (lat_hbm, lat), (mod_hbm, mod), (wqs_hbm, wqs), (wot_hbm, wot),
                (wos_hbm, wos), (wqt_hbm, wqt),
                (cot_hbm.at[rows_of(me, 16)], cot.at[rows_of(me, 16)]),
            ]
        )
    ]
    for load in loads:
        load.start()

    barrier = pltpu.get_barrier_semaphore()

    def greet(j, _):
        pl.semaphore_signal(
            barrier, inc=1, device_id={"seq": lax.rem(me + j, SEQ)}, device_id_type=MESH
        )
        return 0

    lax.fori_loop(1, SEQ, greet, 0)
    loads[0].wait()
    loads[1].wait()
    normalise(lat, mod, 0, normed_s, scale_s, modulated_s)
    pl.semaphore_wait(barrier, SEQ - 1)

    cot_trip = Exchange(cot_hbm, cot, send_sem.at[0], recv_sem.at[0])
    hidden_trip = Exchange(hidden_out, hidden, send_sem.at[1], recv_sem.at[1])
    grad_trip = Exchange(grad_out, grad_hidden, send_sem.at[2], recv_sem.at[2])

    def send_cot(j, _):
        cot_trip.start(j)
        return 0

    lax.fori_loop(1, SEQ, send_cot, 0)

    loads[2].wait()
    project(modulated_s, wqs, packed_s)
    for h in range(HEADS):
        probs = probabilities(packed_s, h, None)
        probs_s[h] = probs
        lane = h * HEAD_DIM
        attended_s[:, lane : lane + HEAD_DIM] = dot(probs.astype(BF16), head(packed_s, h, 2)).astype(BF16)
    loads[4].wait()
    project_back(attended_s, wos, branch_s, D)

    gate_s = mod[2:3, :]

    def make_hidden(j, _):
        peer = lax.rem(me + j, SEQ)
        rows = rows_of(peer, 16)
        value = (lat[rows, :].astype(F32) + gate_s * branch_s[rows, :]).astype(BF16)
        hidden_out[rows, :] = value

        @pl.when(j < SEQ)
        def _():
            hidden_trip.start(j)

        return 0

    lax.fori_loop(1, SEQ + 1, make_hidden, 0)
    hidden[rows_of(me, 16), :] = hidden_out[rows_of(me, 16), :]

    loads[6].wait()
    cot_trip.wait_recv()
    loads[3].wait()
    gated(cot, mod, 5, d_branch_t)
    d_attended[...] = dot(d_branch_t[...], wot[...]).astype(BF16)
    hidden_trip.wait_recv()
    normalise(hidden, mod, 3, normed_t, scale_t, modulated_t)
    loads[5].wait()
    project(modulated_t, wqt, packed_t)
    patch_row = lax.rem(lax.broadcasted_iota(jnp.int32, (TOKENS, TOKENS), 0), 16)
    patch_col = lax.rem(lax.broadcasted_iota(jnp.int32, (TOKENS, TOKENS), 1), 16)
    mask = patch_row == patch_col
    for h in range(HEADS):
        probs = probabilities(packed_t, h, mask)
        weights = probs.astype(BF16)
        lane = h * HEAD_DIM
        attended_t[:, lane : lane + HEAD_DIM] = dot(weights, head(packed_t, h, 2)).astype(BF16)
        head_backward(probs, weights, packed_t, d_attended, h, d_packed_t)
    project_back(d_packed_t, wqt, d_modulated, D)

    def send_grad(i):
        @pl.when(i != me)
        def _():
            grad_trip.start(lax.rem(i + SEQ - me, SEQ))

    d_offset, d_stretch = normalise_back(
        d_modulated, normed_t, scale_t, mod, 3, cot, grad_out, send_grad
    )
    moments[3:4, :] = d_offset
    moments[4:5, :] = d_stretch
    grad_hidden[rows_of(me, 16), :] = grad_out[rows_of(me, 16), :]
    project_back(attended_t, wot, branch_t, D)
    moments[5:6, :] = gate_sum(cot, branch_t)
    weight_gradient(modulated_t, d_packed_t, flipped, dqkv_t, PACKED)
    weight_gradient(d_branch_t, attended_t, flipped, dout_t, HE)

    grad_trip.wait_recv()
    gated(grad_hidden, mod, 2, d_branch_s)
    moments[2:3, :] = gate_sum(grad_hidden, branch_s)
    d_attended[...] = dot(d_branch_s[...], wos[...]).astype(BF16)
    for h in range(HEADS):
        probs = probs_s[h]
        head_backward(probs, probs.astype(BF16), packed_s, d_attended, h, d_packed_s)
    project_back(d_packed_s, wqs, d_modulated, D)
    d_offset, d_stretch = normalise_back(
        d_modulated, normed_s, scale_s, mod, 0, grad_hidden, grad_latents, lambda i: None
    )
    moments[0:1, :] = d_offset
    moments[1:2, :] = d_stretch
    moments[6:8, :] = jnp.zeros((2, D), F32)
    weight_gradient(modulated_s, d_packed_s, flipped, dqkv_s, PACKED)
    weight_gradient(d_branch_s, attended_s, flipped, dout_s, HE)
    cot_trip.wait_send()
    hidden_trip.wait_send()
    grad_trip.wait_send()


def local(latents, cotangent, modulation, spatial_qkv, spatial_out, temporal_qkv, temporal_out):
    vm = pl.BlockSpec(memory_space=pltpu.VMEM)
    hbm = pl.BlockSpec(memory_space=pl.ANY)
    sds = jax.ShapeDtypeStruct
    wide = pltpu.VMEM((TOKENS, D), BF16)
    wide32 = pltpu.VMEM((TOKENS, D), F32)
    narrow = pltpu.VMEM((TOKENS, HE), BF16)
    three = pltpu.VMEM((TOKENS, PACKED), BF16)
    column = pltpu.VMEM((TOKENS, 1), F32)
    wq = pltpu.VMEM((D, PACKED), BF16)
    wo = pltpu.VMEM((D, HE), BF16)
    outs = pl.pallas_call(
        kernel,
        out_shape=[
            sds((TOKENS, D), BF16),
            sds((8, D), F32),
            sds((D, PACKED), BF16),
            sds((D, HE), BF16),
            sds((D, PACKED), BF16),
            sds((D, HE), BF16),
        ],
        in_specs=[hbm] * 7,
        out_specs=[vm] * 6,
        scratch_shapes=[
            wide, wide, pltpu.VMEM((6, D), F32), wq, wo, wq, wo,
            wide32, column, wide, three, pltpu.VMEM((HEADS, TOKENS, TOKENS), F32), narrow, wide32,
            wide32, column, wide, three, narrow, wide32,
            wide, wide, wide, wide,
            wide, wide, narrow, three, three, wide, pltpu.VMEM((D, TOKENS), BF16),
            pltpu.SemaphoreType.DMA((7,)),
            pltpu.SemaphoreType.DMA((3, SEQ)),
            pltpu.SemaphoreType.DMA((3, SEQ)),
        ],
        compiler_params=pltpu.CompilerParams(
            collective_id=0, has_side_effects=True, vmem_limit_bytes=62 * 2**20
        ),
    )(
        latents.reshape(TOKENS, D), cotangent.reshape(TOKENS, D), modulation.reshape(6, D),
        spatial_qkv, spatial_out, temporal_qkv, temporal_out,
    )
    grad, moments, dqkv_s, dout_s, dqkv_t, dout_t = outs
    grad_modulation = lax.psum(moments[:6], "seq")[None]

    def reduce(x):
        return lax.psum_scatter(x, ("dp", "seq"), scatter_dimension=0, tiled=True).astype(F32) / 8

    return (grad.reshape(latents.shape), grad_modulation, reduce(dqkv_s), reduce(dout_s), reduce(dqkv_t), reduce(dout_t))


def solution(mesh):
    in_specs = (
        P("dp", "seq", None, None),
        P("dp", "seq", None, None),
        P("dp", None, None),
        P(),
        P(),
        P(),
        P(),
    )
    out_specs = (
        P("dp", "seq", None, None),
        P("dp", None, None),
        P(("dp", "seq"), None),
        P(("dp", "seq"), None),
        P(("dp", "seq"), None),
        P(("dp", "seq"), None),
    )
    return jax.shard_map(local, mesh=mesh, in_specs=in_specs, out_specs=out_specs, check_vma=False)
```

```python
import functools

import jax
import jax.numpy as jnp
from jax import lax
from jax.experimental import pallas as pl
from jax.experimental.pallas import tpu as pltpu
from jax.sharding import PartitionSpec as P

HEADS = 8
HEAD_DIM = 72
HE = HEADS * HEAD_DIM
PACKED = 3 * HE
D = 1152
TOKENS = 256
SEQ = 16
EPSILON = 1e-06
FACTOR = HEAD_DIM**-0.5
BLOCKS = 16
BLOCK = 80
MESH = pl.DeviceIdType.MESH
F32 = jnp.float32
BF16 = jnp.bfloat16

NN = (((1,), (0,)), ((), ()))
NT = (((1,), (1,)), ((), ()))
TN = (((0,), (0,)), ((), ()))


def dot(a, b, dims=NN):
    return lax.dot_general(a, b, dims, preferred_element_type=F32)


def rows_of(i, size):
    return pl.ds(pl.multiple_of(i * size, size), size)


def normalise(source, mod, row, normed, scale, modulated):
    offset = mod[row : row + 1, :]
    stretch = 1.0 + mod[row + 1 : row + 2, :]

    def body(i, _):
        rows = rows_of(i, 32)
        x = source[rows, :].astype(F32)
        centred = x - jnp.mean(x, axis=-1, keepdims=True)
        spread = jnp.mean(centred * centred, axis=-1, keepdims=True)
        inverse = lax.rsqrt(spread + EPSILON)
        n = centred * inverse
        normed[rows, :] = n
        scale[rows, :] = inverse
        modulated[rows, :] = (n * stretch + offset).astype(BF16)
        return 0

    lax.fori_loop(0, TOKENS // 32, body, 0)


def project(modulated, weight, packed):
    def body(i, _):
        cols = rows_of(i, 256)
        packed[:, cols] = dot(modulated[...], weight[cols, :], NT).astype(BF16)
        return 0

    lax.fori_loop(0, 6, body, 0)
    packed[:, 1536:PACKED] = dot(modulated[...], weight[1536:PACKED, :], NT).astype(BF16)


def project_out(right, weight, out):
    def body(i, _):
        cols = rows_of(i, 384)
        out[:, cols] = dot(right[1, :, HE:], weight[:, cols])
        return 0

    lax.fori_loop(0, 3, body, 0)


def project_back(right, weight, out):
    def body(i, _):
        cols = rows_of(i, 384)
        total = dot(right[0], weight[: 2 * HE, cols]) + dot(right[1, :, :HE], weight[2 * HE :, cols])
        out[:, cols] = total.astype(BF16)
        return 0

    lax.fori_loop(0, 3, body, 0)


def head(ref, h, section=0):
    lane = section * HE + h * HEAD_DIM
    return ref[:, lane : lane + HEAD_DIM]


def probabilities(packed, h, mask):
    scores = dot(head(packed, h, 0), head(packed, h, 1), NT)
    raised = jnp.exp(scores * FACTOR)
    if mask is not None:
        raised = jnp.where(mask, raised, 0.0)
    return raised / jnp.sum(raised, axis=-1, keepdims=True)


def head_backward(probs, weights, packed, d_attended, h, right):
    d_head = head(d_attended, h)
    d_weights = dot(d_head, head(packed, h, 2), NT)
    carried = jnp.sum(d_weights * probs, axis=-1, keepdims=True)
    d_scores = (probs * (d_weights - carried) * FACTOR).astype(BF16)
    lane = h * HEAD_DIM
    right[0, :, lane : lane + HEAD_DIM] = dot(d_scores, head(packed, h, 1)).astype(BF16)
    right[0, :, HE + lane : HE + lane + HEAD_DIM] = dot(d_scores, head(packed, h, 0), TN).astype(BF16)
    right[1, :, lane : lane + HEAD_DIM] = dot(weights, d_head, TN).astype(BF16)


def attend(probs, packed, h, right):
    lane = HE + h * HEAD_DIM
    right[1, :, lane : lane + HEAD_DIM] = dot(probs, head(packed, h, 2)).astype(BF16)


def fold(x):
    return sum(x[8 * i : 8 * i + 8] for i in range(x.shape[0] // 8))


def gated(source, mod, row, out):
    gate = mod[row : row + 1, :]

    def body(i, _):
        rows = rows_of(i, 32)
        out[rows, :] = (source[rows, :].astype(F32) * gate).astype(BF16)
        return 0

    lax.fori_loop(0, TOKENS // 32, body, 0)


def gate_sum(upstream, branch):
    def body(i, total):
        rows = rows_of(i, 32)
        return total + fold(upstream[rows, :].astype(F32) * branch[rows, :])

    total = lax.fori_loop(0, TOKENS // 32, body, jnp.zeros((8, D), F32))
    return jnp.sum(total, axis=0, keepdims=True)


def normalise_back(d_modulated, normed, scale, mod, row, upstream, out, after):
    stretch = 1.0 + mod[row + 1 : row + 2, :]

    def body(i, totals):
        rows = rows_of(i, 16)
        g = d_modulated[rows, :].astype(F32)
        n = normed[rows, :]
        dn = g * stretch
        gn = g * n
        first = jnp.mean(dn, axis=-1, keepdims=True)
        second = jnp.mean(dn * n, axis=-1, keepdims=True)
        dx = scale[rows, :] * (dn - first - n * second)
        out[rows, :] = (upstream[rows, :].astype(F32) + dx).astype(BF16)
        after(i)
        return totals[0] + fold(g), totals[1] + fold(gn)

    zero = jnp.zeros((8, D), F32)
    totals = lax.fori_loop(0, TOKENS // 16, body, (zero, zero))
    return tuple(jnp.sum(t, axis=0, keepdims=True) for t in totals)


def flip(source, flipped, left):
    def turn(i, _):
        cols = rows_of(i, 128)
        flipped[cols, :] = source[:, cols].astype(F32).T
        return 0

    lax.fori_loop(0, D // 128, turn, 0)
    empty = jnp.zeros((BLOCK - 72, TOKENS), F32)
    for k in range(BLOCKS):
        rows = flipped[72 * k : 72 * k + 72, :]
        left[k] = jnp.concatenate([rows, empty], axis=0).astype(BF16)


def swap1(i):
    return i + 1 - 2 * lax.rem(i, 2)


class Place:
    def __init__(self):
        self.dp = lax.axis_index("dp")
        self.seq = lax.axis_index("seq")
        self.x = lax.rem(self.dp, 4)
        self.yh = lax.div(self.dp, 4)
        self.yl = lax.div(self.seq, 8)
        self.y = 2 * self.yh + self.yl
        self.z = lax.rem(lax.div(self.seq, 2), 4)
        self.core = lax.rem(self.seq, 2)

    def at(self, x=None, y=None, z=None, core=None):
        x = self.x if x is None else x
        y = self.y if y is None else y
        z = self.z if z is None else z
        core = self.core if core is None else core
        return {
            "dp": 4 * lax.div(y, 2) + x,
            "seq": 8 * lax.rem(y, 2) + 2 * z + core,
        }

    def pair(self, i):
        near, far = swap1(i), 3 - i
        return near + self.core * (far - near), far + self.core * (near - far)


def remote(src, dst, send, recv, device):
    return pltpu.make_async_remote_copy(
        src_ref=src, dst_ref=dst, send_sem=send, recv_sem=recv, device_id=device, device_id_type=MESH
    )


class PairTerms:
    def __init__(self, place, left, right, left_in, right_in, send, recv):
        self.core = place.core
        other = place.at(core=1 - place.core)
        self.left, self.right, self.left_in, self.right_in = left, right, left_in, right_in
        self.copies = [
            remote(left.at[0], left_in.at[0], send.at[0], recv.at[0], other),
            remote(left.at[1], left_in.at[1], send.at[1], recv.at[1], other),
            remote(right.at[1 - place.core], right_in, send.at[2], recv.at[2], other),
        ]

    def start(self, i):
        if i == 1:
            pl.when(self.core == 0)(self.copies[1].start)
        else:
            self.copies[i].start()

    def wait_recv(self):
        self.copies[0].wait_recv()
        pl.when(self.core == 1)(self.copies[1].wait_recv)
        self.copies[2].wait_recv()

    def wait_send(self):
        self.copies[0].wait_send()
        pl.when(self.core == 0)(self.copies[1].wait_send)
        self.copies[2].wait_send()

    def multiply(self, chunk, out):
        left = 0 if chunk == 0 else self.core
        cols = slice(chunk * HE, chunk * HE + HE)

        def body(i, _):
            blocks = pl.ds(4 * i, 4)
            own = self.left[left, blocks].reshape(4 * BLOCK, TOKENS)
            theirs = self.left_in[left, blocks].reshape(4 * BLOCK, TOKENS)
            total = dot(own, self.right[self.core, :, cols]) + dot(theirs, self.right_in[:, cols])
            out[blocks] = total.astype(BF16).reshape(4, BLOCK, HE)
            return 0

        lax.fori_loop(0, BLOCKS // 4, body, 0)


class Halving:
    def __init__(self, place, x_first, whole, first, second, half, third, fourth, quarter, windows, final, other, send, recv):
        self.place, self.x_first = place, x_first
        self.whole, self.first, self.second = whole, first, second
        self.half, self.third, self.fourth = half, third, fourth
        self.quarter, self.windows, self.final, self.other = quarter, windows, final, other
        x, y = place.x, place.y
        self.a, self.b = (x, y) if x_first else (y, x)
        self.a1, self.a2 = place.pair(self.a)
        self.b1, self.b2 = place.pair(self.b)
        far_a, far_b = lax.rem(self.a + 2, 4), lax.rem(self.b + 2, 4)
        z = place.z

        def copy(i, src, dst, device):
            return remote(src, dst, send.at[i], recv.at[i], device)

        to_a1, to_a2 = self.device(x_first, self.a1), self.device(x_first, self.a2)
        to_b1, to_b2 = self.device(not x_first, self.b1), self.device(not x_first, self.b2)
        self.copies = [
            copy(0, self.block(far_a), first.at[1], to_a1),
            copy(1, self.block(self.a1), first.at[0], to_a1),
            copy(2, self.block(self.a2), second, to_a2),
            copy(3, half.at[far_b], third.at[1], to_b1),
            copy(4, half.at[self.b1], third.at[0], to_b1),
            copy(5, half.at[self.b2], fourth, to_b2),
        ]
        for j in range(1, 4):
            peer = lax.rem(z + j, 4)
            self.copies.append(
                copy(5 + j, quarter.at[rows_of_16(peer)], windows.at[j - 1], place.at(z=peer))
            )
        self.copies.append(copy(9, final, other, place.at(core=1 - place.core)))

    def device(self, on_x, i):
        return self.place.at(x=i) if on_x else self.place.at(y=i)

    def block(self, i):
        if self.x_first:
            return self.whole.at[:, i]
        return self.whole.at[lax.div(i, 2), :, lax.rem(i, 2)]

    def parts(self, i):
        if self.x_first:
            return [self.whole.at[yh, i, yl] for yh in range(2) for yl in range(2)]
        return [self.whole.at[lax.div(i, 2), x, lax.rem(i, 2)] for x in range(4)]

    def slot(self, ref, j):
        return ref.at[j // 2, j % 2] if self.x_first else ref.at[j]

    def stage0(self):
        self.copies[0].start()
        self.copies[1].start()

    def stage1(self):
        self.copies[0].wait_recv()
        for j, part in enumerate(self.parts(self.a2)):
            part[...] = (part[...].astype(F32) + self.slot(self.first.at[1], j)[...].astype(F32)).astype(BF16)
        self.copies[2].start()

    def stage2(self):
        self.copies[1].wait_recv()
        self.copies[2].wait_recv()
        for j, part in enumerate(self.parts(self.a)):
            total = part[...].astype(F32) + self.slot(self.first.at[0], j)[...].astype(F32)
            self.half[j] = (total + self.slot(self.second, j)[...].astype(F32)).astype(BF16)
        self.copies[3].start()
        self.copies[4].start()

    def stage3(self):
        self.copies[3].wait_recv()
        kept = self.half.at[self.b2]
        kept[...] = (kept[...].astype(F32) + self.third[1].astype(F32)).astype(BF16)
        self.copies[5].start()

    def stage4(self):
        self.copies[4].wait_recv()
        self.copies[5].wait_recv()
        total = self.half[self.b].astype(F32) + self.third[0].astype(F32) + self.fourth[...].astype(F32)
        self.quarter[...] = total.astype(BF16)
        for j in range(6, 9):
            self.copies[j].start()

    def stage5(self):
        for j in range(6, 9):
            self.copies[j].wait_recv()
        total = self.quarter[rows_of_16(self.place.z), :].astype(F32)
        for j in range(3):
            total = total + self.windows[j].astype(F32)
        self.final[...] = total * (1.0 / 8)
        self.copies[9].start()

    def stage6(self):
        self.copies[9].wait_recv()
        shift = lax.rem(32 - 2 * self.place.z - 9 * self.place.core, 32)
        own = pltpu.roll(self.final[...], shift, 0)[:16]
        theirs = pltpu.roll(self.other[...], shift, 0)[:16]
        low = self.place.core == 0
        return jnp.where(low, own, theirs)[:9], jnp.where(low, theirs, own)[:9]

    def wait_send(self):
        for copy in self.copies:
            copy.wait_send()


def rows_of_16(i):
    return pl.ds(pl.multiple_of(i * 16, 16), 32)


class ClipSum:
    def __init__(self, place, held, arrived, send, recv):
        self.held, self.arrived = held, arrived
        devices = [
            place.at(core=1 - place.core),
            place.at(z=swap1(place.z)),
            place.at(z=3 - place.z),
            place.at(y=swap1(place.y)),
        ]
        self.copies = [
            remote(held.at[i], arrived.at[i], send.at[i], recv.at[i], device)
            for i, device in enumerate(devices)
        ]

    def start(self):
        self.copies[0].start()

    def step(self, i):
        self.copies[i].wait_recv()
        self.held[i + 1] = self.held[i] + self.arrived[i]
        if i < 3:
            self.copies[i + 1].start()

    def wait_send(self):
        for copy in self.copies:
            copy.wait_send()


class Exchange:
    def __init__(self, source, target, send, recv):
        self.source, self.target, self.send, self.recv = source, target, send, recv
        self.me = lax.axis_index("seq")

    def to(self, j):
        peer = lax.rem(self.me + j, SEQ)
        return pltpu.make_async_remote_copy(
            src_ref=self.source.at[rows_of(peer, 16)],
            dst_ref=self.target.at[rows_of(self.me, 16)],
            send_sem=self.send.at[j],
            recv_sem=self.recv.at[j],
            device_id={"seq": peer},
            device_id_type=MESH,
        )

    def start(self, j):
        self.to(j).start()

    def wait_recv(self):
        def body(j, _):
            sender = lax.rem(self.me + SEQ - j, SEQ)
            pltpu.make_async_remote_copy(
                src_ref=self.source.at[rows_of(sender, 16)],
                dst_ref=self.target.at[rows_of(sender, 16)],
                send_sem=self.send.at[j],
                recv_sem=self.recv.at[j],
                device_id={"seq": sender},
                device_id_type=MESH,
            ).wait_recv()
            return 0

        lax.fori_loop(1, SEQ, body, 0)

    def wait_send(self):
        def body(j, _):
            self.to(j).wait_send()
            return 0

        lax.fori_loop(1, SEQ, body, 0)


def kernel(
    lat_hbm, cot_hbm, mod_hbm, wqs_hbm, wos_hbm, wqt_hbm, wot_hbm,
    grad_latents, moments, dqkv_s, dout_s, dqkv_t, dout_t,
    lat, cot, mod, wqs, wos, wqt, wot,
    normed_s, scale_s, modulated_s, packed_s, probs_s, branch_s,
    normed_t, scale_t, modulated_t, packed_t, branch_t,
    hidden_out, hidden, grad_out, grad_hidden,
    d_branch_s, d_branch_t, d_attended, d_modulated, flipped,
    left_s, right_s, left_in_s, right_in_s, left_t, right_t, left_in_t, right_in_t,
    whole, first_x, first_y, second_x, second_y, half, third, fourth, quarter, windows, final, other,
    held, arrived,
    load_sem, send_sem, recv_sem, pair_send, pair_recv, sum_send, sum_recv, clip_send, clip_recv,
):
    place = Place()
    me = place.seq
    loads = [
        pltpu.make_async_copy(src, dst, load_sem.at[i])
        for i, (src, dst) in enumerate(
            [
                (lat_hbm, lat), (mod_hbm, mod), (wqs_hbm, wqs), (wot_hbm, wot),
                (wos_hbm, wos), (wqt_hbm, wqt),
                (cot_hbm.at[rows_of(me, 16)], cot.at[rows_of(me, 16)]),
            ]
        )
    ]
    for load in loads:
        load.start()

    barrier = pltpu.get_barrier_semaphore()

    def greet(j, _):
        pl.semaphore_signal(
            barrier, inc=1, device_id={"seq": lax.rem(me + j, SEQ)}, device_id_type=MESH
        )
        return 0

    lax.fori_loop(1, SEQ, greet, 0)
    for device in (place.at(x=swap1(place.x)), place.at(x=3 - place.x), place.at(y=3 - place.y)):
        pl.semaphore_signal(barrier, inc=1, device_id=device, device_id_type=MESH)
    loads[0].wait()
    loads[1].wait()
    normalise(lat, mod, 0, normed_s, scale_s, modulated_s)
    pl.semaphore_wait(barrier, SEQ + 2)

    cot_trip = Exchange(cot_hbm, cot, send_sem.at[0], recv_sem.at[0])
    hidden_trip = Exchange(hidden_out, hidden, send_sem.at[1], recv_sem.at[1])
    grad_trip = Exchange(grad_out, grad_hidden, send_sem.at[2], recv_sem.at[2])
    pair_s = PairTerms(place, left_s, right_s, left_in_s, right_in_s, pair_send.at[0], pair_recv.at[0])
    pair_t = PairTerms(place, left_t, right_t, left_in_t, right_in_t, pair_send.at[1], pair_recv.at[1])
    sums_s, sums_t = [
        [
            Halving(
                place, c == 0, whole.at[l, c], (first_x, first_y)[c].at[l], (second_x, second_y)[c].at[l],
                half.at[l, c], third.at[l, c], fourth.at[l, c], quarter.at[l, c], windows.at[l, c],
                final.at[l, c], other.at[l, c], sum_send.at[l, c], sum_recv.at[l, c],
            )
            for c in range(2)
        ]
        for l in range(2)
    ]
    clip = ClipSum(place, held, arrived, clip_send, clip_recv)

    def send_cot(j, _):
        cot_trip.start(j)
        return 0

    lax.fori_loop(1, SEQ, send_cot, 0)

    loads[2].wait()
    project(modulated_s, wqs, packed_s)
    for h in range(HEADS):
        probs = probabilities(packed_s, h, None)
        probs_s[h] = probs
        attend(probs.astype(BF16), packed_s, h, right_s)
    loads[4].wait()
    project_out(right_s, wos, branch_s)

    gate_s = mod[2:3, :]

    def make_hidden(j, _):
        peer = lax.rem(me + j, SEQ)
        rows = rows_of(peer, 16)
        value = (lat[rows, :].astype(F32) + gate_s * branch_s[rows, :]).astype(BF16)
        hidden_out[rows, :] = value

        @pl.when(j < SEQ)
        def _():
            hidden_trip.start(j)

        return 0

    lax.fori_loop(1, SEQ + 1, make_hidden, 0)
    hidden[rows_of(me, 16), :] = hidden_out[rows_of(me, 16), :]

    loads[6].wait()
    cot_trip.wait_recv()
    loads[3].wait()
    gated(cot, mod, 5, d_branch_t)
    d_attended[...] = dot(d_branch_t[...], wot[...], NT).astype(BF16)
    flip(modulated_s, flipped, left_s.at[0])
    flip(d_branch_t, flipped, left_t.at[1])
    hidden_trip.wait_recv()
    normalise(hidden, mod, 3, normed_t, scale_t, modulated_t)
    loads[5].wait()
    project(modulated_t, wqt, packed_t)
    patch_row = lax.rem(lax.broadcasted_iota(jnp.int32, (TOKENS, TOKENS), 0), 16)
    patch_col = lax.rem(lax.broadcasted_iota(jnp.int32, (TOKENS, TOKENS), 1), 16)
    mask = patch_row == patch_col
    for h in range(HEADS):
        probs = probabilities(packed_t, h, mask)
        weights = probs.astype(BF16)
        attend(weights, packed_t, h, right_t)
        head_backward(probs, weights, packed_t, d_attended, h, right_t)
    pair_t.start(2)
    pair_t.start(1)
    project_back(right_t, wqt, d_modulated)

    def send_grad(i):
        @pl.when(i != me)
        def _():
            grad_trip.start(lax.rem(i + SEQ - me, SEQ))

    d_offset, d_stretch = normalise_back(
        d_modulated, normed_t, scale_t, mod, 3, cot, grad_out, send_grad
    )
    clip_first = held.at[0]
    clip_first[3:4, :] = d_offset
    clip_first[4:5, :] = d_stretch
    grad_hidden[rows_of(me, 16), :] = grad_out[rows_of(me, 16), :]
    flip(modulated_t, flipped, left_t.at[0])
    pair_t.start(0)
    project_out(right_t, wot, branch_t)
    clip_first[5:6, :] = gate_sum(cot, branch_t)
    pair_t.wait_recv()
    for c in range(2):
        pair_t.multiply(c, whole.at[1, c].reshape(BLOCKS, BLOCK, HE))
        sums_t[c].stage0()

    grad_trip.wait_recv()
    gated(grad_hidden, mod, 2, d_branch_s)
    clip_first[2:3, :] = gate_sum(grad_hidden, branch_s)
    d_attended[...] = dot(d_branch_s[...], wos[...], NT).astype(BF16)
    flip(d_branch_s, flipped, left_s.at[1])
    pair_s.start(0)
    pair_s.start(1)
    sums_t[0].stage1()
    sums_t[1].stage1()
    for h in range(HEADS):
        probs = probs_s[h]
        head_backward(probs, probs.astype(BF16), packed_s, d_attended, h, right_s)
    pair_s.start(2)
    sums_t[0].stage2()
    sums_t[1].stage2()
    pair_s.wait_recv()
    for c in range(2):
        pair_s.multiply(c, whole.at[0, c].reshape(BLOCKS, BLOCK, HE))
        sums_s[c].stage0()
    sums_t[0].stage3()
    sums_t[1].stage3()
    project_back(right_s, wqs, d_modulated)
    sums_s[0].stage1()
    sums_s[1].stage1()
    d_offset, d_stretch = normalise_back(
        d_modulated, normed_s, scale_s, mod, 0, grad_hidden, grad_latents, lambda i: None
    )
    clip_first[0:1, :] = d_offset
    clip_first[1:2, :] = d_stretch
    clip_first[6:8, :] = jnp.zeros((2, D), F32)
    clip.start()
    sums_t[0].stage4()
    sums_t[1].stage4()
    clip.step(0)
    sums_s[0].stage2()
    sums_s[1].stage2()
    clip.step(1)
    sums_t[0].stage5()
    sums_t[1].stage5()
    sums_s[0].stage3()
    sums_s[1].stage3()
    clip.step(2)
    results_t = [sums.stage6() for sums in sums_t]
    sums_s[0].stage4()
    sums_s[1].stage4()
    clip.step(3)
    sums_s[0].stage5()
    sums_s[1].stage5()
    results_s = [sums.stage6() for sums in sums_s]
    moments[...] = held[4]
    for (d_query, d_value), (d_key, d_out), dqkv, dout in (
        (*results_s, dqkv_s, dout_s),
        (*results_t, dqkv_t, dout_t),
    ):
        dqkv[:, :HE] = d_query
        dqkv[:, HE : 2 * HE] = d_key
        dqkv[:, 2 * HE :] = d_value
        dout[...] = d_out

    cot_trip.wait_send()
    hidden_trip.wait_send()
    grad_trip.wait_send()
    for part in (pair_s, pair_t, *sums_s, *sums_t, clip):
        part.wait_send()


def local(latents, cotangent, modulation, spatial_qkv, spatial_out, temporal_qkv, temporal_out):
    vm = pl.BlockSpec(memory_space=pltpu.VMEM)
    hbm = pl.BlockSpec(memory_space=pl.ANY)
    sds = jax.ShapeDtypeStruct

    def bf16(*shape):
        return pltpu.VMEM(shape, BF16)

    def f32(*shape):
        return pltpu.VMEM(shape, F32)

    wide, wide32, column = bf16(TOKENS, D), f32(TOKENS, D), f32(TOKENS, 1)
    three, wq, wo = bf16(TOKENS, PACKED), bf16(PACKED, D), bf16(HE, D)
    left, right = bf16(2, BLOCKS, BLOCK, TOKENS), bf16(2, TOKENS, 2 * HE)
    dma = pltpu.SemaphoreType.DMA
    outs = pl.pallas_call(
        kernel,
        out_shape=[
            sds((TOKENS, D), BF16),
            sds((8, D), F32),
            sds((9, PACKED), F32),
            sds((9, HE), F32),
            sds((9, PACKED), F32),
            sds((9, HE), F32),
        ],
        in_specs=[hbm] * 7,
        out_specs=[vm] * 6,
        scratch_shapes=[
            wide, wide, f32(6, D), wq, wo, wq, wo,
            wide32, column, wide, three, f32(HEADS, TOKENS, TOKENS), wide32,
            wide32, column, wide, three, wide32,
            wide, wide, wide, wide,
            wide, wide, bf16(TOKENS, HE), wide, f32(D, TOKENS),
            left, right, left, bf16(TOKENS, 2 * HE), left, right, left, bf16(TOKENS, 2 * HE),
            bf16(2, 2, 2, 4, 2, BLOCK, HE), bf16(2, 2, 2, 2, BLOCK, HE), bf16(2, 2, 4, BLOCK, HE),
            bf16(2, 2, 2, BLOCK, HE), bf16(2, 4, BLOCK, HE),
            bf16(2, 2, 4, BLOCK, HE), bf16(2, 2, 2, BLOCK, HE), bf16(2, 2, BLOCK, HE), bf16(2, 2, BLOCK, HE),
            bf16(2, 2, 3, 32, HE), f32(2, 2, 32, HE), f32(2, 2, 32, HE),
            f32(5, 8, D), f32(4, 8, D),
            dma((7,)), dma((3, SEQ)), dma((3, SEQ)), dma((2, 3)), dma((2, 3)),
            dma((2, 2, 10)), dma((2, 2, 10)), dma((4,)), dma((4,)),
        ],
        compiler_params=pltpu.CompilerParams(
            collective_id=0, has_side_effects=True, vmem_limit_bytes=62 * 2**20
        ),
    )(
        latents.reshape(TOKENS, D), cotangent.reshape(TOKENS, D), modulation.reshape(6, D),
        spatial_qkv.T, spatial_out.T, temporal_qkv.T, temporal_out.T,
    )
    grad, moments, dqkv_s, dout_s, dqkv_t, dout_t = outs
    return (grad.reshape(latents.shape), moments[:6][None], dqkv_s, dout_s, dqkv_t, dout_t)


def solution(mesh):
    in_specs = (
        P("dp", "seq", None, None),
        P("dp", "seq", None, None),
        P("dp", None, None),
        P(),
        P(),
        P(),
        P(),
    )
    out_specs = (
        P("dp", "seq", None, None),
        P("dp", None, None),
        P(("dp", "seq"), None),
        P(("dp", "seq"), None),
        P(("dp", "seq"), None),
        P(("dp", "seq"), None),
    )
    return jax.shard_map(local, mesh=mesh, in_specs=in_specs, out_specs=out_specs, check_vma=False)
```

```python
import functools

import jax
import jax.numpy as jnp
from jax import lax
from jax.experimental import pallas as pl
from jax.experimental.pallas import tpu as pltpu
from jax.sharding import PartitionSpec as P

HEADS = 8
HEAD_DIM = 72
HE = HEADS * HEAD_DIM
PACKED = 3 * HE
D = 1152
TOKENS = 256
SEQ = 16
EPSILON = 1e-06
FACTOR = HEAD_DIM**-0.5
BLOCKS = 16
BLOCK = 80
PART = 384
MESH = pl.DeviceIdType.MESH
F32 = jnp.float32
BF16 = jnp.bfloat16

NN = (((1,), (0,)), ((), ()))
NT = (((1,), (1,)), ((), ()))
TN = (((0,), (0,)), ((), ()))


def dot(a, b, dims=NN):
    return lax.dot_general(a, b, dims, preferred_element_type=F32)


def rows_of(i, size):
    return pl.ds(pl.multiple_of(i * size, size), size)


def normalise(read, mod, row, normed, scale, modulated):
    offset = mod[row]
    stretch = 1.0 + mod[row + 1]

    def body(i, _):
        rows = rows_of(i, 32)
        x = read(rows).astype(F32)
        centred = x - jnp.mean(x, axis=-1, keepdims=True)
        spread = jnp.mean(centred * centred, axis=-1, keepdims=True)
        inverse = lax.rsqrt(spread + EPSILON)
        n = centred * inverse
        normed[rows, :] = n
        scale[rows, :] = inverse
        modulated[rows, :] = (n * stretch + offset).astype(BF16)
        return 0

    lax.fori_loop(0, TOKENS // 32, body, 0)


def project(modulated, weight, packed):
    def body(i, _):
        cols = rows_of(i, 256)
        packed[:, cols] = dot(modulated[...], weight[cols, :], NT).astype(BF16)
        return 0

    lax.fori_loop(0, 6, body, 0)
    packed[:, 1536:PACKED] = dot(modulated[...], weight[1536:PACKED, :], NT).astype(BF16)


def project_out(attended, weight, out):
    def body(i, _):
        cols = rows_of(i, 384)
        out[:, cols] = dot(attended[...], weight[:, cols])
        return 0

    lax.fori_loop(0, 3, body, 0)


def project_back(right, weight, out):
    def body(i, _):
        cols = rows_of(i, 384)
        total = dot(right[0], weight[: 2 * HE, cols]) + dot(right[1, :, :HE], weight[2 * HE :, cols])
        out[:, cols] = total.astype(BF16)
        return 0

    lax.fori_loop(0, 3, body, 0)


def head(ref, h, section=0):
    lane = section * HE + h * HEAD_DIM
    return ref[:, lane : lane + HEAD_DIM]


def probabilities(packed, h, mask):
    scores = dot(head(packed, h, 0), head(packed, h, 1), NT)
    raised = jnp.exp(scores * FACTOR)
    if mask is not None:
        raised = jnp.where(mask, raised, 0.0)
    return raised / jnp.sum(raised, axis=-1, keepdims=True)


def head_backward(probs, weights, packed, d_attended, h, right):
    d_head = head(d_attended, h)
    d_weights = dot(d_head, head(packed, h, 2), NT)
    carried = jnp.sum(d_weights * probs, axis=-1, keepdims=True)
    d_scores = (probs * (d_weights - carried) * FACTOR).astype(BF16)
    lane = h * HEAD_DIM
    right[0, :, lane : lane + HEAD_DIM] = dot(d_scores, head(packed, h, 1)).astype(BF16)
    right[0, :, HE + lane : HE + lane + HEAD_DIM] = dot(d_scores, head(packed, h, 0), TN).astype(BF16)
    right[1, :, lane : lane + HEAD_DIM] = dot(weights, d_head, TN).astype(BF16)


def attend(weights, packed, h, attended):
    lane = h * HEAD_DIM
    attended[:, lane : lane + HEAD_DIM] = dot(weights, head(packed, h, 2)).astype(BF16)


def fold(x):
    return sum(x[8 * i : 8 * i + 8] for i in range(x.shape[0] // 8))


def gated(source, mod, row, out):
    gate = mod[row]

    def body(i, _):
        rows = rows_of(i, 32)
        out[rows, :] = (source[rows, :].astype(F32) * gate).astype(BF16)
        return 0

    lax.fori_loop(0, TOKENS // 32, body, 0)


def gate_sum(upstream, branch):
    def body(i, total):
        rows = rows_of(i, 32)
        return total + fold(upstream[rows, :].astype(F32) * branch[rows, :])

    total = lax.fori_loop(0, TOKENS // 32, body, jnp.zeros((8, D), F32))
    return jnp.sum(total, axis=0, keepdims=True)


def normalise_back(d_modulated, normed, scale, mod, row, upstream, out, branch=None, after=None):
    stretch = 1.0 + mod[row + 1]

    def body(i, totals):
        rows = rows_of(i, 16)
        g = d_modulated[rows, :].astype(F32)
        n = normed[rows, :]
        dn = g * stretch
        first = jnp.mean(dn, axis=-1, keepdims=True)
        second = jnp.mean(dn * n, axis=-1, keepdims=True)
        dx = scale[rows, :] * (dn - first - n * second)
        value = (upstream[rows, :].astype(F32) + dx).astype(BF16)
        out[rows, :] = value
        terms = [g, g * n]
        if branch is not None:
            terms.append(value.astype(F32) * branch[rows, :])
        if after is not None:
            after(i)
        return tuple(total + fold(term) for total, term in zip(totals, terms))

    zero = jnp.zeros((8, D), F32)
    totals = lax.fori_loop(0, TOKENS // 16, body, (zero,) * (2 if branch is None else 3))
    return tuple(jnp.sum(t, axis=0, keepdims=True) for t in totals)


def flip(source, flipped, left):
    def turn(i, _):
        cols = rows_of(i, 128)
        flipped[cols, :] = source[:, cols].astype(F32).T
        return 0

    lax.fori_loop(0, D // 128, turn, 0)
    empty = jnp.zeros((BLOCK - 72, TOKENS), F32)
    for k in range(BLOCKS):
        rows = flipped[72 * k : 72 * k + 72, :]
        left[k] = jnp.concatenate([rows, empty], axis=0).astype(BF16)


def swap1(i):
    return i + 1 - 2 * lax.rem(i, 2)


class Place:
    def __init__(self):
        self.dp = lax.axis_index("dp")
        self.seq = lax.axis_index("seq")
        self.x = lax.rem(self.dp, 4)
        self.yh = lax.div(self.dp, 4)
        self.yl = lax.div(self.seq, 8)
        self.y = 2 * self.yh + self.yl
        self.z = lax.rem(lax.div(self.seq, 2), 4)
        self.core = lax.rem(self.seq, 2)

    def at(self, x=None, y=None, z=None, core=None):
        x = self.x if x is None else x
        y = self.y if y is None else y
        z = self.z if z is None else z
        core = self.core if core is None else core
        return {
            "dp": 4 * lax.div(y, 2) + x,
            "seq": 8 * lax.rem(y, 2) + 2 * z + core,
        }


def remote(src, dst, send, recv, device):
    return pltpu.make_async_remote_copy(
        src_ref=src, dst_ref=dst, send_sem=send, recv_sem=recv, device_id=device, device_id_type=MESH
    )


class PairTerms:
    def __init__(self, place, left, right, left_in, right_in, send, recv):
        self.core = place.core
        other = place.at(core=1 - place.core)
        self.left, self.right, self.left_in, self.right_in = left, right, left_in, right_in
        self.copies = [
            remote(left.at[0], left_in.at[0], send.at[0], recv.at[0], other),
            remote(left.at[1], left_in.at[1], send.at[1], recv.at[1], other),
            remote(right.at[1 - place.core], right_in, send.at[2], recv.at[2], other),
        ]

    def start(self, i):
        if i == 1:
            pl.when(self.core == 0)(self.copies[1].start)
        else:
            self.copies[i].start()

    def wait_recv(self):
        self.copies[0].wait_recv()
        pl.when(self.core == 1)(self.copies[1].wait_recv)
        self.copies[2].wait_recv()

    def wait_send(self):
        self.copies[0].wait_send()
        pl.when(self.core == 0)(self.copies[1].wait_send)
        self.copies[2].wait_send()

    def multiply(self, part, out):
        first = PART * part
        pieces = [(first, first + PART)]
        if part == 1:
            pieces = [(first, HE), (HE, first + PART)]

        def body(i, _):
            blocks = pl.ds(4 * i, 4)
            for low, high in pieces:
                left = 0 if high <= HE else self.core
                own = self.left[left, blocks].reshape(4 * BLOCK, TOKENS)
                theirs = self.left_in[left, blocks].reshape(4 * BLOCK, TOKENS)
                total = dot(own, self.right[self.core, :, low:high]) + dot(theirs, self.right_in[:, low:high])
                out[blocks, :, low - first : high - first] = total.astype(BF16).reshape(4, BLOCK, high - low)
            return 0

        lax.fori_loop(0, BLOCKS // 4, body, 0)


class Reduction:
    def __init__(self, place, part, whole, first, half, second, quarter, third, final, mine, other, send, recv):
        self.place, self.part = place, part
        self.whole, self.first, self.half, self.second = whole, first, half, second
        self.quarter, self.third, self.final, self.mine, self.other = quarter, third, final, mine, other
        names = ("zyx", "xyz", "yxz")[part]
        self.at = [getattr(place, name) for name in names]
        self.copies = []
        for stage, name in enumerate(names):
            for j in range(1, 4):
                peer = lax.rem(self.at[stage] + j, 4)
                src, dst = (
                    lambda: (self.slab(peer), first.at[j - 1]),
                    lambda: (half.at[peer], second.at[j - 1]),
                    lambda: (quarter.at[window(peer)], third.at[j - 1]),
                )[stage]()
                i = 3 * stage + j - 1
                self.copies.append(remote(src, dst, send.at[i], recv.at[i], place.at(**{name: peer})))
        if part == 0:
            to = [place.at(x=place.z, z=place.x, core=c) for c in (1 - place.core, place.core)]
            self.copies.append(remote(final, other, send.at[9], recv.at[9], to[0]))
            self.trade = remote(final, mine, send.at[10], recv.at[10], to[1])
        else:
            self.copies.append(remote(final, other, send.at[9], recv.at[9], place.at(core=1 - place.core)))

    def slab(self, i):
        if self.part == 2:
            return self.whole.at[lax.div(i, 2), :, lax.rem(i, 2)]
        return self.whole.at[:, i]

    def start(self, stage):
        for i in range(3 * stage, 3 * stage + 3):
            self.copies[i].start()

    def wait(self, stage):
        for i in range(3 * stage, 3 * stage + 3):
            self.copies[i].wait_recv()

    def stage1(self):
        self.start(0)

    def stage2(self):
        self.wait(0)
        own = self.slab(self.at[0])
        for j in range(4):
            at = (j,) if self.part == 2 else (j // 2, j % 2)
            total = own[at].astype(F32)
            for k in range(3):
                total = total + self.first[(k, *at)].astype(F32)
            self.half[j] = total.astype(BF16)
        self.start(1)

    def stage3(self):
        self.wait(1)
        total = self.half[self.at[1]].astype(F32)
        for k in range(3):
            total = total + self.second[k].astype(F32)
        self.quarter[...] = total.astype(BF16)
        self.start(2)

    def stage4(self):
        self.wait(2)
        total = self.quarter[window(self.at[2]), :].astype(F32)
        for k in range(3):
            total = total + self.third[k].astype(F32)
        self.final[...] = total * (1.0 / 8)
        self.copies[9].start()
        if self.part == 0:
            pl.when(self.place.x != self.place.z)(self.trade.start)

    def stage5(self):
        mine = self.final
        if self.part == 0:
            mine = self.mine

            @pl.when(self.place.x == self.place.z)
            def _():
                self.mine[...] = self.final[...]

            pl.when(self.place.x != self.place.z)(self.trade.wait_recv)
        self.copies[9].wait_recv()
        shift = lax.rem(32 - 2 * self.place.z - 9 * self.place.core, 32)
        own = pltpu.roll(mine[...], shift, 0)[:16]
        theirs = pltpu.roll(self.other[...], shift, 0)[:16]
        low = self.place.core == 0
        return jnp.where(low, own, theirs)[:9], jnp.where(low, theirs, own)[:9]

    def wait_send(self):
        for copy in self.copies:
            copy.wait_send()
        if self.part == 0:
            pl.when(self.place.x != self.place.z)(self.trade.wait_send)


def window(i):
    return pl.ds(pl.multiple_of(i * 16, 16), 32)


class ClipSum:
    def __init__(self, place, held, arrived, send, recv):
        self.held, self.arrived = held, arrived
        devices = [
            place.at(core=1 - place.core),
            place.at(z=swap1(place.z)),
            place.at(z=3 - place.z),
            place.at(y=swap1(place.y)),
        ]
        self.copies = [
            remote(held.at[i], arrived.at[i], send.at[i], recv.at[i], device)
            for i, device in enumerate(devices)
        ]

    def start(self):
        self.copies[0].start()

    def step(self, i):
        self.copies[i].wait_recv()
        self.held[i + 1] = self.held[i] + self.arrived[i]
        if i < 3:
            self.copies[i + 1].start()

    def wait_send(self):
        for copy in self.copies:
            copy.wait_send()


class Exchange:
    def __init__(self, source, target, send, recv):
        self.source, self.target, self.send, self.recv = source, target, send, recv
        self.me = lax.axis_index("seq")

    def to(self, j):
        peer = lax.rem(self.me + j, SEQ)
        return pltpu.make_async_remote_copy(
            src_ref=self.source.at[rows_of(peer, 16)],
            dst_ref=self.target.at[rows_of(self.me, 16)],
            send_sem=self.send.at[j],
            recv_sem=self.recv.at[j],
            device_id={"seq": peer},
            device_id_type=MESH,
        )

    def start(self, j):
        self.to(j).start()

    def wait_recv(self):
        def body(j, _):
            sender = lax.rem(self.me + SEQ - j, SEQ)
            pltpu.make_async_remote_copy(
                src_ref=self.source.at[rows_of(sender, 16)],
                dst_ref=self.target.at[rows_of(sender, 16)],
                send_sem=self.send.at[j],
                recv_sem=self.recv.at[j],
                device_id={"seq": sender},
                device_id_type=MESH,
            ).wait_recv()
            return 0

        lax.fori_loop(1, SEQ, body, 0)

    def wait_send(self):
        def body(j, _):
            self.to(j).wait_send()
            return 0

        lax.fori_loop(1, SEQ, body, 0)


def kernel(
    lat_hbm, cot_hbm, mod_hbm, wqs_hbm, wos_hbm, wqt_hbm, wot_hbm,
    grad_latents, moments, dqkv_s, dout_s, dqkv_t, dout_t,
    lat, mod, wqs, wos, wqt, wot,
    normed_s, scale_s, modulated_s, packed_s, probs_s, attended_s,
    lat_p, attended_p, branch_s, cot, normed_t, scale_t, modulated_t, packed_t, attended_t, branch_t,
    grad_out, grad_hidden,
    d_branch_s, d_branch_t, d_attended, d_modulated, flipped,
    left_s, right_s, left_in_s, right_in_s, left_t, right_t, left_in_t, right_in_t,
    whole, first_a, first_b, half, second, quarter, third, final, mine, other,
    held, arrived,
    load_sem, send_sem, recv_sem, pair_send, pair_recv, sum_send, sum_recv, clip_send, clip_recv,
):
    place = Place()
    me = place.seq
    here = rows_of(me, 16)
    loads = [
        pltpu.make_async_copy(src, dst, load_sem.at[i])
        for i, (src, dst) in enumerate(
            [
                (lat_hbm, lat), (mod_hbm, mod), (wqs_hbm, wqs), (wos_hbm, wos), (wqt_hbm, wqt), (wot_hbm, wot),
                (lat_hbm.at[here], lat_p.at[here]), (cot_hbm.at[here], cot.at[here]),
            ]
        )
    ]
    for load in loads:
        load.start()

    barrier = pltpu.get_barrier_semaphore()

    def signal(device):
        pl.semaphore_signal(barrier, inc=1, device_id=device, device_id_type=MESH)

    def greet(j, _):
        signal({"seq": lax.rem(me + j, SEQ)})
        return 0

    lax.fori_loop(1, SEQ, greet, 0)
    for j in range(1, 4):
        signal(place.at(x=lax.rem(place.x + j, 4)))
    signal(place.at(y=lax.rem(place.y + 2, 4)))
    signal(place.at(y=3 - place.y))

    @pl.when(place.x != place.z)
    def _():
        signal(place.at(x=place.z, z=place.x))
        signal(place.at(x=place.z, z=place.x, core=1 - place.core))

    loads[0].wait()
    loads[1].wait()
    normalise(lambda rows: lat[rows, :], mod, 0, normed_s, scale_s, modulated_s)
    pl.semaphore_wait(barrier, jnp.where(place.x == place.z, SEQ + 4, SEQ + 6))

    trips = [
        Exchange(source, target, send_sem.at[i], recv_sem.at[i])
        for i, (source, target) in enumerate(
            [(lat_hbm, lat_p), (cot_hbm, cot), (attended_s, attended_p), (grad_out, grad_hidden)]
        )
    ]
    lat_trip, cot_trip, attended_trip, grad_trip = trips
    pair_s = PairTerms(place, left_s, right_s, left_in_s, right_in_s, pair_send.at[0], pair_recv.at[0])
    pair_t = PairTerms(place, left_t, right_t, left_in_t, right_in_t, pair_send.at[1], pair_recv.at[1])
    sums_s, sums_t = [
        [
            Reduction(
                place, p, whole.at[l, p], first_b.at[l] if p == 2 else first_a.at[l, p], half.at[l, p],
                second.at[l, p], quarter.at[l, p], third.at[l, p], final.at[l, p], mine.at[l], other.at[l, p],
                sum_send.at[l, p], sum_recv.at[l, p],
            )
            for p in range(3)
        ]
        for l in range(2)
    ]
    clip = ClipSum(place, held, arrived, clip_send, clip_recv)

    def send_all(trip):
        def body(j, _):
            trip.start(j)
            return 0

        lax.fori_loop(1, SEQ, body, 0)

    send_all(lat_trip)

    loads[2].wait()
    project(modulated_s, wqs, packed_s)
    for h in range(HEADS):
        probs = probabilities(packed_s, h, None)
        probs_s[h] = probs
        attend(probs.astype(BF16), packed_s, h, attended_s)
    send_all(attended_trip)
    send_all(cot_trip)
    attended_p[here, :] = attended_s[here, :]
    right_s[1, :, HE:] = attended_s[...]
    flip(modulated_s, flipped, left_s.at[0])

    loads[3].wait()
    attended_trip.wait_recv()
    project_out(attended_p, wos, branch_s)
    loads[6].wait()
    lat_trip.wait_recv()
    gate_s = mod[2]

    def hidden(rows):
        return (lat_p[rows, :].astype(F32) + gate_s * branch_s[rows, :]).astype(BF16)

    normalise(hidden, mod, 3, normed_t, scale_t, modulated_t)
    loads[4].wait()
    project(modulated_t, wqt, packed_t)
    loads[7].wait()
    cot_trip.wait_recv()
    loads[5].wait()
    gated(cot, mod, 5, d_branch_t)
    d_attended[...] = dot(d_branch_t[...], wot[...], NT).astype(BF16)
    patch_row = lax.rem(lax.broadcasted_iota(jnp.int32, (TOKENS, TOKENS), 0), 16)
    patch_col = lax.rem(lax.broadcasted_iota(jnp.int32, (TOKENS, TOKENS), 1), 16)
    mask = patch_row == patch_col
    for h in range(HEADS):
        probs = probabilities(packed_t, h, mask)
        weights = probs.astype(BF16)
        attend(weights, packed_t, h, attended_t)
        head_backward(probs, weights, packed_t, d_attended, h, right_t)
    right_t[1, :, HE:] = attended_t[...]
    pair_t.start(2)
    project_back(right_t, wqt, d_modulated)

    def send_grad(i):
        @pl.when(i != me)
        def _():
            grad_trip.start(lax.rem(i + SEQ - me, SEQ))

    d_offset, d_stretch, d_gate = normalise_back(
        d_modulated, normed_t, scale_t, mod, 3, cot, grad_out, branch_s, send_grad
    )
    clip_first = held.at[0]
    clip_first[2:3, :] = d_gate
    clip_first[3:4, :] = d_offset
    clip_first[4:5, :] = d_stretch
    grad_hidden[here, :] = grad_out[here, :]
    flip(modulated_t, flipped, left_t.at[0])
    pair_t.start(0)
    flip(d_branch_t, flipped, left_t.at[1])
    pair_t.start(1)
    project_out(attended_t, wot, branch_t)
    clip_first[5:6, :] = gate_sum(cot, branch_t)
    pair_t.wait_recv()
    for p in range(3):
        pair_t.multiply(p, whole.at[1, p].reshape(BLOCKS, BLOCK, PART))
        sums_t[p].stage1()

    grad_trip.wait_recv()
    gated(grad_hidden, mod, 2, d_branch_s)
    d_attended[...] = dot(d_branch_s[...], wos[...], NT).astype(BF16)
    flip(d_branch_s, flipped, left_s.at[1])
    pair_s.start(0)
    pair_s.start(1)
    for h in range(HEADS):
        probs = probs_s[h]
        head_backward(probs, probs.astype(BF16), packed_s, d_attended, h, right_s)
    pair_s.start(2)
    sums_t[0].stage2()
    pair_s.wait_recv()
    for p in range(3):
        pair_s.multiply(p, whole.at[0, p].reshape(BLOCKS, BLOCK, PART))
        sums_s[p].stage1()
    sums_t[1].stage2()
    sums_t[2].stage2()
    project_back(right_s, wqs, d_modulated)
    sums_t[0].stage3()
    d_offset, d_stretch = normalise_back(
        d_modulated, normed_s, scale_s, mod, 0, grad_hidden, grad_latents
    )
    clip_first[0:1, :] = d_offset
    clip_first[1:2, :] = d_stretch
    clip_first[6:8, :] = jnp.zeros((2, D), F32)
    clip.start()
    sums_t[1].stage3()
    sums_t[2].stage3()
    sums_t[0].stage4()
    clip.step(0)
    sums_t[1].stage4()
    sums_t[2].stage4()
    clip.step(1)
    for p in range(3):
        sums_s[p].stage2()
    clip.step(2)
    results_t = [sums.stage5() for sums in sums_t]
    write_rows(results_t, dqkv_t, dout_t)
    for p in range(3):
        sums_s[p].stage3()
    clip.step(3)
    for i in range(6):
        moments[i] = held[4, i : i + 1, :]
    for p in range(3):
        sums_s[p].stage4()
    for part in (*trips, pair_s, pair_t, *sums_t, clip):
        part.wait_send()
    results_s = [sums.stage5() for sums in sums_s]
    write_rows(results_s, dqkv_s, dout_s)
    for part in sums_s:
        part.wait_send()


def write_rows(results, dqkv, dout):
    for p, (low, high) in enumerate(results):
        dqkv[:, PART * p : PART * p + PART] = low
        start = 2 * HE + PART * p
        if p == 0:
            dqkv[:, start : start + PART] = high
        elif p == 1:
            dqkv[:, start:] = high[:, : PACKED - start]
            dout[:, : PART - (PACKED - start)] = high[:, PACKED - start :]
        else:
            dout[:, start - PACKED :] = high


def copy_out(*refs):
    sources, targets, sems = refs[:6], refs[6:12], refs[12]
    copies = [pltpu.make_async_copy(a, b, sems.at[i]) for i, (a, b) in enumerate(zip(sources, targets))]
    for copy in copies:
        copy.start()
    for copy in copies:
        copy.wait()


def local(latents, cotangent, modulation, spatial_qkv, spatial_out, temporal_qkv, temporal_out):
    vm = pl.BlockSpec(memory_space=pltpu.VMEM)
    hbm = pl.BlockSpec(memory_space=pl.ANY)
    sds = jax.ShapeDtypeStruct

    def bf16(*shape):
        return pltpu.VMEM(shape, BF16)

    def f32(*shape):
        return pltpu.VMEM(shape, F32)

    wide, wide32, column, narrow = bf16(TOKENS, D), f32(TOKENS, D), f32(TOKENS, 1), bf16(TOKENS, HE)
    three, wq, wo = bf16(TOKENS, PACKED), bf16(PACKED, D), bf16(HE, D)
    left, right = bf16(2, BLOCKS, BLOCK, TOKENS), bf16(2, TOKENS, 2 * HE)
    right_in = bf16(TOKENS, 2 * HE)
    dma = pltpu.SemaphoreType.DMA
    shapes = [
        sds((TOKENS, D), BF16),
        sds((6, 1, D), F32),
        sds((9, PACKED), F32),
        sds((9, HE), F32),
        sds((9, PACKED), F32),
        sds((9, HE), F32),
    ]
    outs = pl.pallas_call(
        kernel,
        out_shape=shapes,
        in_specs=[hbm] * 7,
        out_specs=[vm] * 6,
        scratch_shapes=[
            wide, f32(6, 1, D), wq, wo, wq, wo,
            wide32, column, wide, three, f32(HEADS, TOKENS, TOKENS), narrow,
            wide, narrow, wide32, wide, wide32, column, wide, three, narrow, wide32,
            wide, wide,
            wide, wide, narrow, wide, f32(D, TOKENS),
            left, right, left, right_in, left, right, left, right_in,
            bf16(2, 3, 2, 4, 2, BLOCK, PART), bf16(2, 2, 3, 2, 2, BLOCK, PART), bf16(2, 3, 4, BLOCK, PART),
            bf16(2, 3, 4, BLOCK, PART), bf16(2, 3, 3, BLOCK, PART), bf16(2, 3, BLOCK, PART),
            bf16(2, 3, 3, 32, PART), f32(2, 3, 32, PART), f32(2, 32, PART), f32(2, 3, 32, PART),
            f32(5, 8, D), f32(4, 8, D),
            dma((8,)), dma((4, SEQ)), dma((4, SEQ)), dma((2, 3)), dma((2, 3)),
            dma((2, 3, 11)), dma((2, 3, 11)), dma((4,)), dma((4,)),
        ],
        compiler_params=pltpu.CompilerParams(
            collective_id=0, has_side_effects=True, vmem_limit_bytes=62 * 2**20
        ),
    )(
        latents.reshape(TOKENS, D), cotangent.reshape(TOKENS, D), modulation.transpose(1, 0, 2),
        spatial_qkv.T, spatial_out.T, temporal_qkv.T, temporal_out.T,
    )
    grad, moments, *grads = pl.pallas_call(
        copy_out,
        out_shape=shapes,
        in_specs=[hbm] * 6,
        out_specs=[hbm] * 6,
        scratch_shapes=[dma((6,))],
    )(*outs)
    return (grad.reshape(latents.shape), moments.transpose(1, 0, 2), *grads)


def solution(mesh):
    in_specs = (
        P("dp", "seq", None, None),
        P("dp", "seq", None, None),
        P("dp", None, None),
        P(),
        P(),
        P(),
        P(),
    )
    out_specs = (
        P("dp", "seq", None, None),
        P("dp", None, None),
        P(("dp", "seq"), None),
        P(("dp", "seq"), None),
        P(("dp", "seq"), None),
        P(("dp", "seq"), None),
    )
    return jax.shard_map(local, mesh=mesh, in_specs=in_specs, out_specs=out_specs, check_vma=False)
```

```python
import functools

import jax
import jax.numpy as jnp
from jax import lax
from jax.experimental import pallas as pl
from jax.experimental.pallas import tpu as pltpu
from jax.sharding import PartitionSpec as P

HEADS = 8
HEAD_DIM = 72
HE = HEADS * HEAD_DIM
PACKED = 3 * HE
D = 1152
TOKENS = 256
SEQ = 16
EPSILON = 1e-06
FACTOR = HEAD_DIM**-0.5
BLOCKS = 16
BLOCK = 80
PART = 384
MESH = pl.DeviceIdType.MESH
F32 = jnp.float32
BF16 = jnp.bfloat16

NN = (((1,), (0,)), ((), ()))
NT = (((1,), (1,)), ((), ()))
TN = (((0,), (0,)), ((), ()))


def dot(a, b, dims=NN):
    return lax.dot_general(a, b, dims, preferred_element_type=F32)


def rows_of(i, size):
    return pl.ds(pl.multiple_of(i * size, size), size)


def chunks(size=32):
    return [slice(i, i + size) for i in range(0, TOKENS, size)]


def normalise(source, mod, row, normed, scale, modulated):
    offset = mod[row]
    stretch = 1.0 + mod[row + 1]
    for rows in chunks():
        x = source[rows, :].astype(F32)
        centred = x - jnp.mean(x, axis=-1, keepdims=True)
        spread = jnp.mean(centred * centred, axis=-1, keepdims=True)
        inverse = lax.rsqrt(spread + EPSILON)
        n = centred * inverse
        normed[rows, :] = n
        scale[rows, :] = inverse
        modulated[rows, :] = (n * stretch + offset).astype(BF16)


def project(modulated, weight, packed):
    packed[...] = dot(modulated[...], weight[...], NT).astype(BF16)


def project_out(attended, weight, out):
    out[...] = dot(attended[...], weight[...])


def project_back(right, weight, out):
    total = dot(right[0], weight[: 2 * HE, :]) + dot(right[2, :, :HE], weight[2 * HE :, :])
    out[...] = total.astype(BF16)


def head(ref, h, section=0):
    lane = section * HE + h * HEAD_DIM
    return ref[:, lane : lane + HEAD_DIM]


def probabilities(packed, h, mask):
    scores = dot(head(packed, h, 1), head(packed, h, 0), NT)
    raised = jnp.exp(scores * FACTOR)
    if mask is not None:
        raised = jnp.where(mask, raised, 0.0)
    return raised * (1.0 / jnp.sum(raised, axis=0, keepdims=True))


def head_backward(probs, weights, packed, d_attended, h, right):
    d_head = head(d_attended, h)
    d_weights = dot(head(packed, h, 2), d_head, NT)
    carried = jnp.sum(d_weights * probs, axis=0, keepdims=True)
    d_scores = (probs * (d_weights - carried) * FACTOR).astype(BF16)
    lane = h * HEAD_DIM
    right[0, :, lane : lane + HEAD_DIM] = dot(d_scores, head(packed, h, 1), TN).astype(BF16)
    right[0, :, HE + lane : HE + lane + HEAD_DIM] = dot(d_scores, head(packed, h, 0)).astype(BF16)
    right[2, :, lane : lane + HEAD_DIM] = dot(weights, d_head).astype(BF16)


def attend(weights, packed, h, attended):
    lane = h * HEAD_DIM
    attended[:, lane : lane + HEAD_DIM] = dot(weights, head(packed, h, 2), TN).astype(BF16)


def fold(x):
    return sum(x[8 * i : 8 * i + 8] for i in range(x.shape[0] // 8))


def gated(source, mod, row, out):
    out[...] = (source[...].astype(F32) * mod[row]).astype(BF16)


def gate_sum(upstream, branch):
    total = jnp.zeros((8, D), F32)
    for rows in chunks():
        total = total + fold(upstream[rows, :].astype(F32) * branch[rows, :])
    return jnp.sum(total, axis=0, keepdims=True)


def normalise_back(d_modulated, normed, scale, mod, row, upstream, out):
    stretch = 1.0 + mod[row + 1]
    totals = [jnp.zeros((8, D), F32)] * 2
    for rows in chunks():
        g = d_modulated[rows, :].astype(F32)
        n = normed[rows, :]
        dn = g * stretch
        first = jnp.mean(dn, axis=-1, keepdims=True)
        second = jnp.mean(dn * n, axis=-1, keepdims=True)
        dx = scale[rows, :] * (dn - first - n * second)
        out[rows, :] = (upstream[rows, :].astype(F32) + dx).astype(BF16)
        totals = [total + fold(term) for total, term in zip(totals, (g, g * n))]
    return [jnp.sum(t, axis=0, keepdims=True) for t in totals]


def swap1(i):
    return i + 1 - 2 * lax.rem(i, 2)


class Place:
    def __init__(self):
        self.dp = lax.axis_index("dp")
        self.seq = lax.axis_index("seq")
        self.x = lax.rem(self.dp, 4)
        self.yh = lax.div(self.dp, 4)
        self.yl = lax.div(self.seq, 8)
        self.y = 2 * self.yh + self.yl
        self.z = lax.rem(lax.div(self.seq, 2), 4)
        self.core = lax.rem(self.seq, 2)

    def at(self, x=None, y=None, z=None, core=None):
        x = self.x if x is None else x
        y = self.y if y is None else y
        z = self.z if z is None else z
        core = self.core if core is None else core
        return {
            "dp": 4 * lax.div(y, 2) + x,
            "seq": 8 * lax.rem(y, 2) + 2 * z + core,
        }


def remote(src, dst, send, recv, device):
    return pltpu.make_async_remote_copy(
        src_ref=src, dst_ref=dst, send_sem=send, recv_sem=recv, device_id=device, device_id_type=MESH
    )


class PairTerms:
    def __init__(self, place, left, right, send, recv):
        self.core = place.core
        other = place.at(core=1 - place.core)
        away = 2 - 2 * place.core
        self.left, self.right = left, right
        self.copies = [
            remote(left.at[0, 0], left.at[0, 1], send.at[0], recv.at[0], other),
            remote(left.at[1, 0], left.at[1, 1], send.at[1], recv.at[1], other),
            remote(right.at[away], right.at[away + 1], send.at[2], recv.at[2], other),
        ]

    def start(self, i):
        if i == 1:
            pl.when(self.core == 0)(self.copies[1].start)
        else:
            self.copies[i].start()

    def wait_recv(self):
        self.copies[0].wait_recv()
        pl.when(self.core == 1)(self.copies[1].wait_recv)
        self.copies[2].wait_recv()

    def wait_send(self):
        self.copies[0].wait_send()
        pl.when(self.core == 0)(self.copies[1].wait_send)
        self.copies[2].wait_send()

    def multiply(self, part, out):
        first = PART * part
        pieces = [(first, first + PART)]
        if part == 1:
            pieces = [(first, HE), (HE, first + PART)]
        for low, high in pieces:
            left = self.left[0 if high <= HE else self.core].reshape(2 * TOKENS, D)
            right = self.right[pl.ds(2 * self.core, 2), :, low:high].reshape(2 * TOKENS, high - low)
            total = dot(left, right, TN)
            for k in range(BLOCKS):
                out[k, :72, low - first : high - first] = total[72 * k : 72 * k + 72].astype(BF16)


class Reduction:
    def __init__(self, place, part, whole, first, half, second, quarter, third, final, mine, other, send, recv):
        self.place, self.part = place, part
        self.whole, self.first, self.half, self.second = whole, first, half, second
        self.quarter, self.third, self.final, self.mine, self.other = quarter, third, final, mine, other
        names = ("zyx", "xyz", "yxz")[part]
        self.at = [getattr(place, name) for name in names]
        self.copies = []
        for stage, name in enumerate(names):
            for j in range(1, 4):
                peer = lax.rem(self.at[stage] + j, 4)
                src, dst = (
                    lambda: (self.slab(peer), first.at[j - 1]),
                    lambda: (half.at[peer], second.at[j - 1]),
                    lambda: (quarter.at[window(peer)], third.at[j - 1]),
                )[stage]()
                i = 3 * stage + j - 1
                self.copies.append(remote(src, dst, send.at[i], recv.at[i], place.at(**{name: peer})))
        if part == 0:
            to = [place.at(x=place.z, z=place.x, core=c) for c in (1 - place.core, place.core)]
            self.copies.append(remote(final, other, send.at[9], recv.at[9], to[0]))
            self.trade = remote(final, mine, send.at[10], recv.at[10], to[1])
        else:
            self.copies.append(remote(final, other, send.at[9], recv.at[9], place.at(core=1 - place.core)))

    def slab(self, i):
        if self.part == 2:
            return self.whole.at[lax.div(i, 2), :, lax.rem(i, 2)]
        return self.whole.at[:, i]

    def start(self, stage):
        for i in range(3 * stage, 3 * stage + 3):
            self.copies[i].start()

    def wait(self, stage):
        for i in range(3 * stage, 3 * stage + 3):
            self.copies[i].wait_recv()

    def stage1(self):
        self.start(0)

    def stage2(self):
        self.wait(0)
        own = self.slab(self.at[0])
        for j in range(4):
            at = (j,) if self.part == 2 else (j // 2, j % 2)
            total = own[at].astype(F32)
            for k in range(3):
                total = total + self.first[(k, *at)].astype(F32)
            self.half[j] = total.astype(BF16)
        self.start(1)

    def stage3(self):
        self.wait(1)
        total = self.half[self.at[1]].astype(F32)
        for k in range(3):
            total = total + self.second[k].astype(F32)
        self.quarter[...] = total.astype(BF16)
        self.start(2)

    def stage4(self):
        self.wait(2)
        total = self.quarter[window(self.at[2]), :].astype(F32)
        for k in range(3):
            total = total + self.third[k].astype(F32)
        self.final[...] = total * (1.0 / 8)
        self.copies[9].start()
        if self.part == 0:
            pl.when(self.place.x != self.place.z)(self.trade.start)

    def stage5(self):
        mine = self.final
        if self.part == 0:
            mine = self.mine

            @pl.when(self.place.x == self.place.z)
            def _():
                self.mine[...] = self.final[...]

            pl.when(self.place.x != self.place.z)(self.trade.wait_recv)
        self.copies[9].wait_recv()
        shift = lax.rem(32 - 2 * self.place.z - 9 * self.place.core, 32)
        own = pltpu.roll(mine[...], shift, 0)[:16]
        theirs = pltpu.roll(self.other[...], shift, 0)[:16]
        low = self.place.core == 0
        return jnp.where(low, own, theirs)[:9], jnp.where(low, theirs, own)[:9]

    def wait_send(self):
        for copy in self.copies:
            copy.wait_send()
        if self.part == 0:
            pl.when(self.place.x != self.place.z)(self.trade.wait_send)


def window(i):
    return pl.ds(pl.multiple_of(i * 16, 16), 32)


class ClipSum:
    def __init__(self, place, held, arrived, send, recv):
        self.held, self.arrived = held, arrived
        devices = [
            place.at(core=1 - place.core),
            place.at(z=swap1(place.z)),
            place.at(z=3 - place.z),
            place.at(y=swap1(place.y)),
        ]
        self.copies = [
            remote(held.at[i], arrived.at[i], send.at[i], recv.at[i], device)
            for i, device in enumerate(devices)
        ]

    def start(self):
        self.copies[0].start()

    def step(self, i):
        self.copies[i].wait_recv()
        self.held[i + 1] = self.held[i] + self.arrived[i]
        if i < 3:
            self.copies[i + 1].start()

    def wait_send(self):
        for copy in self.copies:
            copy.wait_send()


class Exchange:
    def __init__(self, source, target, send, recv):
        self.source, self.target, self.send, self.recv = source, target, send, recv
        self.me = lax.axis_index("seq")

    def to(self, j):
        peer = lax.rem(self.me + j, SEQ)
        return pltpu.make_async_remote_copy(
            src_ref=self.source.at[rows_of(peer, 16)],
            dst_ref=self.target.at[rows_of(self.me, 16)],
            send_sem=self.send.at[j],
            recv_sem=self.recv.at[j],
            device_id={"seq": peer},
            device_id_type=MESH,
        )

    def start(self, j):
        self.to(j).start()

    def wait_recv(self):
        def body(j, _):
            sender = lax.rem(self.me + SEQ - j, SEQ)
            pltpu.make_async_remote_copy(
                src_ref=self.source.at[rows_of(sender, 16)],
                dst_ref=self.target.at[rows_of(sender, 16)],
                send_sem=self.send.at[j],
                recv_sem=self.recv.at[j],
                device_id={"seq": sender},
                device_id_type=MESH,
            ).wait_recv()
            return 0

        lax.fori_loop(1, SEQ, body, 0)

    def wait_send(self):
        def body(j, _):
            self.to(j).wait_send()
            return 0

        lax.fori_loop(1, SEQ, body, 0)


def kernel(
    lat_hbm, cot_hbm, mod_hbm, wqs_hbm, wos_hbm, wqt_hbm, wot_hbm,
    grad_latents, moments, dqkv_s, dout_s, dqkv_t, dout_t,
    lat, mod, wqs, wos, wqt, wot,
    normed_s, scale_s, packed_s, probs_s, attended_s, branch_s, hidden_out, hidden,
    cot, normed_t, scale_t, packed_t, attended_t, branch_t, grad_out, grad_hidden, d_attended, d_modulated,
    left_s, right_s, left_t, right_t,
    whole, first_a, first_b, half, second, quarter, third, final, mine, other,
    held, arrived,
    load_sem, send_sem, recv_sem, pair_send, pair_recv, sum_send, sum_recv, clip_send, clip_recv,
):
    place = Place()
    me = place.seq
    here = rows_of(me, 16)
    modulated_s, d_branch_s = left_s.at[0, 0], left_s.at[1, 0]
    modulated_t, d_branch_t = left_t.at[0, 0], left_t.at[1, 0]
    loads = [
        pltpu.make_async_copy(src, dst, load_sem.at[i])
        for i, (src, dst) in enumerate(
            [
                (lat_hbm, lat), (mod_hbm, mod), (wqs_hbm, wqs), (wos_hbm, wos), (wqt_hbm, wqt), (wot_hbm, wot),
                (cot_hbm.at[here], cot.at[here]),
            ]
        )
    ]
    for load in loads:
        load.start()

    barrier = pltpu.get_barrier_semaphore()

    def signal(device):
        pl.semaphore_signal(barrier, inc=1, device_id=device, device_id_type=MESH)

    def greet(j, _):
        signal({"seq": lax.rem(me + j, SEQ)})
        return 0

    lax.fori_loop(1, SEQ, greet, 0)
    for j in range(1, 4):
        signal(place.at(x=lax.rem(place.x + j, 4)))
    signal(place.at(y=lax.rem(place.y + 2, 4)))
    signal(place.at(y=3 - place.y))

    @pl.when(place.x != place.z)
    def _():
        signal(place.at(x=place.z, z=place.x))
        signal(place.at(x=place.z, z=place.x, core=1 - place.core))

    loads[0].wait()
    loads[1].wait()
    normalise(lat, mod, 0, normed_s, scale_s, modulated_s)
    pl.semaphore_wait(barrier, jnp.where(place.x == place.z, SEQ + 4, SEQ + 6))

    trips = [
        Exchange(source, target, send_sem.at[i], recv_sem.at[i])
        for i, (source, target) in enumerate(
            [(cot_hbm, cot), (hidden_out, hidden), (grad_out, grad_hidden)]
        )
    ]
    cot_trip, hidden_trip, grad_trip = trips
    pair_s = PairTerms(place, left_s, right_s, pair_send.at[0], pair_recv.at[0])
    pair_t = PairTerms(place, left_t, right_t, pair_send.at[1], pair_recv.at[1])
    sums_s, sums_t = [
        [
            Reduction(
                place, p, whole.at[l, p], first_b.at[l] if p == 2 else first_a.at[l, p], half.at[l, p],
                second.at[l, p], quarter.at[l, p], third.at[l, p], final.at[l, p], mine.at[l], other.at[l, p],
                sum_send.at[l, p], sum_recv.at[l, p],
            )
            for p in range(3)
        ]
        for l in range(2)
    ]
    clip = ClipSum(place, held, arrived, clip_send, clip_recv)

    def send_all(trip):
        for j in range(1, SEQ):
            trip.start(j)

    send_all(cot_trip)

    loads[2].wait()
    project(modulated_s, wqs, packed_s)
    for h in range(HEADS):
        probs = probabilities(packed_s, h, None)
        probs_s[h] = probs
        attend(probs.astype(BF16), packed_s, h, attended_s)
    loads[3].wait()
    project_out(attended_s, wos, branch_s)
    for rows in chunks():
        hidden_out[rows, :] = (lat[rows, :].astype(F32) + mod[2] * branch_s[rows, :]).astype(BF16)
    send_all(hidden_trip)
    hidden[here, :] = hidden_out[here, :]
    right_s[2, :, HE:] = attended_s[...]
    pair_s.start(0)

    loads[6].wait()
    cot_trip.wait_recv()
    loads[5].wait()
    gated(cot, mod, 5, d_branch_t)
    d_attended[...] = dot(d_branch_t[...], wot[...], NT).astype(BF16)
    pair_t.start(1)
    hidden_trip.wait_recv()
    normalise(hidden, mod, 3, normed_t, scale_t, modulated_t)
    pair_t.start(0)
    loads[4].wait()
    project(modulated_t, wqt, packed_t)
    patch_row = lax.rem(lax.broadcasted_iota(jnp.int32, (TOKENS, TOKENS), 0), 16)
    patch_col = lax.rem(lax.broadcasted_iota(jnp.int32, (TOKENS, TOKENS), 1), 16)
    mask = patch_row == patch_col
    for h in range(HEADS):
        probs = probabilities(packed_t, h, mask)
        weights = probs.astype(BF16)
        attend(weights, packed_t, h, attended_t)
        head_backward(probs, weights, packed_t, d_attended, h, right_t)
    right_t[2, :, HE:] = attended_t[...]
    pair_t.start(2)
    project_back(right_t, wqt, d_modulated)
    d_offset, d_stretch = normalise_back(
        d_modulated, normed_t, scale_t, mod, 3, cot, grad_out
    )
    send_all(grad_trip)
    clip_first = held.at[0]
    clip_first[3:4, :] = d_offset
    clip_first[4:5, :] = d_stretch
    grad_hidden[here, :] = grad_out[here, :]
    pair_t.wait_recv()
    for p in range(3):
        pair_t.multiply(p, whole.at[1, p].reshape(BLOCKS, BLOCK, PART))
        sums_t[p].stage1()
    project_out(attended_t, wot, branch_t)
    clip_first[5:6, :] = gate_sum(cot, branch_t)

    grad_trip.wait_recv()
    gated(grad_hidden, mod, 2, d_branch_s)
    pair_s.start(1)
    d_attended[...] = dot(d_branch_s[...], wos[...], NT).astype(BF16)
    for h in range(HEADS):
        probs = probs_s[h]
        head_backward(probs, probs.astype(BF16), packed_s, d_attended, h, right_s)
    pair_s.start(2)
    pair_s.wait_recv()
    for p in range(3):
        pair_s.multiply(p, whole.at[0, p].reshape(BLOCKS, BLOCK, PART))
        sums_s[p].stage1()
    project_back(right_s, wqs, d_modulated)
    d_offset, d_stretch = normalise_back(
        d_modulated, normed_s, scale_s, mod, 0, grad_hidden, grad_latents
    )
    clip_first[0:1, :] = d_offset
    clip_first[1:2, :] = d_stretch
    clip_first[2:3, :] = gate_sum(grad_hidden, branch_s)
    clip_first[6:8, :] = jnp.zeros((2, D), F32)
    clip.start()
    for p in range(3):
        sums_t[p].stage2()
    clip.step(0)
    for p in range(3):
        sums_t[p].stage3()
    clip.step(1)
    for p in range(3):
        sums_s[p].stage2()
    for p in range(3):
        sums_t[p].stage4()
    clip.step(2)
    for p in range(3):
        sums_s[p].stage3()
    write_rows([sums.stage5() for sums in sums_t], dqkv_t, dout_t)
    clip.step(3)
    for i in range(6):
        moments[i] = held[4, i : i + 1, :]
    for p in range(3):
        sums_s[p].stage4()
    for part in (*trips, pair_s, pair_t, *sums_t, clip):
        part.wait_send()
    results_s = [sums.stage5() for sums in sums_s]
    write_rows(results_s, dqkv_s, dout_s)
    for part in sums_s:
        part.wait_send()


def write_rows(results, dqkv, dout):
    for p, (low, high) in enumerate(results):
        dqkv[:, PART * p : PART * p + PART] = low
        start = 2 * HE + PART * p
        if p == 0:
            dqkv[:, start : start + PART] = high
        elif p == 1:
            dqkv[:, start:] = high[:, : PACKED - start]
            dout[:, : PART - (PACKED - start)] = high[:, PACKED - start :]
        else:
            dout[:, start - PACKED :] = high


def copy_out(*refs):
    for source, target in zip(refs[:6], refs[6:]):
        target[...] = source[...]


def local(latents, cotangent, modulation, spatial_qkv, spatial_out, temporal_qkv, temporal_out):
    vm = pl.BlockSpec(memory_space=pltpu.VMEM)
    hbm = pl.BlockSpec(memory_space=pl.ANY)
    sds = jax.ShapeDtypeStruct

    def bf16(*shape):
        return pltpu.VMEM(shape, BF16)

    def f32(*shape):
        return pltpu.VMEM(shape, F32)

    wide, wide32, column, narrow = bf16(TOKENS, D), f32(TOKENS, D), f32(TOKENS, 1), bf16(TOKENS, HE)
    three, wq, wo = bf16(TOKENS, PACKED), bf16(PACKED, D), bf16(HE, D)
    left, right = bf16(2, 2, TOKENS, D), bf16(4, TOKENS, 2 * HE)
    dma = pltpu.SemaphoreType.DMA
    shapes = [
        sds((TOKENS, D), BF16),
        sds((6, 1, D), F32),
        sds((9, PACKED), F32),
        sds((9, HE), F32),
        sds((9, PACKED), F32),
        sds((9, HE), F32),
    ]
    outs = pl.pallas_call(
        kernel,
        out_shape=shapes,
        in_specs=[hbm] * 7,
        out_specs=[vm] * 6,
        scratch_shapes=[
            wide, f32(6, 1, D), wq, wo, wq, wo,
            wide32, column, three, f32(HEADS, TOKENS, TOKENS), narrow, wide32, wide, wide,
            wide, wide32, column, three, narrow, wide32, wide, wide, narrow, wide,
            left, right, left, right,
            bf16(2, 3, 2, 4, 2, BLOCK, PART), bf16(2, 2, 3, 2, 2, BLOCK, PART), bf16(2, 3, 4, BLOCK, PART),
            bf16(2, 3, 4, BLOCK, PART), bf16(2, 3, 3, BLOCK, PART), bf16(2, 3, BLOCK, PART),
            bf16(2, 3, 3, 32, PART), f32(2, 3, 32, PART), f32(2, 32, PART), f32(2, 3, 32, PART),
            f32(5, 8, D), f32(4, 8, D),
            dma((7,)), dma((3, SEQ)), dma((3, SEQ)), dma((2, 3)), dma((2, 3)),
            dma((2, 3, 11)), dma((2, 3, 11)), dma((4,)), dma((4,)),
        ],
        compiler_params=pltpu.CompilerParams(
            collective_id=0, has_side_effects=True, vmem_limit_bytes=62 * 2**20
        ),
    )(
        latents.reshape(TOKENS, D), cotangent.reshape(TOKENS, D), modulation.transpose(1, 0, 2),
        spatial_qkv.T, spatial_out.T, temporal_qkv.T, temporal_out.T,
    )
    grad, moments, *grads = pl.pallas_call(
        copy_out,
        out_shape=shapes,
        in_specs=[vm] * 6,
        out_specs=[vm] * 6,
    )(*outs)
    return (grad.reshape(latents.shape), moments.transpose(1, 0, 2), *grads)


def solution(mesh):
    in_specs = (
        P("dp", "seq", None, None),
        P("dp", "seq", None, None),
        P("dp", None, None),
        P(),
        P(),
        P(),
        P(),
    )
    out_specs = (
        P("dp", "seq", None, None),
        P("dp", None, None),
        P(("dp", "seq"), None),
        P(("dp", "seq"), None),
        P(("dp", "seq"), None),
        P(("dp", "seq"), None),
    )
    return jax.shard_map(local, mesh=mesh, in_specs=in_specs, out_specs=out_specs, check_vma=False)
```

```python
import functools

import jax
import jax.numpy as jnp
from jax import lax
from jax.experimental import pallas as pl
from jax.experimental.pallas import tpu as pltpu
from jax.sharding import PartitionSpec as P

HEADS = 8
HEAD_DIM = 72
HE = HEADS * HEAD_DIM
PACKED = 3 * HE
D = 1152
TOKENS = 256
SEQ = 16
EPSILON = 1e-06
FACTOR = HEAD_DIM**-0.5
SLAB = 144
BLOCK = 80
PART = 384
MESH = pl.DeviceIdType.MESH
F32 = jnp.float32
BF16 = jnp.bfloat16

NN = (((1,), (0,)), ((), ()))
NT = (((1,), (1,)), ((), ()))
TN = (((0,), (0,)), ((), ()))


def dot(a, b, dims=NN):
    return lax.dot_general(a, b, dims, preferred_element_type=F32)


def rows_of(i, size):
    return pl.ds(pl.multiple_of(i * size, size), size)


def chunks(size=32):
    return [slice(i, i + size) for i in range(0, TOKENS, size)]


def normalise(source, mod, row, normed, scale, modulated):
    offset = mod[row]
    stretch = 1.0 + mod[row + 1]
    for rows in chunks():
        x = source[rows, :].astype(F32)
        centred = x - jnp.mean(x, axis=-1, keepdims=True)
        spread = jnp.mean(centred * centred, axis=-1, keepdims=True)
        inverse = lax.rsqrt(spread + EPSILON)
        n = centred * inverse
        normed[rows, :] = n
        scale[rows, :] = inverse
        modulated[rows, :] = (n * stretch + offset).astype(BF16)


def project(modulated, weight, packed):
    packed[...] = dot(modulated[...], weight[...], NT).astype(BF16)


def project_out(attended, weight, out):
    out[...] = dot(attended[...], weight[...])


def project_back(right, weight, out):
    total = dot(right[0], weight[: 2 * HE, :]) + dot(right[2, :, :HE], weight[2 * HE :, :])
    out[...] = total.astype(BF16)


def head(ref, h, section=0):
    lane = section * HE + h * HEAD_DIM
    return ref[:, lane : lane + HEAD_DIM]


def probabilities(packed, h, mask):
    scores = dot(head(packed, h, 1), head(packed, h, 0), NT)
    raised = jnp.exp(scores * FACTOR)
    if mask is not None:
        raised = jnp.where(mask, raised, 0.0)
    return raised * (1.0 / jnp.sum(raised, axis=0, keepdims=True))


def head_backward(probs, weights, packed, d_attended, h, right):
    d_head = head(d_attended, h)
    d_weights = dot(head(packed, h, 2), d_head, NT)
    carried = jnp.sum(d_weights * probs, axis=0, keepdims=True)
    d_scores = (probs * (d_weights - carried) * FACTOR).astype(BF16)
    lane = h * HEAD_DIM
    right[0, :, lane : lane + HEAD_DIM] = dot(d_scores, head(packed, h, 1), TN).astype(BF16)
    right[0, :, HE + lane : HE + lane + HEAD_DIM] = dot(d_scores, head(packed, h, 0)).astype(BF16)
    right[2, :, lane : lane + HEAD_DIM] = dot(weights, d_head).astype(BF16)


def attend(weights, packed, h, attended):
    lane = h * HEAD_DIM
    attended[:, lane : lane + HEAD_DIM] = dot(weights, head(packed, h, 2), TN).astype(BF16)


def fold(x):
    return sum(x[8 * i : 8 * i + 8] for i in range(x.shape[0] // 8))


def gated(source, mod, row, out):
    out[...] = (source[...].astype(F32) * mod[row]).astype(BF16)


def gate_sum(upstream, branch):
    total = jnp.zeros((8, D), F32)
    for rows in chunks():
        total = total + fold(upstream[rows, :].astype(F32) * branch[rows, :])
    return jnp.sum(total, axis=0, keepdims=True)


def normalise_back(d_modulated, normed, scale, mod, row, upstream, out):
    stretch = 1.0 + mod[row + 1]
    totals = [jnp.zeros((8, D), F32)] * 2
    for rows in chunks():
        g = d_modulated[rows, :].astype(F32)
        n = normed[rows, :]
        dn = g * stretch
        first = jnp.mean(dn, axis=-1, keepdims=True)
        second = jnp.mean(dn * n, axis=-1, keepdims=True)
        dx = scale[rows, :] * (dn - first - n * second)
        out[rows, :] = (upstream[rows, :].astype(F32) + dx).astype(BF16)
        totals = [total + fold(term) for total, term in zip(totals, (g, g * n))]
    return [jnp.sum(t, axis=0, keepdims=True) for t in totals]


def swap1(i):
    return i + 1 - 2 * lax.rem(i, 2)


class Place:
    def __init__(self):
        self.dp = lax.axis_index("dp")
        self.seq = lax.axis_index("seq")
        self.x = lax.rem(self.dp, 4)
        self.yh = lax.div(self.dp, 4)
        self.yl = lax.div(self.seq, 8)
        self.y = 2 * self.yh + self.yl
        self.z = lax.rem(lax.div(self.seq, 2), 4)
        self.core = lax.rem(self.seq, 2)

    def at(self, x=None, y=None, z=None, core=None):
        x = self.x if x is None else x
        y = self.y if y is None else y
        z = self.z if z is None else z
        core = self.core if core is None else core
        return {
            "dp": 4 * lax.div(y, 2) + x,
            "seq": 8 * lax.rem(y, 2) + 2 * z + core,
        }

    def pair(self, i):
        near, far = swap1(i), 3 - i
        return near + self.core * (far - near), far + self.core * (near - far)


def remote(src, dst, send, recv, device):
    return pltpu.make_async_remote_copy(
        src_ref=src, dst_ref=dst, send_sem=send, recv_sem=recv, device_id=device, device_id_type=MESH
    )


class PairTerms:
    def __init__(self, place, left, right, send, recv):
        self.core = place.core
        other = place.at(core=1 - place.core)
        away = 2 - 2 * place.core
        self.left, self.right = left, right
        self.copies = [
            remote(left.at[0, 0], left.at[0, 1], send.at[0], recv.at[0], other),
            remote(left.at[1, 0], left.at[1, 1], send.at[1], recv.at[1], other),
            remote(right.at[away], right.at[away + 1], send.at[2], recv.at[2], other),
        ]

    def start(self, i):
        if i == 1:
            pl.when(self.core == 0)(self.copies[1].start)
        else:
            self.copies[i].start()

    def wait_recv(self):
        self.copies[0].wait_recv()
        pl.when(self.core == 1)(self.copies[1].wait_recv)
        self.copies[2].wait_recv()

    def wait_send(self):
        self.copies[0].wait_send()
        pl.when(self.core == 0)(self.copies[1].wait_send)
        self.copies[2].wait_send()

    def multiply(self, part, out):
        first = PART * part
        pieces = [(first, first + PART)]
        if part == 1:
            pieces = [(first, HE), (HE, first + PART)]
        for low, high in pieces:
            left = self.left[0 if high <= HE else self.core].reshape(2 * TOKENS, D)
            right = self.right[pl.ds(2 * self.core, 2), :, low:high].reshape(2 * TOKENS, high - low)
            total = dot(left, right, TN)
            for yh in range(2):
                for x in range(4):
                    row = SLAB * (4 * yh + x)
                    out[yh, x, :, low - first : high - first] = total[row : row + SLAB].astype(BF16)


class Reduction:
    def __init__(self, place, names, whole, first, pair, half, second, quarter, third, final, mine, other, send, recv):
        self.place, self.names = place, names
        self.whole, self.first, self.pair, self.half, self.second = whole, first, pair, half, second
        self.quarter, self.third, self.final, self.mine, self.other = quarter, third, final, mine, other
        self.at = [getattr(place, name) for name in names]
        a = self.at[0]
        a1, self.a2 = place.pair(a)
        to_a1, to_a2 = place.at(**{names[0]: a1}), place.at(**{names[0]: self.a2})
        self.copies = [
            remote(whole.at[:, lax.rem(a + 2, 4)], first.at[1], send.at[0], recv.at[0], to_a1),
            remote(whole.at[:, a1], first.at[0], send.at[1], recv.at[1], to_a1),
            remote(whole.at[:, self.a2], pair, send.at[2], recv.at[2], to_a2),
        ]
        for stage in (1, 2):
            for j in range(1, 4):
                peer = lax.rem(self.at[stage] + j, 4)
                if stage == 1:
                    src, dst = half.at[peer], second.at[j - 1]
                else:
                    src, dst = quarter.at[window(peer)], third.at[j - 1]
                i = 3 * stage + j - 1
                self.copies.append(remote(src, dst, send.at[i], recv.at[i], place.at(**{names[stage]: peer})))
        turned = {n: getattr(place, m) for n, m in zip("xyz", names)}
        self.trades = names != "xyz"
        self.moves = place.x != getattr(place, names[0])
        core = 1 - place.core
        self.copies.append(remote(final, other, send.at[9], recv.at[9], place.at(**turned, core=core)))
        self.trade = remote(final, mine, send.at[10], recv.at[10], place.at(**turned)) if self.trades else None

    def start(self, stage):
        for i in range(3 * stage, 3 * stage + 3):
            self.copies[i].start()

    def wait(self, stage):
        for i in range(3 * stage, 3 * stage + 3):
            self.copies[i].wait_recv()

    def stage0(self):
        self.copies[0].start()
        self.copies[1].start()

    def stage1(self):
        self.copies[0].wait_recv()
        for yh in range(2):
            kept = self.whole.at[yh, self.a2]
            kept[...] = (kept[...].astype(F32) + self.first[1, yh].astype(F32)).astype(BF16)
        self.copies[2].start()

    def stage2(self):
        self.copies[1].wait_recv()
        self.copies[2].wait_recv()
        for yh in range(2):
            total = self.whole[yh, self.at[0]].astype(F32) + self.first[0, yh].astype(F32)
            total = total + self.pair[yh].astype(F32)
            self.half[2 * yh, :72] = total[:72].astype(BF16)
            self.half[2 * yh + 1, :72] = total[72:].astype(BF16)
        self.start(1)

    def stage3(self):
        self.wait(1)
        total = self.half[self.at[1]].astype(F32)
        for k in range(3):
            total = total + self.second[k].astype(F32)
        self.quarter[...] = total.astype(BF16)
        self.start(2)

    def stage4(self):
        self.wait(2)
        total = self.quarter[window(self.at[2]), :].astype(F32)
        for k in range(3):
            total = total + self.third[k].astype(F32)
        self.final[...] = total * (1.0 / 8)
        self.copies[9].start()
        if self.trades:
            pl.when(self.moves)(self.trade.start)

    def stage5(self):
        mine = self.final
        if self.trades:
            mine = self.mine

            @pl.when(jnp.logical_not(self.moves))
            def _():
                self.mine[...] = self.final[...]

            pl.when(self.moves)(self.trade.wait_recv)
        self.copies[9].wait_recv()
        shift = lax.rem(32 - 2 * self.place.z - 9 * self.place.core, 32)
        own = pltpu.roll(mine[...], shift, 0)[:16]
        theirs = pltpu.roll(self.other[...], shift, 0)[:16]
        low = self.place.core == 0
        return jnp.where(low, own, theirs)[:9], jnp.where(low, theirs, own)[:9]

    def wait_send(self):
        for copy in self.copies:
            copy.wait_send()
        if self.trades:
            pl.when(self.moves)(self.trade.wait_send)


def window(i):
    return pl.ds(pl.multiple_of(i * 16, 16), 32)


class ClipSum:
    def __init__(self, place, held, arrived, send, recv):
        self.held, self.arrived = held, arrived
        devices = [
            place.at(core=1 - place.core),
            place.at(z=swap1(place.z)),
            place.at(z=3 - place.z),
            place.at(y=swap1(place.y)),
        ]
        self.copies = [
            remote(held.at[i], arrived.at[i], send.at[i], recv.at[i], device)
            for i, device in enumerate(devices)
        ]

    def start(self):
        self.copies[0].start()

    def step(self, i):
        self.copies[i].wait_recv()
        self.held[i + 1] = self.held[i] + self.arrived[i]
        if i < 3:
            self.copies[i + 1].start()

    def wait_send(self):
        for copy in self.copies:
            copy.wait_send()


class Exchange:
    def __init__(self, source, target, send, recv):
        self.source, self.target, self.send, self.recv = source, target, send, recv
        self.me = lax.axis_index("seq")

    def to(self, j):
        peer = lax.rem(self.me + j, SEQ)
        return pltpu.make_async_remote_copy(
            src_ref=self.source.at[rows_of(peer, 16)],
            dst_ref=self.target.at[rows_of(self.me, 16)],
            send_sem=self.send.at[j],
            recv_sem=self.recv.at[j],
            device_id={"seq": peer},
            device_id_type=MESH,
        )

    def start(self, j):
        self.to(j).start()

    def wait_recv(self):
        def body(j, _):
            sender = lax.rem(self.me + SEQ - j, SEQ)
            pltpu.make_async_remote_copy(
                src_ref=self.source.at[rows_of(sender, 16)],
                dst_ref=self.target.at[rows_of(sender, 16)],
                send_sem=self.send.at[j],
                recv_sem=self.recv.at[j],
                device_id={"seq": sender},
                device_id_type=MESH,
            ).wait_recv()
            return 0

        lax.fori_loop(1, SEQ, body, 0)

    def wait_send(self):
        def body(j, _):
            self.to(j).wait_send()
            return 0

        lax.fori_loop(1, SEQ, body, 0)


def kernel(
    lat_hbm, cot_hbm, mod_hbm, wqs_hbm, wos_hbm, wqt_hbm, wot_hbm,
    grad_latents, moments, dqkv_s, dout_s, dqkv_t, dout_t,
    lat, mod, wqs, wos, wqt, wot,
    normed_s, scale_s, packed_s, probs_s, attended_s, branch_s, hidden_out, hidden,
    cot, normed_t, scale_t, packed_t, attended_t, branch_t, grad_out, grad_hidden, d_attended, d_modulated,
    left_s, right_s, left_t, right_t,
    whole, first, pair, half, second, quarter, third, final, mine, other,
    held, arrived,
    load_sem, send_sem, recv_sem, pair_send, pair_recv, sum_send, sum_recv, clip_send, clip_recv,
):
    place = Place()
    me = place.seq
    here = rows_of(me, 16)
    modulated_s, d_branch_s = left_s.at[0, 0], left_s.at[1, 0]
    modulated_t, d_branch_t = left_t.at[0, 0], left_t.at[1, 0]
    loads = [
        pltpu.make_async_copy(src, dst, load_sem.at[i])
        for i, (src, dst) in enumerate(
            [
                (lat_hbm, lat), (mod_hbm, mod), (wqs_hbm, wqs), (wos_hbm, wos), (wqt_hbm, wqt), (wot_hbm, wot),
                (cot_hbm.at[here], cot.at[here]),
            ]
        )
    ]
    for load in loads:
        load.start()

    barrier = pltpu.get_barrier_semaphore()

    def signal(device):
        pl.semaphore_signal(barrier, inc=1, device_id=device, device_id_type=MESH)

    def greet(j, _):
        signal({"seq": lax.rem(me + j, SEQ)})
        return 0

    lax.fori_loop(1, SEQ, greet, 0)
    for j in range(1, 4):
        signal(place.at(x=lax.rem(place.x + j, 4)))
    signal(place.at(y=lax.rem(place.y + 2, 4)))
    signal(place.at(y=3 - place.y))

    @pl.when(place.x != place.z)
    def _():
        signal(place.at(x=place.z, z=place.x))
        signal(place.at(x=place.z, z=place.x, core=1 - place.core))

    @pl.when(place.x != place.y)
    def _():
        signal(place.at(x=place.y, y=place.x))
        signal(place.at(x=place.y, y=place.x, core=1 - place.core))

    loads[0].wait()
    loads[1].wait()
    normalise(lat, mod, 0, normed_s, scale_s, modulated_s)
    traders = jnp.where(place.x == place.z, 0, 2) + jnp.where(place.x == place.y, 0, 2)
    pl.semaphore_wait(barrier, SEQ + 4 + traders)

    trips = [
        Exchange(source, target, send_sem.at[i], recv_sem.at[i])
        for i, (source, target) in enumerate(
            [(cot_hbm, cot), (hidden_out, hidden), (grad_out, grad_hidden)]
        )
    ]
    cot_trip, hidden_trip, grad_trip = trips
    pair_s = PairTerms(place, left_s, right_s, pair_send.at[0], pair_recv.at[0])
    pair_t = PairTerms(place, left_t, right_t, pair_send.at[1], pair_recv.at[1])
    sums_s, sums_t = [
        [
            Reduction(
                place, names[p], whole.at[l, p], first.at[l, p], pair.at[l, p], half.at[l, p], second.at[l, p],
                quarter.at[l, p], third.at[l, p], final.at[l, p], mine.at[l, p], other.at[l, p],
                sum_send.at[l, p], sum_recv.at[l, p],
            )
            for p in range(3)
        ]
        for l, names in enumerate((("xyz", "yxz", "zyx"), ("xyz", "xyz", "yxz")))
    ]
    clip = ClipSum(place, held, arrived, clip_send, clip_recv)

    def send_all(trip):
        for j in range(1, SEQ):
            trip.start(j)

    send_all(cot_trip)

    loads[2].wait()
    project(modulated_s, wqs, packed_s)
    for h in range(HEADS):
        probs = probabilities(packed_s, h, None)
        probs_s[h] = probs
        attend(probs.astype(BF16), packed_s, h, attended_s)
    loads[3].wait()
    project_out(attended_s, wos, branch_s)
    for rows in chunks():
        hidden_out[rows, :] = (lat[rows, :].astype(F32) + mod[2] * branch_s[rows, :]).astype(BF16)
    send_all(hidden_trip)
    hidden[here, :] = hidden_out[here, :]
    right_s[2, :, HE:] = attended_s[...]
    pair_s.start(0)

    loads[6].wait()
    cot_trip.wait_recv()
    loads[5].wait()
    gated(cot, mod, 5, d_branch_t)
    d_attended[...] = dot(d_branch_t[...], wot[...], NT).astype(BF16)
    pair_t.start(1)
    hidden_trip.wait_recv()
    normalise(hidden, mod, 3, normed_t, scale_t, modulated_t)
    pair_t.start(0)
    loads[4].wait()
    project(modulated_t, wqt, packed_t)
    patch_row = lax.rem(lax.broadcasted_iota(jnp.int32, (TOKENS, TOKENS), 0), 16)
    patch_col = lax.rem(lax.broadcasted_iota(jnp.int32, (TOKENS, TOKENS), 1), 16)
    mask = patch_row == patch_col
    for h in range(HEADS):
        probs = probabilities(packed_t, h, mask)
        weights = probs.astype(BF16)
        attend(weights, packed_t, h, attended_t)
        head_backward(probs, weights, packed_t, d_attended, h, right_t)
    right_t[2, :, HE:] = attended_t[...]
    pair_t.start(2)
    project_back(right_t, wqt, d_modulated)
    d_offset, d_stretch = normalise_back(
        d_modulated, normed_t, scale_t, mod, 3, cot, grad_out
    )
    send_all(grad_trip)
    clip_first = held.at[0]
    clip_first[3:4, :] = d_offset
    clip_first[4:5, :] = d_stretch
    grad_hidden[here, :] = grad_out[here, :]
    pair_t.wait_recv()
    for p in range(3):
        pair_t.multiply(p, whole.at[1, p])
        if p < 2:
            sums_t[p].stage0()
    project_out(attended_t, wot, branch_t)
    clip_first[5:6, :] = gate_sum(cot, branch_t)
    sums_t[0].stage1()

    grad_trip.wait_recv()
    sums_t[2].stage0()
    gated(grad_hidden, mod, 2, d_branch_s)
    pair_s.start(1)
    d_attended[...] = dot(d_branch_s[...], wos[...], NT).astype(BF16)
    for h in range(HEADS):
        probs = probs_s[h]
        head_backward(probs, probs.astype(BF16), packed_s, d_attended, h, right_s)
    pair_s.start(2)
    pair_s.wait_recv()
    for p in (2, 1, 0):
        pair_s.multiply(p, whole.at[0, p])
        sums_s[p].stage0()
    sums_t[1].stage1()
    sums_t[0].stage2()
    sums_t[2].stage1()
    project_back(right_s, wqs, d_modulated)
    d_offset, d_stretch = normalise_back(
        d_modulated, normed_s, scale_s, mod, 0, grad_hidden, grad_latents
    )
    clip_first[0:1, :] = d_offset
    clip_first[1:2, :] = d_stretch
    clip_first[2:3, :] = gate_sum(grad_hidden, branch_s)
    clip_first[6:8, :] = jnp.zeros((2, D), F32)
    clip.start()
    sums_t[1].stage2()
    for p in (2, 1, 0):
        sums_s[p].stage1()
    sums_t[2].stage2()
    clip.step(0)
    for p in range(3):
        sums_t[p].stage3()
    clip.step(1)
    for p in (2, 1, 0):
        sums_s[p].stage2()
    for p in range(3):
        sums_t[p].stage4()
    clip.step(2)
    for p in (2, 1, 0):
        sums_s[p].stage3()
    write_rows([sums.stage5() for sums in sums_t], dqkv_t, dout_t)
    clip.step(3)
    for i in range(6):
        moments[i] = held[4, i : i + 1, :]
    for p in (2, 1, 0):
        sums_s[p].stage4()
    for part in (*trips, pair_s, pair_t, *sums_t, clip):
        part.wait_send()
    results_s = [sums.stage5() for sums in sums_s]
    write_rows(results_s, dqkv_s, dout_s)
    for part in sums_s:
        part.wait_send()


def write_rows(results, dqkv, dout):
    for p, (low, high) in enumerate(results):
        dqkv[:, PART * p : PART * p + PART] = low
        start = 2 * HE + PART * p
        if p == 0:
            dqkv[:, start : start + PART] = high
        elif p == 1:
            dqkv[:, start:] = high[:, : PACKED - start]
            dout[:, : PART - (PACKED - start)] = high[:, PACKED - start :]
        else:
            dout[:, start - PACKED :] = high


def copy_out(*refs):
    for source, target in zip(refs[:6], refs[6:]):
        target[...] = source[...]


def local(latents, cotangent, modulation, spatial_qkv, spatial_out, temporal_qkv, temporal_out):
    vm = pl.BlockSpec(memory_space=pltpu.VMEM)
    hbm = pl.BlockSpec(memory_space=pl.ANY)
    sds = jax.ShapeDtypeStruct

    def bf16(*shape):
        return pltpu.VMEM(shape, BF16)

    def f32(*shape):
        return pltpu.VMEM(shape, F32)

    wide, wide32, column, narrow = bf16(TOKENS, D), f32(TOKENS, D), f32(TOKENS, 1), bf16(TOKENS, HE)
    three, wq, wo = bf16(TOKENS, PACKED), bf16(PACKED, D), bf16(HE, D)
    left, right = bf16(2, 2, TOKENS, D), bf16(4, TOKENS, 2 * HE)
    dma = pltpu.SemaphoreType.DMA
    shapes = [
        sds((TOKENS, D), BF16),
        sds((6, 1, D), F32),
        sds((9, PACKED), F32),
        sds((9, HE), F32),
        sds((9, PACKED), F32),
        sds((9, HE), F32),
    ]
    outs = pl.pallas_call(
        kernel,
        out_shape=shapes,
        in_specs=[hbm] * 7,
        out_specs=[vm] * 6,
        scratch_shapes=[
            wide, f32(6, 1, D), wq, wo, wq, wo,
            wide32, column, three, f32(HEADS, TOKENS, TOKENS), narrow, wide32, wide, wide,
            wide, wide32, column, three, narrow, wide32, wide, wide, narrow, wide,
            left, right, left, right,
            bf16(2, 3, 2, 4, SLAB, PART), bf16(2, 3, 2, 2, SLAB, PART), bf16(2, 3, 2, SLAB, PART),
            bf16(2, 3, 4, BLOCK, PART), bf16(2, 3, 3, BLOCK, PART), bf16(2, 3, BLOCK, PART),
            bf16(2, 3, 3, 32, PART), f32(2, 3, 32, PART), f32(2, 3, 32, PART), f32(2, 3, 32, PART),
            f32(5, 8, D), f32(4, 8, D),
            dma((7,)), dma((3, SEQ)), dma((3, SEQ)), dma((2, 3)), dma((2, 3)),
            dma((2, 3, 11)), dma((2, 3, 11)), dma((4,)), dma((4,)),
        ],
        compiler_params=pltpu.CompilerParams(
            collective_id=0, has_side_effects=True, vmem_limit_bytes=62 * 2**20
        ),
    )(
        latents.reshape(TOKENS, D), cotangent.reshape(TOKENS, D), modulation.transpose(1, 0, 2),
        spatial_qkv.T, spatial_out.T, temporal_qkv.T, temporal_out.T,
    )
    grad, moments, *grads = pl.pallas_call(
        copy_out,
        out_shape=shapes,
        in_specs=[vm] * 6,
        out_specs=[vm] * 6,
    )(*outs)
    return (grad.reshape(latents.shape), moments.transpose(1, 0, 2), *grads)


def solution(mesh):
    in_specs = (
        P("dp", "seq", None, None),
        P("dp", "seq", None, None),
        P("dp", None, None),
        P(),
        P(),
        P(),
        P(),
    )
    out_specs = (
        P("dp", "seq", None, None),
        P("dp", None, None),
        P(("dp", "seq"), None),
        P(("dp", "seq"), None),
        P(("dp", "seq"), None),
        P(("dp", "seq"), None),
    )
    return jax.shard_map(local, mesh=mesh, in_specs=in_specs, out_specs=out_specs, check_vma=False)
```

```python
import functools

import jax
import jax.numpy as jnp
from jax import lax
from jax.experimental import pallas as pl
from jax.experimental.pallas import tpu as pltpu
from jax.sharding import PartitionSpec as P

HEADS = 8
HEAD_DIM = 72
HE = HEADS * HEAD_DIM
PACKED = 3 * HE
D = 1152
TOKENS = 256
SEQ = 16
EPSILON = 1e-06
FACTOR = HEAD_DIM**-0.5
SLAB = 144
BLOCK = 80
PART = 384
MESH = pl.DeviceIdType.MESH
F32 = jnp.float32
BF16 = jnp.bfloat16

NN = (((1,), (0,)), ((), ()))
NT = (((1,), (1,)), ((), ()))
TN = (((0,), (0,)), ((), ()))


def dot(a, b, dims=NN):
    return lax.dot_general(a, b, dims, preferred_element_type=F32)


def rows_of(i, size):
    return pl.ds(pl.multiple_of(i * size, size), size)


def chunks(size=32):
    return [slice(i, i + size) for i in range(0, TOKENS, size)]


def normalise(source, mod, row, normed, scale, modulated):
    offset = mod[row]
    stretch = 1.0 + mod[row + 1]
    for rows in chunks():
        x = source[rows, :].astype(F32)
        centred = x - jnp.mean(x, axis=-1, keepdims=True)
        spread = jnp.mean(centred * centred, axis=-1, keepdims=True)
        inverse = lax.rsqrt(spread + EPSILON)
        n = centred * inverse
        normed[rows, :] = n
        scale[rows, :] = inverse
        modulated[rows, :] = (n * stretch + offset).astype(BF16)


def project(modulated, weight, packed):
    packed[...] = dot(modulated[...], weight[...], NT).astype(BF16)


def project_out(attended, weight, out):
    out[...] = dot(attended[...], weight[...])


def project_back(right, weight, out):
    total = dot(right[0], weight[: 2 * HE, :]) + dot(right[2, :, :HE], weight[2 * HE :, :])
    out[...] = total.astype(BF16)


def head(ref, h, section=0):
    lane = section * HE + h * HEAD_DIM
    return ref[:, lane : lane + HEAD_DIM]


def probabilities(packed, h, mask):
    scores = dot(head(packed, h, 1), head(packed, h, 0), NT)
    raised = jnp.exp(scores * FACTOR)
    if mask is not None:
        raised = jnp.where(mask, raised, 0.0)
    return raised * (1.0 / jnp.sum(raised, axis=0, keepdims=True))


def head_backward(probs, weights, packed, d_attended, h, right):
    d_head = head(d_attended, h)
    d_weights = dot(head(packed, h, 2), d_head, NT)
    carried = jnp.sum(d_weights * probs, axis=0, keepdims=True)
    d_scores = (probs * (d_weights - carried) * FACTOR).astype(BF16)
    lane = h * HEAD_DIM
    right[0, :, lane : lane + HEAD_DIM] = dot(d_scores, head(packed, h, 1), TN).astype(BF16)
    right[0, :, HE + lane : HE + lane + HEAD_DIM] = dot(d_scores, head(packed, h, 0)).astype(BF16)
    right[2, :, lane : lane + HEAD_DIM] = dot(weights, d_head).astype(BF16)


def attend(weights, packed, h, attended):
    lane = h * HEAD_DIM
    attended[:, lane : lane + HEAD_DIM] = dot(weights, head(packed, h, 2), TN).astype(BF16)


def fold(x):
    return sum(x[8 * i : 8 * i + 8] for i in range(x.shape[0] // 8))


def gated(source, mod, row, out):
    out[...] = (source[...].astype(F32) * mod[row]).astype(BF16)


def gate_sum(upstream, branch):
    total = jnp.zeros((8, D), F32)
    for rows in chunks():
        total = total + fold(upstream[rows, :].astype(F32) * branch[rows, :])
    return jnp.sum(total, axis=0, keepdims=True)


def normalise_back(d_modulated, normed, scale, mod, row, upstream, out):
    stretch = 1.0 + mod[row + 1]
    totals = [jnp.zeros((8, D), F32)] * 2
    for rows in chunks():
        g = d_modulated[rows, :].astype(F32)
        n = normed[rows, :]
        dn = g * stretch
        first = jnp.mean(dn, axis=-1, keepdims=True)
        second = jnp.mean(dn * n, axis=-1, keepdims=True)
        dx = scale[rows, :] * (dn - first - n * second)
        out[rows, :] = (upstream[rows, :].astype(F32) + dx).astype(BF16)
        totals = [total + fold(term) for total, term in zip(totals, (g, g * n))]
    return [jnp.sum(t, axis=0, keepdims=True) for t in totals]


def swap1(i):
    return i + 1 - 2 * lax.rem(i, 2)


class Place:
    def __init__(self):
        self.dp = lax.axis_index("dp")
        self.seq = lax.axis_index("seq")
        self.x = lax.rem(self.dp, 4)
        self.yh = lax.div(self.dp, 4)
        self.yl = lax.div(self.seq, 8)
        self.y = 2 * self.yh + self.yl
        self.z = lax.rem(lax.div(self.seq, 2), 4)
        self.core = lax.rem(self.seq, 2)

    def at(self, x=None, y=None, z=None, core=None):
        x = self.x if x is None else x
        y = self.y if y is None else y
        z = self.z if z is None else z
        core = self.core if core is None else core
        return {
            "dp": 4 * lax.div(y, 2) + x,
            "seq": 8 * lax.rem(y, 2) + 2 * z + core,
        }

    def pair(self, i):
        near, far = swap1(i), 3 - i
        return near + self.core * (far - near), far + self.core * (near - far)


def remote(src, dst, send, recv, device):
    return pltpu.make_async_remote_copy(
        src_ref=src, dst_ref=dst, send_sem=send, recv_sem=recv, device_id=device, device_id_type=MESH
    )


class PairTerms:
    def __init__(self, place, left, right, send, recv):
        self.core = place.core
        other = place.at(core=1 - place.core)
        away = 2 - 2 * place.core
        self.left, self.right = left, right
        self.copies = [
            remote(left.at[0, 0], left.at[0, 1], send.at[0], recv.at[0], other),
            remote(left.at[1, 0], left.at[1, 1], send.at[1], recv.at[1], other),
            remote(right.at[away], right.at[away + 1], send.at[2], recv.at[2], other),
        ]

    def start(self, i):
        if i == 1:
            pl.when(self.core == 0)(self.copies[1].start)
        else:
            self.copies[i].start()

    def wait_recv(self):
        self.copies[0].wait_recv()
        pl.when(self.core == 1)(self.copies[1].wait_recv)
        self.copies[2].wait_recv()

    def wait_send(self):
        self.copies[0].wait_send()
        pl.when(self.core == 0)(self.copies[1].wait_send)
        self.copies[2].wait_send()

    def multiply(self, part, out):
        first = PART * part
        pieces = [(first, first + PART)]
        if part == 1:
            pieces = [(first, HE), (HE, first + PART)]
        for low, high in pieces:
            left = self.left[0 if high <= HE else self.core].reshape(2 * TOKENS, D)
            right = self.right[pl.ds(2 * self.core, 2), :, low:high].reshape(2 * TOKENS, high - low)
            total = dot(left, right, TN)
            for yh in range(2):
                for x in range(4):
                    row = SLAB * (4 * yh + x)
                    out[yh, x, :, low - first : high - first] = total[row : row + SLAB].astype(BF16)


class Reduction:
    def __init__(self, place, names, whole, first, pair, half, second, quarter, third, final, other, send, recv):
        self.place, self.names = place, names
        self.whole, self.first, self.pair, self.half, self.second = whole, first, pair, half, second
        self.quarter, self.third, self.final, self.other = quarter, third, final, other
        self.at = [getattr(place, name) for name in names]
        a = self.at[0]
        a1, self.a2 = place.pair(a)
        to_a1, to_a2 = place.at(**{names[0]: a1}), place.at(**{names[0]: self.a2})
        self.copies = [
            remote(whole.at[:, lax.rem(a + 2, 4)], first.at[1], send.at[0], recv.at[0], to_a1),
            remote(whole.at[:, a1], first.at[0], send.at[1], recv.at[1], to_a1),
            remote(whole.at[:, self.a2], pair, send.at[2], recv.at[2], to_a2),
        ]
        for j in range(1, 4):
            peer = lax.rem(self.at[1] + j, 4)
            self.copies.append(
                remote(half.at[peer], second.at[j - 1], send.at[2 + j], recv.at[2 + j], place.at(**{names[1]: peer}))
            )
        x, y, z = place.x, place.y, place.z
        owner = {n: getattr(place, m) for n, m in zip("xy", names)}
        came = dict(zip(names[:2], (x, y)))
        self.owns = [jnp.logical_and(jnp.logical_and(owner["x"] == x, owner["y"] == y), z == j) for j in range(4)]
        self.took = [
            jnp.logical_and(
                jnp.logical_and(getattr(place, names[0]) == x, getattr(place, names[1]) == y), self.at[2] == k
            )
            for k in range(4)
        ]
        self.out = [
            remote(
                quarter.at[window(j)], third.at[self.at[2]], send.at[6 + j], recv.at[6 + self.at[2]],
                place.at(**owner, z=j),
            )
            for j in range(4)
        ]
        self.back = [
            remote(
                quarter.at[window(z)], third.at[k], send.at[6 + k], recv.at[6 + k],
                place.at(**came, **{names[2]: k}),
            )
            for k in range(4)
        ]
        self.swap = remote(final, other, send.at[10], recv.at[10], place.at(core=1 - place.core))

    def start_out(self):
        for j in range(4):
            pl.when(jnp.logical_not(self.owns[j]))(self.out[j].start)

            @pl.when(self.owns[j])
            def _():
                self.third[self.at[2]] = self.quarter[window(j), :]

    def wait_back(self):
        for k in range(4):
            pl.when(jnp.logical_not(self.took[k]))(self.back[k].wait_recv)

    def stage0(self):
        self.copies[0].start()
        self.copies[1].start()

    def stage1(self):
        self.copies[0].wait_recv()
        for yh in range(2):
            kept = self.whole.at[yh, self.a2]
            kept[...] = (kept[...].astype(F32) + self.first[1, yh].astype(F32)).astype(BF16)
        self.copies[2].start()

    def stage2(self):
        self.copies[1].wait_recv()
        self.copies[2].wait_recv()
        for yh in range(2):
            total = self.whole[yh, self.at[0]].astype(F32) + self.first[0, yh].astype(F32)
            total = total + self.pair[yh].astype(F32)
            self.half[2 * yh, :72] = total[:72].astype(BF16)
            self.half[2 * yh + 1, :72] = total[72:].astype(BF16)
        for copy in self.copies[3:]:
            copy.start()

    def stage3(self):
        for copy in self.copies[3:]:
            copy.wait_recv()
        total = self.half[self.at[1]].astype(F32)
        for k in range(3):
            total = total + self.second[k].astype(F32)
        self.quarter[...] = total.astype(BF16)
        self.start_out()

    def stage4(self):
        self.wait_back()
        total = self.third[0].astype(F32)
        for k in range(1, 4):
            total = total + self.third[k].astype(F32)
        total = total * (1.0 / 8)
        start, core = 2 * self.place.z, self.place.core
        self.final[...] = pltpu.roll(total, lax.rem(32 - start - 9 * (1 - core), 32), 0)[:16]
        self.swap.start()
        return pltpu.roll(total, lax.rem(32 - start - 9 * core, 32), 0)[:16]

    def stage5(self, own):
        self.swap.wait_recv()
        low = self.place.core == 0
        theirs = self.other[...]
        return jnp.where(low, own, theirs)[:9], jnp.where(low, theirs, own)[:9]

    def wait_send(self):
        for copy in self.copies:
            copy.wait_send()
        for j in range(4):
            pl.when(jnp.logical_not(self.owns[j]))(self.out[j].wait_send)
        self.swap.wait_send()


def window(i):
    return pl.ds(pl.multiple_of(i * 16, 16), 32)


class ClipSum:
    def __init__(self, place, held, arrived, send, recv):
        self.held, self.arrived = held, arrived
        devices = [
            place.at(core=1 - place.core),
            place.at(z=swap1(place.z)),
            place.at(z=3 - place.z),
            place.at(y=swap1(place.y)),
        ]
        self.copies = [
            remote(held.at[i], arrived.at[i], send.at[i], recv.at[i], device)
            for i, device in enumerate(devices)
        ]

    def start(self):
        self.copies[0].start()

    def step(self, i):
        self.copies[i].wait_recv()
        self.held[i + 1] = self.held[i] + self.arrived[i]
        if i < 3:
            self.copies[i + 1].start()

    def wait_send(self):
        for copy in self.copies:
            copy.wait_send()


class Exchange:
    def __init__(self, source, target, send, recv):
        self.source, self.target, self.send, self.recv = source, target, send, recv
        self.me = lax.axis_index("seq")

    def to(self, j):
        peer = lax.rem(self.me + j, SEQ)
        return pltpu.make_async_remote_copy(
            src_ref=self.source.at[rows_of(peer, 16)],
            dst_ref=self.target.at[rows_of(self.me, 16)],
            send_sem=self.send.at[j],
            recv_sem=self.recv.at[j],
            device_id={"seq": peer},
            device_id_type=MESH,
        )

    def start(self, j):
        self.to(j).start()

    def wait_recv(self):
        def body(j, _):
            sender = lax.rem(self.me + SEQ - j, SEQ)
            pltpu.make_async_remote_copy(
                src_ref=self.source.at[rows_of(sender, 16)],
                dst_ref=self.target.at[rows_of(sender, 16)],
                send_sem=self.send.at[j],
                recv_sem=self.recv.at[j],
                device_id={"seq": sender},
                device_id_type=MESH,
            ).wait_recv()
            return 0

        lax.fori_loop(1, SEQ, body, 0)

    def wait_send(self):
        def body(j, _):
            self.to(j).wait_send()
            return 0

        lax.fori_loop(1, SEQ, body, 0)


def kernel(
    lat_hbm, cot_hbm, mod_hbm, wqs_hbm, wos_hbm, wqt_hbm, wot_hbm,
    grad_latents, moments, dqkv_s, dout_s, dqkv_t, dout_t,
    lat, mod, wqs, wos, wqt, wot,
    normed_s, scale_s, packed_s, probs_s, attended_s, branch_s, hidden_out, hidden,
    cot, normed_t, scale_t, packed_t, probs_t, attended_t, branch_t, grad_out, grad_hidden, d_attended, d_modulated,
    left_s, right_s, left_t, right_t,
    whole, first, pair, half, second, quarter, third, final, other,
    held, arrived,
    load_sem, send_sem, recv_sem, pair_send, pair_recv, sum_send, sum_recv, clip_send, clip_recv,
):
    place = Place()
    me = place.seq
    here = rows_of(me, 16)
    modulated_s, d_branch_s = left_s.at[0, 0], left_s.at[1, 0]
    modulated_t, d_branch_t = left_t.at[0, 0], left_t.at[1, 0]
    loads = [
        pltpu.make_async_copy(src, dst, load_sem.at[i])
        for i, (src, dst) in enumerate(
            [
                (lat_hbm, lat), (mod_hbm, mod), (wqs_hbm, wqs), (wos_hbm, wos), (wqt_hbm, wqt), (wot_hbm, wot),
                (cot_hbm.at[here], cot.at[here]),
            ]
        )
    ]
    for load in loads:
        load.start()

    barrier = pltpu.get_barrier_semaphore()

    def signal(device):
        pl.semaphore_signal(barrier, inc=1, device_id=device, device_id_type=MESH)

    def greet(j, _):
        signal({"seq": lax.rem(me + j, SEQ)})
        return 0

    lax.fori_loop(1, SEQ, greet, 0)
    for j in range(1, 4):
        for k in range(4):
            signal(place.at(x=lax.rem(place.x + j, 4), z=k))
    signal(place.at(y=lax.rem(place.y + 2, 4)))
    signal(place.at(y=3 - place.y))

    @pl.when(place.x != place.y)
    def _():
        for k in range(4):
            signal(place.at(x=place.y, y=place.x, z=k))

    loads[0].wait()
    loads[1].wait()
    normalise(lat, mod, 0, normed_s, scale_s, modulated_s)
    trips = [
        Exchange(source, target, send_sem.at[i], recv_sem.at[i])
        for i, (source, target) in enumerate(
            [(cot_hbm, cot), (hidden_out, hidden), (grad_out, grad_hidden)]
        )
    ]
    cot_trip, hidden_trip, grad_trip = trips
    pair_s = PairTerms(place, left_s, right_s, pair_send.at[0], pair_recv.at[0])
    pair_t = PairTerms(place, left_t, right_t, pair_send.at[1], pair_recv.at[1])
    sums_s, sums_t = [
        [
            Reduction(
                place, names[p], whole.at[l, p], first.at[l, p], pair.at[l, p], half.at[l, p], second.at[l, p],
                quarter.at[l, p], third.at[l, p], final.at[l, p], other.at[l, p],
                sum_send.at[l, p], sum_recv.at[l, p],
            )
            for p in range(3)
        ]
        for l, names in enumerate((("xyz", "yxz", "zyx"), ("xyz", "xyz", "yxz")))
    ]
    clip = ClipSum(place, held, arrived, clip_send, clip_recv)

    def send_all(trip):
        for j in range(1, SEQ):
            trip.start(j)

    loads[2].wait()
    project(modulated_s, wqs, packed_s)
    for h in range(HEADS):
        probs = probabilities(packed_s, h, None)
        probs_s[h] = probs
        attend(probs.astype(BF16), packed_s, h, attended_s)
    loads[3].wait()
    project_out(attended_s, wos, branch_s)
    for rows in chunks():
        hidden_out[rows, :] = (lat[rows, :].astype(F32) + mod[2] * branch_s[rows, :]).astype(BF16)
    pl.semaphore_wait(barrier, SEQ + 13 + jnp.where(place.x == place.y, 0, 4))
    send_all(hidden_trip)
    send_all(cot_trip)
    hidden[here, :] = hidden_out[here, :]
    right_s[2, :, HE:] = attended_s[...]
    pair_s.start(0)

    hidden_trip.wait_recv()
    normalise(hidden, mod, 3, normed_t, scale_t, modulated_t)
    pair_t.start(0)
    loads[4].wait()
    project(modulated_t, wqt, packed_t)
    patch_row = lax.rem(lax.broadcasted_iota(jnp.int32, (TOKENS, TOKENS), 0), 16)
    patch_col = lax.rem(lax.broadcasted_iota(jnp.int32, (TOKENS, TOKENS), 1), 16)
    mask = patch_row == patch_col
    for h in range(HEADS):
        probs = probabilities(packed_t, h, mask)
        probs_t[h] = probs
        attend(probs.astype(BF16), packed_t, h, attended_t)
    loads[5].wait()
    project_out(attended_t, wot, branch_t)
    loads[6].wait()
    cot_trip.wait_recv()
    gated(cot, mod, 5, d_branch_t)
    d_attended[...] = dot(d_branch_t[...], wot[...], NT).astype(BF16)
    pair_t.start(1)
    for h in range(HEADS):
        probs = probs_t[h]
        head_backward(probs, probs.astype(BF16), packed_t, d_attended, h, right_t)
    right_t[2, :, HE:] = attended_t[...]
    pair_t.start(2)
    project_back(right_t, wqt, d_modulated)
    d_offset, d_stretch = normalise_back(
        d_modulated, normed_t, scale_t, mod, 3, cot, grad_out
    )
    send_all(grad_trip)
    clip_first = held.at[0]
    clip_first[3:4, :] = d_offset
    clip_first[4:5, :] = d_stretch
    grad_hidden[here, :] = grad_out[here, :]
    pair_t.wait_recv()
    for p in range(3):
        pair_t.multiply(p, whole.at[1, p])
        if p < 2:
            sums_t[p].stage0()
    clip_first[5:6, :] = gate_sum(cot, branch_t)
    sums_t[0].stage1()

    grad_trip.wait_recv()
    sums_t[2].stage0()
    gated(grad_hidden, mod, 2, d_branch_s)
    pair_s.start(1)
    d_attended[...] = dot(d_branch_s[...], wos[...], NT).astype(BF16)
    for h in range(HEADS):
        probs = probs_s[h]
        head_backward(probs, probs.astype(BF16), packed_s, d_attended, h, right_s)
    pair_s.start(2)
    project_back(right_s, wqs, d_modulated)
    pair_s.wait_recv()
    for p in (2, 1, 0):
        pair_s.multiply(p, whole.at[0, p])
        sums_s[p].stage0()
    sums_t[1].stage1()
    sums_t[0].stage2()
    sums_t[2].stage1()
    d_offset, d_stretch = normalise_back(
        d_modulated, normed_s, scale_s, mod, 0, grad_hidden, grad_latents
    )
    clip_first[0:1, :] = d_offset
    clip_first[1:2, :] = d_stretch
    clip_first[2:3, :] = gate_sum(grad_hidden, branch_s)
    clip_first[6:8, :] = jnp.zeros((2, D), F32)
    clip.start()
    sums_t[1].stage2()
    for p in (2, 1, 0):
        sums_s[p].stage1()
    sums_t[2].stage2()
    clip.step(0)
    for p in range(3):
        sums_t[p].stage3()
    clip.step(1)
    for p in (2, 1, 0):
        sums_s[p].stage2()
    owned = [sums.stage4() for sums in sums_t]
    clip.step(2)
    for p in (2, 1, 0):
        sums_s[p].stage3()
    write_rows([sums.stage5(own) for sums, own in zip(sums_t, owned)], dqkv_t, dout_t)
    clip.step(3)
    for i in range(6):
        moments[i] = held[4, i : i + 1, :]
    owned = [sums.stage4() for sums in sums_s]
    for part in (*trips, pair_s, pair_t, *sums_t, clip):
        part.wait_send()
    results_s = [sums.stage5(own) for sums, own in zip(sums_s, owned)]
    write_rows(results_s, dqkv_s, dout_s)
    for part in sums_s:
        part.wait_send()


def write_rows(results, dqkv, dout):
    for p, (low, high) in enumerate(results):
        dqkv[:, PART * p : PART * p + PART] = low
        start = 2 * HE + PART * p
        if p == 0:
            dqkv[:, start : start + PART] = high
        elif p == 1:
            dqkv[:, start:] = high[:, : PACKED - start]
            dout[:, : PART - (PACKED - start)] = high[:, PACKED - start :]
        else:
            dout[:, start - PACKED :] = high


def copy_out(*refs):
    for source, target in zip(refs[:6], refs[6:]):
        target[...] = source[...]


def local(latents, cotangent, modulation, spatial_qkv, spatial_out, temporal_qkv, temporal_out):
    vm = pl.BlockSpec(memory_space=pltpu.VMEM)
    hbm = pl.BlockSpec(memory_space=pl.ANY)
    sds = jax.ShapeDtypeStruct

    def bf16(*shape):
        return pltpu.VMEM(shape, BF16)

    def f32(*shape):
        return pltpu.VMEM(shape, F32)

    wide, wide32, column, narrow = bf16(TOKENS, D), f32(TOKENS, D), f32(TOKENS, 1), bf16(TOKENS, HE)
    three, wq, wo = bf16(TOKENS, PACKED), bf16(PACKED, D), bf16(HE, D)
    left, right = bf16(2, 2, TOKENS, D), bf16(4, TOKENS, 2 * HE)
    dma = pltpu.SemaphoreType.DMA
    shapes = [
        sds((TOKENS, D), BF16),
        sds((6, 1, D), F32),
        sds((9, PACKED), F32),
        sds((9, HE), F32),
        sds((9, PACKED), F32),
        sds((9, HE), F32),
    ]
    outs = pl.pallas_call(
        kernel,
        out_shape=shapes,
        in_specs=[hbm] * 7,
        out_specs=[vm] * 6,
        scratch_shapes=[
            wide, f32(6, 1, D), wq, wo, wq, wo,
            wide32, column, three, f32(HEADS, TOKENS, TOKENS), narrow, wide32, wide, wide,
            wide, wide32, column, three, f32(HEADS, TOKENS, TOKENS), narrow, wide32, wide, wide, narrow, wide,
            left, right, left, right,
            bf16(2, 3, 2, 4, SLAB, PART), bf16(2, 3, 2, 2, SLAB, PART), bf16(2, 3, 2, SLAB, PART),
            bf16(2, 3, 4, BLOCK, PART), bf16(2, 3, 3, BLOCK, PART), bf16(2, 3, BLOCK, PART),
            bf16(2, 3, 4, 32, PART), f32(2, 3, 16, PART), f32(2, 3, 16, PART),
            f32(5, 8, D), f32(4, 8, D),
            dma((7,)), dma((3, SEQ)), dma((3, SEQ)), dma((2, 3)), dma((2, 3)),
            dma((2, 3, 11)), dma((2, 3, 11)), dma((4,)), dma((4,)),
        ],
        compiler_params=pltpu.CompilerParams(
            collective_id=0, has_side_effects=True, vmem_limit_bytes=62 * 2**20
        ),
    )(
        latents.reshape(TOKENS, D), cotangent.reshape(TOKENS, D), modulation.transpose(1, 0, 2),
        spatial_qkv.T, spatial_out.T, temporal_qkv.T, temporal_out.T,
    )
    grad, moments, *grads = pl.pallas_call(
        copy_out,
        out_shape=shapes,
        in_specs=[vm] * 6,
        out_specs=[vm] * 6,
    )(*outs)
    return (grad.reshape(latents.shape), moments.transpose(1, 0, 2), *grads)


def solution(mesh):
    in_specs = (
        P("dp", "seq", None, None),
        P("dp", "seq", None, None),
        P("dp", None, None),
        P(),
        P(),
        P(),
        P(),
    )
    out_specs = (
        P("dp", "seq", None, None),
        P("dp", None, None),
        P(("dp", "seq"), None),
        P(("dp", "seq"), None),
        P(("dp", "seq"), None),
        P(("dp", "seq"), None),
    )
    return jax.shard_map(local, mesh=mesh, in_specs=in_specs, out_specs=out_specs, check_vma=False)
```

```python
import functools

import jax
import jax.numpy as jnp
from jax import lax
from jax.experimental import pallas as pl
from jax.experimental.pallas import tpu as pltpu
from jax.sharding import PartitionSpec as P

HEADS = 8
HEAD_DIM = 72
HE = HEADS * HEAD_DIM
PACKED = 3 * HE
D = 1152
TOKENS = 256
SEQ = 16
EPSILON = 1e-06
FACTOR = HEAD_DIM**-0.5
SLAB = 144
BLOCK = 80
PART = 384
MESH = pl.DeviceIdType.MESH
F32 = jnp.float32
BF16 = jnp.bfloat16

NN = (((1,), (0,)), ((), ()))
NT = (((1,), (1,)), ((), ()))
TN = (((0,), (0,)), ((), ()))


def dot(a, b, dims=NN):
    return lax.dot_general(a, b, dims, preferred_element_type=F32)


def rows_of(i, size):
    return pl.ds(pl.multiple_of(i * size, size), size)


def chunks(size=32):
    return [slice(i, i + size) for i in range(0, TOKENS, size)]


def normalise(source, mod, row, normed, scale, modulated):
    offset = mod[row]
    stretch = 1.0 + mod[row + 1]
    for rows in chunks():
        x = source[rows, :].astype(F32)
        centred = x - jnp.mean(x, axis=-1, keepdims=True)
        spread = jnp.mean(centred * centred, axis=-1, keepdims=True)
        inverse = lax.rsqrt(spread + EPSILON)
        n = centred * inverse
        normed[rows, :] = n
        scale[rows, :] = inverse
        modulated[rows, :] = (n * stretch + offset).astype(BF16)


def project(modulated, weight, packed):
    packed[...] = dot(modulated[...], weight[...], NT).astype(BF16)


def project_out(attended, weight, out):
    out[...] = dot(attended[...], weight[...])


def project_back(right, weight, out):
    total = dot(right[0], weight[: 2 * HE, :]) + dot(right[2, :, :HE], weight[2 * HE :, :])
    out[...] = total.astype(BF16)


def head(ref, h, section=0):
    lane = section * HE + h * HEAD_DIM
    return ref[:, lane : lane + HEAD_DIM]


def probabilities(packed, h, mask):
    scores = dot(head(packed, h, 1), head(packed, h, 0), NT)
    raised = jnp.exp(scores * FACTOR)
    if mask is not None:
        raised = jnp.where(mask, raised, 0.0)
    return raised * (1.0 / jnp.sum(raised, axis=0, keepdims=True))


def head_backward(probs, weights, packed, d_attended, h, right):
    d_head = head(d_attended, h)
    d_weights = dot(head(packed, h, 2), d_head, NT)
    carried = jnp.sum(d_weights * probs, axis=0, keepdims=True)
    d_scores = (probs * (d_weights - carried) * FACTOR).astype(BF16)
    lane = h * HEAD_DIM
    right[0, :, lane : lane + HEAD_DIM] = dot(d_scores, head(packed, h, 1), TN).astype(BF16)
    right[0, :, HE + lane : HE + lane + HEAD_DIM] = dot(d_scores, head(packed, h, 0)).astype(BF16)
    right[2, :, lane : lane + HEAD_DIM] = dot(weights, d_head).astype(BF16)


def attend(weights, packed, h, attended):
    lane = h * HEAD_DIM
    attended[:, lane : lane + HEAD_DIM] = dot(weights, head(packed, h, 2), TN).astype(BF16)


def fold(x):
    return sum(x[8 * i : 8 * i + 8] for i in range(x.shape[0] // 8))


def gated(source, mod, row, out):
    out[...] = (source[...].astype(F32) * mod[row]).astype(BF16)


def gate_sum(upstream, branch):
    total = jnp.zeros((8, D), F32)
    for rows in chunks():
        total = total + fold(upstream[rows, :].astype(F32) * branch[rows, :])
    return jnp.sum(total, axis=0, keepdims=True)


def normalise_back(d_modulated, normed, scale, mod, row, upstream, out):
    stretch = 1.0 + mod[row + 1]
    totals = [jnp.zeros((8, D), F32)] * 2
    for rows in chunks():
        g = d_modulated[rows, :].astype(F32)
        n = normed[rows, :]
        dn = g * stretch
        first = jnp.mean(dn, axis=-1, keepdims=True)
        second = jnp.mean(dn * n, axis=-1, keepdims=True)
        dx = scale[rows, :] * (dn - first - n * second)
        out[rows, :] = (upstream[rows, :].astype(F32) + dx).astype(BF16)
        totals = [total + fold(term) for total, term in zip(totals, (g, g * n))]
    return [jnp.sum(t, axis=0, keepdims=True) for t in totals]


def swap1(i):
    return i + 1 - 2 * lax.rem(i, 2)


class Place:
    def __init__(self):
        self.dp = lax.axis_index("dp")
        self.seq = lax.axis_index("seq")
        self.x = lax.rem(self.dp, 4)
        self.yh = lax.div(self.dp, 4)
        self.yl = lax.div(self.seq, 8)
        self.y = 2 * self.yh + self.yl
        self.z = lax.rem(lax.div(self.seq, 2), 4)
        self.core = lax.rem(self.seq, 2)

    def at(self, x=None, y=None, z=None, core=None):
        x = self.x if x is None else x
        y = self.y if y is None else y
        z = self.z if z is None else z
        core = self.core if core is None else core
        return {
            "dp": 4 * lax.div(y, 2) + x,
            "seq": 8 * lax.rem(y, 2) + 2 * z + core,
        }

    def pair(self, i):
        near, far = swap1(i), 3 - i
        return near + self.core * (far - near), far + self.core * (near - far)


def remote(src, dst, send, recv, device):
    return pltpu.make_async_remote_copy(
        src_ref=src, dst_ref=dst, send_sem=send, recv_sem=recv, device_id=device, device_id_type=MESH
    )


class PairTerms:
    def __init__(self, place, left, right, send, recv):
        self.core = place.core
        other = place.at(core=1 - place.core)
        away = 2 - 2 * place.core
        self.left, self.right = left, right
        self.copies = [
            remote(left.at[0, 0], left.at[0, 1], send.at[0], recv.at[0], other),
            remote(left.at[1, 0], left.at[1, 1], send.at[1], recv.at[1], other),
            remote(right.at[away], right.at[away + 1], send.at[2], recv.at[2], other),
        ]

    def start(self, i):
        if i == 1:
            pl.when(self.core == 0)(self.copies[1].start)
        else:
            self.copies[i].start()

    def wait_recv(self):
        self.copies[0].wait_recv()
        pl.when(self.core == 1)(self.copies[1].wait_recv)
        self.copies[2].wait_recv()

    def wait_send(self):
        self.copies[0].wait_send()
        pl.when(self.core == 0)(self.copies[1].wait_send)
        self.copies[2].wait_send()

    def multiply(self, part, out):
        first = PART * part
        pieces = [(first, first + PART)]
        if part == 1:
            pieces = [(first, HE), (HE, first + PART)]
        for low, high in pieces:
            left = self.left[0 if high <= HE else self.core].reshape(2 * TOKENS, D)
            right = self.right[pl.ds(2 * self.core, 2), :, low:high].reshape(2 * TOKENS, high - low)
            total = dot(left, right, TN)
            for yh in range(2):
                for x in range(4):
                    row = SLAB * (4 * yh + x)
                    out[yh, x, :, low - first : high - first] = total[row : row + SLAB].astype(BF16)


class Reduction:
    def __init__(self, place, names, whole, first, pair, half, second, quarter, third, final, other, send, recv):
        self.place, self.names = place, names
        self.whole, self.first, self.pair, self.half, self.second = whole, first, pair, half, second
        self.quarter, self.third, self.final, self.other = quarter, third, final, other
        self.at = [getattr(place, name) for name in names]
        a = self.at[0]
        a1, self.a2 = place.pair(a)
        to_a1, to_a2 = place.at(**{names[0]: a1}), place.at(**{names[0]: self.a2})
        self.copies = [
            remote(whole.at[:, lax.rem(a + 2, 4)], first.at[1], send.at[0], recv.at[0], to_a1),
            remote(whole.at[:, a1], first.at[0], send.at[1], recv.at[1], to_a1),
            remote(whole.at[:, self.a2], pair, send.at[2], recv.at[2], to_a2),
        ]
        for j in range(1, 4):
            peer = lax.rem(self.at[1] + j, 4)
            self.copies.append(
                remote(half.at[peer], second.at[j - 1], send.at[2 + j], recv.at[2 + j], place.at(**{names[1]: peer}))
            )
        x, y, z = place.x, place.y, place.z
        owner = {n: getattr(place, m) for n, m in zip("xy", names)}
        came = dict(zip(names[:2], (x, y)))
        self.owns = [jnp.logical_and(jnp.logical_and(owner["x"] == x, owner["y"] == y), z == j) for j in range(4)]
        self.took = [
            jnp.logical_and(
                jnp.logical_and(getattr(place, names[0]) == x, getattr(place, names[1]) == y), self.at[2] == k
            )
            for k in range(4)
        ]
        self.out = [
            remote(
                quarter.at[window(j)], third.at[self.at[2]], send.at[6 + j], recv.at[6 + self.at[2]],
                place.at(**owner, z=j),
            )
            for j in range(4)
        ]
        self.back = [
            remote(
                quarter.at[window(z)], third.at[k], send.at[6 + k], recv.at[6 + k],
                place.at(**came, **{names[2]: k}),
            )
            for k in range(4)
        ]
        self.swap = remote(final, other, send.at[10], recv.at[10], place.at(core=1 - place.core))

    def start_out(self):
        for j in range(4):
            pl.when(jnp.logical_not(self.owns[j]))(self.out[j].start)

            @pl.when(self.owns[j])
            def _():
                self.third[self.at[2]] = self.quarter[window(j), :]

    def wait_back(self):
        for k in range(4):
            pl.when(jnp.logical_not(self.took[k]))(self.back[k].wait_recv)

    def stage0(self):
        self.copies[0].start()
        self.copies[1].start()

    def stage1(self):
        self.copies[0].wait_recv()
        for yh in range(2):
            kept = self.whole.at[yh, self.a2]
            kept[...] = (kept[...].astype(F32) + self.first[1, yh].astype(F32)).astype(BF16)
        self.copies[2].start()

    def stage2(self):
        self.copies[1].wait_recv()
        self.copies[2].wait_recv()
        for yh in range(2):
            total = self.whole[yh, self.at[0]].astype(F32) + self.first[0, yh].astype(F32)
            total = total + self.pair[yh].astype(F32)
            self.half[2 * yh, :72] = total[:72].astype(BF16)
            self.half[2 * yh + 1, :72] = total[72:].astype(BF16)
        for copy in self.copies[3:]:
            copy.start()

    def stage3(self):
        for copy in self.copies[3:]:
            copy.wait_recv()
        total = self.half[self.at[1]].astype(F32)
        for k in range(3):
            total = total + self.second[k].astype(F32)
        self.quarter[...] = total.astype(BF16)
        self.start_out()

    def stage4(self):
        self.wait_back()
        total = self.third[0].astype(F32)
        for k in range(1, 4):
            total = total + self.third[k].astype(F32)
        total = total * (1.0 / 8)
        start, core = 2 * self.place.z, self.place.core
        self.final[...] = pltpu.roll(total, lax.rem(32 - start - 9 * (1 - core), 32), 0)[:16]
        self.swap.start()
        return pltpu.roll(total, lax.rem(32 - start - 9 * core, 32), 0)[:16]

    def stage5(self, own):
        self.swap.wait_recv()
        low = self.place.core == 0
        theirs = self.other[...]
        return jnp.where(low, own, theirs)[:9], jnp.where(low, theirs, own)[:9]

    def wait_send(self):
        for copy in self.copies:
            copy.wait_send()
        for j in range(4):
            pl.when(jnp.logical_not(self.owns[j]))(self.out[j].wait_send)
        self.swap.wait_send()


def window(i):
    return pl.ds(pl.multiple_of(i * 16, 16), 32)


class ClipSum:
    def __init__(self, place, held, arrived, send, recv):
        self.held, self.arrived = held, arrived
        devices = [
            place.at(core=1 - place.core),
            place.at(z=swap1(place.z)),
            place.at(z=3 - place.z),
            place.at(y=swap1(place.y)),
        ]
        self.copies = [
            remote(held.at[i], arrived.at[i], send.at[i], recv.at[i], device)
            for i, device in enumerate(devices)
        ]

    def start(self):
        self.copies[0].start()

    def step(self, i):
        self.copies[i].wait_recv()
        self.held[i + 1] = self.held[i] + self.arrived[i]
        if i < 3:
            self.copies[i + 1].start()

    def wait_send(self):
        for copy in self.copies:
            copy.wait_send()


class Exchange:
    def __init__(self, source, target, send, recv):
        self.source, self.target, self.send, self.recv = source, target, send, recv
        self.me = lax.axis_index("seq")

    def to(self, j):
        peer = lax.rem(self.me + j, SEQ)
        return pltpu.make_async_remote_copy(
            src_ref=self.source.at[rows_of(peer, 16)],
            dst_ref=self.target.at[rows_of(self.me, 16)],
            send_sem=self.send.at[j],
            recv_sem=self.recv.at[j],
            device_id={"seq": peer},
            device_id_type=MESH,
        )

    def start(self, j):
        self.to(j).start()

    def wait_recv(self):
        def body(j, _):
            sender = lax.rem(self.me + SEQ - j, SEQ)
            pltpu.make_async_remote_copy(
                src_ref=self.source.at[rows_of(sender, 16)],
                dst_ref=self.target.at[rows_of(sender, 16)],
                send_sem=self.send.at[j],
                recv_sem=self.recv.at[j],
                device_id={"seq": sender},
                device_id_type=MESH,
            ).wait_recv()
            return 0

        lax.fori_loop(1, SEQ, body, 0)

    def wait_send(self):
        def body(j, _):
            self.to(j).wait_send()
            return 0

        lax.fori_loop(1, SEQ, body, 0)


def kernel(
    lat_hbm, cot_hbm, mod_hbm, wqs_hbm, wos_hbm, wqt_hbm, wot_hbm,
    grad_latents, moments, dqkv_s, dout_s, dqkv_t, dout_t,
    lat, mod, wqs, wos, wqt, wot,
    normed_s, scale_s, packed_s, probs_s, attended_s, branch_s, hidden_out, hidden,
    cot, normed_t, scale_t, packed_t, probs_t, attended_t, branch_t, grad_out, grad_hidden, d_attended, d_modulated,
    left_s, right_s, left_t, right_t,
    whole, first, pair, half, second, quarter, third, final, other,
    held, arrived,
    load_sem, send_sem, recv_sem, pair_send, pair_recv, sum_send, sum_recv, clip_send, clip_recv,
):
    place = Place()
    me = place.seq
    here = rows_of(me, 16)
    modulated_s, d_branch_s = left_s.at[0, 0], left_s.at[1, 0]
    modulated_t, d_branch_t = left_t.at[0, 0], left_t.at[1, 0]
    loads = [
        pltpu.make_async_copy(src, dst, load_sem.at[i])
        for i, (src, dst) in enumerate(
            [
                (lat_hbm, lat), (mod_hbm, mod), (wqs_hbm, wqs), (wos_hbm, wos), (wqt_hbm, wqt), (wot_hbm, wot),
                (cot_hbm.at[here], cot.at[here]),
            ]
        )
    ]
    for load in loads:
        load.start()

    barrier = pltpu.get_barrier_semaphore()

    def signal(device):
        pl.semaphore_signal(barrier, inc=1, device_id=device, device_id_type=MESH)

    def greet(j, _):
        signal({"seq": lax.rem(me + j, SEQ)})
        return 0

    lax.fori_loop(1, SEQ, greet, 0)
    for j in range(1, 4):
        for k in range(4):
            signal(place.at(x=lax.rem(place.x + j, 4), z=k))
    for k in range(4):
        signal(place.at(y=lax.rem(place.y + 2, 4), z=k))
        signal(place.at(y=3 - place.y, z=k))

    @pl.when(place.x != place.y)
    def _():
        for k in range(4):
            signal(place.at(x=place.y, y=place.x, z=k))

    loads[0].wait()
    loads[1].wait()
    normalise(lat, mod, 0, normed_s, scale_s, modulated_s)
    trips = [
        Exchange(source, target, send_sem.at[i], recv_sem.at[i])
        for i, (source, target) in enumerate(
            [(cot_hbm, cot), (hidden_out, hidden), (grad_out, grad_hidden)]
        )
    ]
    cot_trip, hidden_trip, grad_trip = trips
    pair_s = PairTerms(place, left_s, right_s, pair_send.at[0], pair_recv.at[0])
    pair_t = PairTerms(place, left_t, right_t, pair_send.at[1], pair_recv.at[1])
    sums_s, sums_t = [
        [
            Reduction(
                place, names[p], whole.at[l, p], first.at[l, p], pair.at[l, p], half.at[l, p], second.at[l, p],
                quarter.at[l, p], third.at[l, p], final.at[l, p], other.at[l, p],
                sum_send.at[l, p], sum_recv.at[l, p],
            )
            for p in range(3)
        ]
        for l, names in enumerate((("xzy", "yxz", "zyx"), ("xyz", "xzy", "yxz")))
    ]
    clip = ClipSum(place, held, arrived, clip_send, clip_recv)

    def send_all(trip):
        for j in range(1, SEQ):
            trip.start(j)

    loads[2].wait()
    project(modulated_s, wqs, packed_s)
    for h in range(HEADS):
        probs = probabilities(packed_s, h, None)
        probs_s[h] = probs
        attend(probs.astype(BF16), packed_s, h, attended_s)
    loads[3].wait()
    project_out(attended_s, wos, branch_s)
    for rows in chunks():
        hidden_out[rows, :] = (lat[rows, :].astype(F32) + mod[2] * branch_s[rows, :]).astype(BF16)
    pl.semaphore_wait(barrier, SEQ + 19 + jnp.where(place.x == place.y, 0, 4))
    send_all(hidden_trip)
    send_all(cot_trip)
    hidden[here, :] = hidden_out[here, :]
    right_s[2, :, HE:] = attended_s[...]
    pair_s.start(0)

    hidden_trip.wait_recv()
    normalise(hidden, mod, 3, normed_t, scale_t, modulated_t)
    pair_t.start(0)
    loads[4].wait()
    project(modulated_t, wqt, packed_t)
    patch_row = lax.rem(lax.broadcasted_iota(jnp.int32, (TOKENS, TOKENS), 0), 16)
    patch_col = lax.rem(lax.broadcasted_iota(jnp.int32, (TOKENS, TOKENS), 1), 16)
    mask = patch_row == patch_col
    for h in range(HEADS):
        probs = probabilities(packed_t, h, mask)
        probs_t[h] = probs
        attend(probs.astype(BF16), packed_t, h, attended_t)
    loads[5].wait()
    project_out(attended_t, wot, branch_t)
    loads[6].wait()
    cot_trip.wait_recv()
    gated(cot, mod, 5, d_branch_t)
    d_attended[...] = dot(d_branch_t[...], wot[...], NT).astype(BF16)
    pair_t.start(1)
    for h in range(HEADS):
        probs = probs_t[h]
        head_backward(probs, probs.astype(BF16), packed_t, d_attended, h, right_t)
    right_t[2, :, HE:] = attended_t[...]
    pair_t.start(2)
    project_back(right_t, wqt, d_modulated)
    d_offset, d_stretch = normalise_back(
        d_modulated, normed_t, scale_t, mod, 3, cot, grad_out
    )
    send_all(grad_trip)
    clip_first = held.at[0]
    clip_first[3:4, :] = d_offset
    clip_first[4:5, :] = d_stretch
    grad_hidden[here, :] = grad_out[here, :]
    pair_t.wait_recv()
    for p in range(3):
        pair_t.multiply(p, whole.at[1, p])
        if p < 2:
            sums_t[p].stage0()
    clip_first[5:6, :] = gate_sum(cot, branch_t)
    sums_t[0].stage1()

    grad_trip.wait_recv()
    sums_t[2].stage0()
    gated(grad_hidden, mod, 2, d_branch_s)
    pair_s.start(1)
    d_attended[...] = dot(d_branch_s[...], wos[...], NT).astype(BF16)
    sums_t[1].stage1()
    for h in range(HEADS):
        probs = probs_s[h]
        head_backward(probs, probs.astype(BF16), packed_s, d_attended, h, right_s)
        if h == 3:
            sums_t[0].stage2()
    pair_s.start(2)
    project_back(right_s, wqs, d_modulated)
    pair_s.wait_recv()
    for p in (2, 1, 0):
        pair_s.multiply(p, whole.at[0, p])
        sums_s[p].stage0()
    sums_t[1].stage2()
    d_offset, d_stretch = normalise_back(
        d_modulated, normed_s, scale_s, mod, 0, grad_hidden, grad_latents
    )
    clip_first[0:1, :] = d_offset
    clip_first[1:2, :] = d_stretch
    clip_first[2:3, :] = gate_sum(grad_hidden, branch_s)
    clip_first[6:8, :] = jnp.zeros((2, D), F32)
    clip.start()
    sums_t[2].stage1()
    sums_t[0].stage3()
    for p in (2, 1, 0):
        sums_s[p].stage1()
    clip.step(0)
    sums_t[1].stage3()
    sums_t[2].stage2()
    for p in (2, 1, 0):
        sums_s[p].stage2()
    clip.step(1)
    owned = [sums_t[0].stage4(), sums_t[1].stage4()]
    sums_t[2].stage3()
    for p in (2, 1, 0):
        sums_s[p].stage3()
    clip.step(2)
    owned.append(sums_t[2].stage4())
    owned_s = [sums.stage4() for sums in sums_s]
    clip.step(3)
    for i in range(6):
        moments[i] = held[4, i : i + 1, :]
    write_rows([sums.stage5(own) for sums, own in zip(sums_t, owned)], dqkv_t, dout_t)
    for part in (*trips, pair_s, pair_t, *sums_t, clip):
        part.wait_send()
    results_s = [sums.stage5(own) for sums, own in zip(sums_s, owned_s)]
    write_rows(results_s, dqkv_s, dout_s)
    for part in sums_s:
        part.wait_send()


def write_rows(results, dqkv, dout):
    for p, (low, high) in enumerate(results):
        dqkv[:, PART * p : PART * p + PART] = low
        start = 2 * HE + PART * p
        if p == 0:
            dqkv[:, start : start + PART] = high
        elif p == 1:
            dqkv[:, start:] = high[:, : PACKED - start]
            dout[:, : PART - (PACKED - start)] = high[:, PACKED - start :]
        else:
            dout[:, start - PACKED :] = high


def copy_out(*refs):
    for source, target in zip(refs[:6], refs[6:]):
        target[...] = source[...]


def local(latents, cotangent, modulation, spatial_qkv, spatial_out, temporal_qkv, temporal_out):
    vm = pl.BlockSpec(memory_space=pltpu.VMEM)
    hbm = pl.BlockSpec(memory_space=pl.ANY)
    sds = jax.ShapeDtypeStruct

    def bf16(*shape):
        return pltpu.VMEM(shape, BF16)

    def f32(*shape):
        return pltpu.VMEM(shape, F32)

    wide, wide32, column, narrow = bf16(TOKENS, D), f32(TOKENS, D), f32(TOKENS, 1), bf16(TOKENS, HE)
    three, wq, wo = bf16(TOKENS, PACKED), bf16(PACKED, D), bf16(HE, D)
    left, right = bf16(2, 2, TOKENS, D), bf16(4, TOKENS, 2 * HE)
    dma = pltpu.SemaphoreType.DMA
    shapes = [
        sds((TOKENS, D), BF16),
        sds((6, 1, D), F32),
        sds((9, PACKED), F32),
        sds((9, HE), F32),
        sds((9, PACKED), F32),
        sds((9, HE), F32),
    ]
    outs = pl.pallas_call(
        kernel,
        out_shape=shapes,
        in_specs=[hbm] * 7,
        out_specs=[vm] * 6,
        scratch_shapes=[
            wide, f32(6, 1, D), wq, wo, wq, wo,
            wide32, column, three, f32(HEADS, TOKENS, TOKENS), narrow, wide32, wide, wide,
            wide, wide32, column, three, f32(HEADS, TOKENS, TOKENS), narrow, wide32, wide, wide, narrow, wide,
            left, right, left, right,
            bf16(2, 3, 2, 4, SLAB, PART), bf16(2, 3, 2, 2, SLAB, PART), bf16(2, 3, 2, SLAB, PART),
            bf16(2, 3, 4, BLOCK, PART), bf16(2, 3, 3, BLOCK, PART), bf16(2, 3, BLOCK, PART),
            bf16(2, 3, 4, 32, PART), f32(2, 3, 16, PART), f32(2, 3, 16, PART),
            f32(5, 8, D), f32(4, 8, D),
            dma((7,)), dma((3, SEQ)), dma((3, SEQ)), dma((2, 3)), dma((2, 3)),
            dma((2, 3, 11)), dma((2, 3, 11)), dma((4,)), dma((4,)),
        ],
        compiler_params=pltpu.CompilerParams(
            collective_id=0, has_side_effects=True, vmem_limit_bytes=62 * 2**20
        ),
    )(
        latents.reshape(TOKENS, D), cotangent.reshape(TOKENS, D), modulation.transpose(1, 0, 2),
        spatial_qkv.T, spatial_out.T, temporal_qkv.T, temporal_out.T,
    )
    grad, moments, *grads = pl.pallas_call(
        copy_out,
        out_shape=shapes,
        in_specs=[vm] * 6,
        out_specs=[vm] * 6,
    )(*outs)
    return (grad.reshape(latents.shape), moments.transpose(1, 0, 2), *grads)


def solution(mesh):
    in_specs = (
        P("dp", "seq", None, None),
        P("dp", "seq", None, None),
        P("dp", None, None),
        P(),
        P(),
        P(),
        P(),
    )
    out_specs = (
        P("dp", "seq", None, None),
        P("dp", None, None),
        P(("dp", "seq"), None),
        P(("dp", "seq"), None),
        P(("dp", "seq"), None),
        P(("dp", "seq"), None),
    )
    return jax.shard_map(local, mesh=mesh, in_specs=in_specs, out_specs=out_specs, check_vma=False)
```

```python
import functools

import jax
import jax.numpy as jnp
from jax import lax
from jax.experimental import pallas as pl
from jax.experimental.pallas import tpu as pltpu
from jax.sharding import PartitionSpec as P

HEADS = 8
HEAD_DIM = 72
HE = HEADS * HEAD_DIM
PACKED = 3 * HE
D = 1152
TOKENS = 256
SEQ = 16
EPSILON = 1e-06
FACTOR = HEAD_DIM**-0.5
SLAB = 144
BLOCK = 80
PART = 384
MESH = pl.DeviceIdType.MESH
F32 = jnp.float32
BF16 = jnp.bfloat16

NN = (((1,), (0,)), ((), ()))
NT = (((1,), (1,)), ((), ()))
TN = (((0,), (0,)), ((), ()))


def dot(a, b, dims=NN):
    return lax.dot_general(a, b, dims, preferred_element_type=F32)


def rows_of(i, size):
    return pl.ds(pl.multiple_of(i * size, size), size)


def chunks(size=32):
    return [slice(i, i + size) for i in range(0, TOKENS, size)]


def normalise(source, mod, row, normed, scale, modulated):
    offset = mod[row]
    stretch = 1.0 + mod[row + 1]
    for rows in chunks():
        x = source[rows, :].astype(F32)
        centred = x - jnp.mean(x, axis=-1, keepdims=True)
        spread = jnp.mean(centred * centred, axis=-1, keepdims=True)
        inverse = lax.rsqrt(spread + EPSILON)
        n = centred * inverse
        normed[rows, :] = n
        scale[rows, :] = inverse
        modulated[rows, :] = (n * stretch + offset).astype(BF16)


def project(modulated, weight, packed):
    packed[...] = dot(modulated[...], weight[...], NT).astype(BF16)


def project_out(attended, weight, out):
    out[...] = dot(attended[...], weight[...])


def project_back(right, weight, out):
    total = dot(right[0], weight[: 2 * HE, :]) + dot(right[2, :, :HE], weight[2 * HE :, :])
    out[...] = total.astype(BF16)


def head(ref, h, section=0):
    lane = section * HE + h * HEAD_DIM
    return ref[:, lane : lane + HEAD_DIM]


def probabilities(packed, h, mask):
    scores = dot(head(packed, h, 1), head(packed, h, 0), NT)
    raised = jnp.exp(scores * FACTOR)
    if mask is not None:
        raised = jnp.where(mask, raised, 0.0)
    return raised * (1.0 / jnp.sum(raised, axis=0, keepdims=True))


def head_backward(probs, weights, packed, d_attended, h, right):
    d_head = head(d_attended, h)
    d_weights = dot(head(packed, h, 2), d_head, NT)
    carried = jnp.sum(d_weights * probs, axis=0, keepdims=True)
    d_scores = (probs * (d_weights - carried) * FACTOR).astype(BF16)
    lane = h * HEAD_DIM
    right[0, :, lane : lane + HEAD_DIM] = dot(d_scores, head(packed, h, 1), TN).astype(BF16)
    right[0, :, HE + lane : HE + lane + HEAD_DIM] = dot(d_scores, head(packed, h, 0)).astype(BF16)
    right[2, :, lane : lane + HEAD_DIM] = dot(weights, d_head).astype(BF16)


def attend(weights, packed, h, attended):
    lane = h * HEAD_DIM
    attended[:, lane : lane + HEAD_DIM] = dot(weights, head(packed, h, 2), TN).astype(BF16)


def fold(x):
    return sum(x[8 * i : 8 * i + 8] for i in range(x.shape[0] // 8))


def gated(source, mod, row, out):
    out[...] = (source[...].astype(F32) * mod[row]).astype(BF16)


def gate_sum(upstream, branch):
    total = jnp.zeros((8, D), F32)
    for rows in chunks():
        total = total + fold(upstream[rows, :].astype(F32) * branch[rows, :])
    return jnp.sum(total, axis=0, keepdims=True)


def normalise_back(d_modulated, normed, scale, mod, row, upstream, out):
    stretch = 1.0 + mod[row + 1]
    totals = [jnp.zeros((8, D), F32)] * 2
    for rows in chunks():
        g = d_modulated[rows, :].astype(F32)
        n = normed[rows, :]
        dn = g * stretch
        first = jnp.mean(dn, axis=-1, keepdims=True)
        second = jnp.mean(dn * n, axis=-1, keepdims=True)
        dx = scale[rows, :] * (dn - first - n * second)
        out[rows, :] = (upstream[rows, :].astype(F32) + dx).astype(BF16)
        totals = [total + fold(term) for total, term in zip(totals, (g, g * n))]
    return [jnp.sum(t, axis=0, keepdims=True) for t in totals]


def swap1(i):
    return i + 1 - 2 * lax.rem(i, 2)


class Place:
    def __init__(self):
        self.dp = lax.axis_index("dp")
        self.seq = lax.axis_index("seq")
        self.x = lax.rem(self.dp, 4)
        self.yh = lax.div(self.dp, 4)
        self.yl = lax.div(self.seq, 8)
        self.y = 2 * self.yh + self.yl
        self.z = lax.rem(lax.div(self.seq, 2), 4)
        self.core = lax.rem(self.seq, 2)

    def at(self, x=None, y=None, z=None, core=None):
        x = self.x if x is None else x
        y = self.y if y is None else y
        z = self.z if z is None else z
        core = self.core if core is None else core
        return {
            "dp": 4 * lax.div(y, 2) + x,
            "seq": 8 * lax.rem(y, 2) + 2 * z + core,
        }

    def pair(self, i):
        near, far = swap1(i), 3 - i
        return near + self.core * (far - near), far + self.core * (near - far)


def remote(src, dst, send, recv, device):
    return pltpu.make_async_remote_copy(
        src_ref=src, dst_ref=dst, send_sem=send, recv_sem=recv, device_id=device, device_id_type=MESH
    )


class PairTerms:
    def __init__(self, place, left, right, send, recv):
        self.core = place.core
        other = place.at(core=1 - place.core)
        away = 2 - 2 * place.core
        self.left, self.right = left, right
        self.copies = [
            remote(left.at[0, 0], left.at[0, 1], send.at[0], recv.at[0], other),
            remote(left.at[1, 0], left.at[1, 1], send.at[1], recv.at[1], other),
            remote(right.at[away], right.at[away + 1], send.at[2], recv.at[2], other),
        ]

    def start(self, i):
        if i == 1:
            pl.when(self.core == 0)(self.copies[1].start)
        else:
            self.copies[i].start()

    def wait_recv(self):
        self.copies[0].wait_recv()
        pl.when(self.core == 1)(self.copies[1].wait_recv)
        self.copies[2].wait_recv()

    def wait_send(self):
        self.copies[0].wait_send()
        pl.when(self.core == 0)(self.copies[1].wait_send)
        self.copies[2].wait_send()

    def multiply(self, part, out):
        first = PART * part
        pieces = [(first, first + PART)]
        if part == 1:
            pieces = [(first, HE), (HE, first + PART)]
        for low, high in pieces:
            left = self.left[0 if high <= HE else self.core].reshape(2 * TOKENS, D)
            right = self.right[pl.ds(2 * self.core, 2), :, low:high].reshape(2 * TOKENS, high - low)
            total = dot(left, right, TN)
            for yh in range(2):
                for x in range(4):
                    row = SLAB * (4 * yh + x)
                    out[yh, x, :, low - first : high - first] = total[row : row + SLAB].astype(BF16)


class Reduction:
    def __init__(self, place, names, whole, first, pair, half, second, quarter, third, final, other, send, recv):
        self.place, self.names = place, names
        self.whole, self.first, self.pair, self.half, self.second = whole, first, pair, half, second
        self.quarter, self.third, self.final, self.other = quarter, third, final, other
        self.at = [getattr(place, name) for name in names]
        a = self.at[0]
        a1, self.a2 = place.pair(a)
        to_a1, to_a2 = place.at(**{names[0]: a1}), place.at(**{names[0]: self.a2})
        self.copies = [
            remote(whole.at[:, lax.rem(a + 2, 4)], first.at[1], send.at[0], recv.at[0], to_a1),
            remote(whole.at[:, a1], first.at[0], send.at[1], recv.at[1], to_a1),
            remote(whole.at[:, self.a2], pair, send.at[2], recv.at[2], to_a2),
        ]
        for j in range(1, 4):
            peer = lax.rem(self.at[1] + j, 4)
            self.copies.append(
                remote(half.at[peer], second.at[j - 1], send.at[2 + j], recv.at[2 + j], place.at(**{names[1]: peer}))
            )
        x, y, z = place.x, place.y, place.z
        owner = {n: getattr(place, m) for n, m in zip("xy", names)}
        came = dict(zip(names[:2], (x, y)))
        self.owns = [jnp.logical_and(jnp.logical_and(owner["x"] == x, owner["y"] == y), z == j) for j in range(4)]
        self.took = [
            jnp.logical_and(
                jnp.logical_and(getattr(place, names[0]) == x, getattr(place, names[1]) == y), self.at[2] == k
            )
            for k in range(4)
        ]
        self.out = [
            remote(
                quarter.at[j], third.at[self.at[2]], send.at[6 + j], recv.at[6 + self.at[2]],
                place.at(**owner, z=j),
            )
            for j in range(4)
        ]
        self.back = [
            remote(
                quarter.at[0], third.at[k], send.at[6 + k], recv.at[6 + k],
                place.at(**came, **{names[2]: k}),
            )
            for k in range(4)
        ]
        self.swap = remote(final, other, send.at[10], recv.at[10], place.at(core=1 - place.core))

    def start_out(self):
        for j in range(4):
            pl.when(jnp.logical_not(self.owns[j]))(self.out[j].start)

            @pl.when(self.owns[j])
            def _():
                self.third[self.at[2]] = self.quarter[j]

    def wait_back(self):
        for k in range(4):
            pl.when(jnp.logical_not(self.took[k]))(self.back[k].wait_recv)

    def stage0(self):
        self.copies[0].start()
        self.copies[1].start()

    def stage1(self):
        self.copies[0].wait_recv()
        for yh in range(2):
            kept = self.whole.at[yh, self.a2]
            kept[...] = (kept[...].astype(F32) + self.first[1, yh].astype(F32)).astype(BF16)
        self.copies[2].start()

    def stage2(self):
        self.copies[1].wait_recv()
        self.copies[2].wait_recv()
        for yh in range(2):
            total = self.whole[yh, self.at[0]].astype(F32) + self.first[0, yh].astype(F32)
            total = total + self.pair[yh].astype(F32)
            self.half[2 * yh, :72] = total[:72].astype(BF16)
            self.half[2 * yh + 1, :72] = total[72:].astype(BF16)
        for copy in self.copies[3:]:
            copy.start()

    def stage3(self):
        for copy in self.copies[3:]:
            copy.wait_recv()
        total = self.half[self.at[1]].astype(F32)
        for k in range(3):
            total = total + self.second[k].astype(F32)
        for j in range(4):
            main, rest = total[18 * j : 18 * j + 16], total[18 * j + 16 : 18 * j + 18]
            strips = [rest[:, 128 * i : 128 * i + 128] for i in range(3)]
            strips.append(jnp.zeros((10, 128), F32))
            self.quarter[j] = jnp.concatenate([main, jnp.concatenate(strips, axis=0)], axis=1).astype(BF16)
        self.start_out()

    def stage4(self):
        self.wait_back()
        total = self.third[0].astype(F32)
        for k in range(1, 4):
            total = total + self.third[k].astype(F32)
        total = total * (1.0 / 8)
        strips = [total[2 * i : 2 * i + 2, PART:] for i in range(3)]
        rows = [total[:, :PART], jnp.concatenate(strips, axis=1), jnp.zeros((6, PART), F32)]
        rows, core = jnp.concatenate(rows, axis=0), self.place.core
        self.final[...] = pltpu.roll(rows, lax.rem(24 - 9 * (1 - core), 24), 0)[:16]
        self.swap.start()
        return pltpu.roll(rows, lax.rem(24 - 9 * core, 24), 0)[:16]

    def stage5(self, own):
        self.swap.wait_recv()
        low = self.place.core == 0
        theirs = self.other[...]
        return jnp.where(low, own, theirs)[:9], jnp.where(low, theirs, own)[:9]

    def wait_send(self):
        for copy in self.copies:
            copy.wait_send()
        for j in range(4):
            pl.when(jnp.logical_not(self.owns[j]))(self.out[j].wait_send)
        self.swap.wait_send()


class ClipSum:
    def __init__(self, place, held, arrived, send, recv):
        self.held, self.arrived = held, arrived
        devices = [
            place.at(core=1 - place.core),
            place.at(z=swap1(place.z)),
            place.at(z=3 - place.z),
            place.at(y=swap1(place.y)),
        ]
        self.copies = [
            remote(held.at[i], arrived.at[i], send.at[i], recv.at[i], device)
            for i, device in enumerate(devices)
        ]

    def start(self):
        self.copies[0].start()

    def step(self, i):
        self.copies[i].wait_recv()
        self.held[i + 1] = self.held[i] + self.arrived[i]
        if i < 3:
            self.copies[i + 1].start()

    def wait_send(self):
        for copy in self.copies:
            copy.wait_send()


class Exchange:
    def __init__(self, source, target, send, recv):
        self.source, self.target, self.send, self.recv = source, target, send, recv
        self.me = lax.axis_index("seq")

    def to(self, j):
        peer = lax.rem(self.me + j, SEQ)
        return pltpu.make_async_remote_copy(
            src_ref=self.source.at[rows_of(peer, 16)],
            dst_ref=self.target.at[rows_of(self.me, 16)],
            send_sem=self.send.at[j],
            recv_sem=self.recv.at[j],
            device_id={"seq": peer},
            device_id_type=MESH,
        )

    def start(self, j):
        self.to(j).start()

    def wait_recv(self):
        def body(j, _):
            sender = lax.rem(self.me + SEQ - j, SEQ)
            pltpu.make_async_remote_copy(
                src_ref=self.source.at[rows_of(sender, 16)],
                dst_ref=self.target.at[rows_of(sender, 16)],
                send_sem=self.send.at[j],
                recv_sem=self.recv.at[j],
                device_id={"seq": sender},
                device_id_type=MESH,
            ).wait_recv()
            return 0

        lax.fori_loop(1, SEQ, body, 0)

    def wait_send(self):
        def body(j, _):
            self.to(j).wait_send()
            return 0

        lax.fori_loop(1, SEQ, body, 0)


def kernel(
    lat_hbm, cot_hbm, mod_hbm, wqs_hbm, wos_hbm, wqt_hbm, wot_hbm,
    grad_latents, moments, dqkv_s, dout_s, dqkv_t, dout_t,
    lat, mod, wqs, wos, wqt, wot,
    normed_s, scale_s, packed_s, probs_s, attended_s, branch_s, hidden_out, hidden,
    cot, normed_t, scale_t, packed_t, probs_t, attended_t, branch_t, grad_out, grad_hidden, d_attended_out, d_attended, d_modulated,
    left_s, right_s, left_t, right_t,
    whole, first, pair, half, second, quarter, third, final, other,
    held, arrived,
    load_sem, send_sem, recv_sem, pair_send, pair_recv, sum_send, sum_recv, clip_send, clip_recv,
):
    place = Place()
    me = place.seq
    here = rows_of(me, 16)
    modulated_s, d_branch_s = left_s.at[0, 0], left_s.at[1, 0]
    modulated_t, d_branch_t = left_t.at[0, 0], left_t.at[1, 0]
    loads = [
        pltpu.make_async_copy(src, dst, load_sem.at[i])
        for i, (src, dst) in enumerate(
            [
                (lat_hbm, lat), (mod_hbm, mod), (wqs_hbm, wqs), (wos_hbm, wos), (cot_hbm, grad_out), (wot_hbm, wot),
                (wqt_hbm, wqt), (cot_hbm.at[here], cot.at[here]),
            ]
        )
    ]
    for load in loads:
        load.start()

    barrier = pltpu.get_barrier_semaphore()

    def signal(device):
        pl.semaphore_signal(barrier, inc=1, device_id=device, device_id_type=MESH)

    def greet(j, _):
        signal({"seq": lax.rem(me + j, SEQ)})
        return 0

    lax.fori_loop(1, SEQ, greet, 0)
    for j in range(1, 4):
        for k in range(4):
            signal(place.at(x=lax.rem(place.x + j, 4), z=k))
    signal(place.at(y=lax.rem(place.y + 2, 4)))
    signal(place.at(y=3 - place.y))

    @pl.when(place.x != place.y)
    def _():
        for k in range(4):
            signal(place.at(x=place.y, y=place.x, z=k))

    loads[0].wait()
    loads[1].wait()
    normalise(lat, mod, 0, normed_s, scale_s, modulated_s)
    trips = [
        Exchange(source, target, send_sem.at[i], recv_sem.at[i])
        for i, (source, target) in enumerate(
            [(cot_hbm, cot), (hidden_out, hidden), (grad_out, grad_hidden), (d_attended_out, d_attended)]
        )
    ]
    cot_trip, hidden_trip, grad_trip, attended_trip = trips
    pair_s = PairTerms(place, left_s, right_s, pair_send.at[0], pair_recv.at[0])
    pair_t = PairTerms(place, left_t, right_t, pair_send.at[1], pair_recv.at[1])
    sums_s, sums_t = [
        [
            Reduction(
                place, names[p], whole.at[l, p], first.at[l, p], pair.at[l, p], half.at[l, p], second.at[l, p],
                quarter.at[l, p], third.at[l, p], final.at[l, p], other.at[l, p],
                sum_send.at[l, p], sum_recv.at[l, p],
            )
            for p in range(3)
        ]
        for l, names in enumerate((("xyz", "yxz", "zyx"), ("xyz", "xyz", "yxz")))
    ]
    clip = ClipSum(place, held, arrived, clip_send, clip_recv)

    def send_all(trip):
        for j in range(1, SEQ):
            trip.start(j)

    loads[2].wait()
    project(modulated_s, wqs, packed_s)
    for h in range(HEADS):
        probs = probabilities(packed_s, h, None)
        probs_s[h] = probs
        attend(probs.astype(BF16), packed_s, h, attended_s)
    loads[3].wait()
    project_out(attended_s, wos, branch_s)
    for rows in chunks():
        hidden_out[rows, :] = (lat[rows, :].astype(F32) + mod[2] * branch_s[rows, :]).astype(BF16)
    loads[4].wait()
    loads[5].wait()
    gated(grad_out, mod, 5, d_modulated)
    d_attended_out[...] = dot(d_modulated[...], wot[...], NT).astype(BF16)
    pl.semaphore_wait(barrier, SEQ + 13 + jnp.where(place.x == place.y, 0, 4))
    send_all(hidden_trip)
    send_all(attended_trip)
    send_all(cot_trip)
    d_attended[here, :] = d_attended_out[here, :]
    hidden[here, :] = hidden_out[here, :]
    right_s[2, :, HE:] = attended_s[...]
    pair_s.start(0)

    hidden_trip.wait_recv()
    normalise(hidden, mod, 3, normed_t, scale_t, modulated_t)
    pair_t.start(0)
    loads[6].wait()
    project(modulated_t, wqt, packed_t)
    patch_row = lax.rem(lax.broadcasted_iota(jnp.int32, (TOKENS, TOKENS), 0), 16)
    patch_col = lax.rem(lax.broadcasted_iota(jnp.int32, (TOKENS, TOKENS), 1), 16)
    mask = patch_row == patch_col
    for h in range(HEADS):
        probs = probabilities(packed_t, h, mask)
        probs_t[h] = probs
        attend(probs.astype(BF16), packed_t, h, attended_t)
    project_out(attended_t, wot, branch_t)
    attended_trip.wait_recv()
    for h in range(HEADS):
        probs = probs_t[h]
        head_backward(probs, probs.astype(BF16), packed_t, d_attended, h, right_t)
    right_t[2, :, HE:] = attended_t[...]
    pair_t.start(2)
    project_back(right_t, wqt, d_modulated)
    loads[7].wait()
    cot_trip.wait_recv()
    d_offset, d_stretch = normalise_back(
        d_modulated, normed_t, scale_t, mod, 3, cot, grad_out
    )
    send_all(grad_trip)
    gated(cot, mod, 5, d_branch_t)
    pair_t.start(1)
    clip_first = held.at[0]
    clip_first[3:4, :] = d_offset
    clip_first[4:5, :] = d_stretch
    clip_first[5:6, :] = gate_sum(cot, branch_t)
    grad_hidden[here, :] = grad_out[here, :]
    pair_t.wait_recv()
    for p in range(3):
        pair_t.multiply(p, whole.at[1, p])
        if p < 2:
            sums_t[p].stage0()
    sums_t[0].stage1()

    grad_trip.wait_recv()
    sums_t[2].stage0()
    gated(grad_hidden, mod, 2, d_branch_s)
    pair_s.start(1)
    d_attended[...] = dot(d_branch_s[...], wos[...], NT).astype(BF16)
    for h in range(HEADS):
        probs = probs_s[h]
        head_backward(probs, probs.astype(BF16), packed_s, d_attended, h, right_s)
    pair_s.start(2)
    project_back(right_s, wqs, d_modulated)
    sums_t[1].stage1()
    pair_s.wait_recv()
    for p in (2, 1, 0):
        pair_s.multiply(p, whole.at[0, p])
        sums_s[p].stage0()
    sums_t[0].stage2()
    sums_t[2].stage1()
    d_offset, d_stretch = normalise_back(
        d_modulated, normed_s, scale_s, mod, 0, grad_hidden, grad_latents
    )
    clip_first[0:1, :] = d_offset
    clip_first[1:2, :] = d_stretch
    clip_first[2:3, :] = gate_sum(grad_hidden, branch_s)
    clip_first[6:8, :] = jnp.zeros((2, D), F32)
    clip.start()
    sums_t[1].stage2()
    for p in (2, 1, 0):
        sums_s[p].stage1()
    sums_t[2].stage2()
    sums_t[0].stage3()
    sums_t[1].stage3()
    clip.step(0)
    for p in (2, 1, 0):
        sums_s[p].stage2()
    sums_t[2].stage3()
    owned = [sums_t[0].stage4(), sums_t[1].stage4()]
    clip.step(1)
    for p in (2, 1, 0):
        sums_s[p].stage3()
    owned.append(sums_t[2].stage4())
    clip.step(2)
    owned_s = [sums.stage4() for sums in sums_s]
    clip.step(3)
    for i in range(6):
        moments[i] = held[4, i : i + 1, :]
    write_rows([sums.stage5(own) for sums, own in zip(sums_t, owned)], dqkv_t, dout_t)
    for part in (*trips, pair_s, pair_t, *sums_t, clip):
        part.wait_send()
    results_s = [sums.stage5(own) for sums, own in zip(sums_s, owned_s)]
    write_rows(results_s, dqkv_s, dout_s)
    for part in sums_s:
        part.wait_send()


def write_rows(results, dqkv, dout):
    for p, (low, high) in enumerate(results):
        dqkv[:, PART * p : PART * p + PART] = low
        start = 2 * HE + PART * p
        if p == 0:
            dqkv[:, start : start + PART] = high
        elif p == 1:
            dqkv[:, start:] = high[:, : PACKED - start]
            dout[:, : PART - (PACKED - start)] = high[:, PACKED - start :]
        else:
            dout[:, start - PACKED :] = high


def copy_out(*refs):
    for source, target in zip(refs[:6], refs[6:]):
        target[...] = source[...]


def local(latents, cotangent, modulation, spatial_qkv, spatial_out, temporal_qkv, temporal_out):
    vm = pl.BlockSpec(memory_space=pltpu.VMEM)
    hbm = pl.BlockSpec(memory_space=pl.ANY)
    sds = jax.ShapeDtypeStruct

    def bf16(*shape):
        return pltpu.VMEM(shape, BF16)

    def f32(*shape):
        return pltpu.VMEM(shape, F32)

    wide, wide32, column, narrow = bf16(TOKENS, D), f32(TOKENS, D), f32(TOKENS, 1), bf16(TOKENS, HE)
    three, wq, wo = bf16(TOKENS, PACKED), bf16(PACKED, D), bf16(HE, D)
    left, right = bf16(2, 2, TOKENS, D), bf16(4, TOKENS, 2 * HE)
    dma = pltpu.SemaphoreType.DMA
    shapes = [
        sds((TOKENS, D), BF16),
        sds((6, 1, D), F32),
        sds((9, PACKED), F32),
        sds((9, HE), F32),
        sds((9, PACKED), F32),
        sds((9, HE), F32),
    ]
    outs = pl.pallas_call(
        kernel,
        out_shape=shapes,
        in_specs=[hbm] * 7,
        out_specs=[vm] * 6,
        scratch_shapes=[
            wide, f32(6, 1, D), wq, wo, wq, wo,
            wide32, column, three, f32(HEADS, TOKENS, TOKENS), narrow, wide32, wide, wide,
            wide, wide32, column, three, f32(HEADS, TOKENS, TOKENS), narrow, wide32, wide, wide, narrow, narrow, wide,
            left, right, left, right,
            bf16(2, 3, 2, 4, SLAB, PART), bf16(2, 3, 2, 2, SLAB, PART), bf16(2, 3, 2, SLAB, PART),
            bf16(2, 3, 4, BLOCK, PART), bf16(2, 3, 3, BLOCK, PART), bf16(2, 3, 4, 16, PART + 128),
            bf16(2, 3, 4, 16, PART + 128), f32(2, 3, 16, PART), f32(2, 3, 16, PART),
            f32(5, 8, D), f32(4, 8, D),
            dma((8,)), dma((4, SEQ)), dma((4, SEQ)), dma((2, 3)), dma((2, 3)),
            dma((2, 3, 11)), dma((2, 3, 11)), dma((4,)), dma((4,)),
        ],
        compiler_params=pltpu.CompilerParams(
            collective_id=0, has_side_effects=True, vmem_limit_bytes=62 * 2**20
        ),
    )(
        latents.reshape(TOKENS, D), cotangent.reshape(TOKENS, D), modulation.transpose(1, 0, 2),
        spatial_qkv.T, spatial_out.T, temporal_qkv.T, temporal_out.T,
    )
    grad, moments, *grads = pl.pallas_call(
        copy_out,
        out_shape=shapes,
        in_specs=[vm] * 6,
        out_specs=[vm] * 6,
    )(*outs)
    return (grad.reshape(latents.shape), moments.transpose(1, 0, 2), *grads)


def solution(mesh):
    in_specs = (
        P("dp", "seq", None, None),
        P("dp", "seq", None, None),
        P("dp", None, None),
        P(),
        P(),
        P(),
        P(),
    )
    out_specs = (
        P("dp", "seq", None, None),
        P("dp", None, None),
        P(("dp", "seq"), None),
        P(("dp", "seq"), None),
        P(("dp", "seq"), None),
        P(("dp", "seq"), None),
    )
    return jax.shard_map(local, mesh=mesh, in_specs=in_specs, out_specs=out_specs, check_vma=False)
```

```python
import functools

import jax
import jax.numpy as jnp
from jax import lax
from jax.experimental import pallas as pl
from jax.experimental.pallas import tpu as pltpu
from jax.sharding import PartitionSpec as P

HEADS = 8
HEAD_DIM = 72
HE = HEADS * HEAD_DIM
PACKED = 3 * HE
D = 1152
TOKENS = 256
SEQ = 16
EPSILON = 1e-06
FACTOR = HEAD_DIM**-0.5
SLAB = 144
BLOCK = 80
PART = 384
MESH = pl.DeviceIdType.MESH
F32 = jnp.float32
BF16 = jnp.bfloat16

NN = (((1,), (0,)), ((), ()))
NT = (((1,), (1,)), ((), ()))
TN = (((0,), (0,)), ((), ()))


def dot(a, b, dims=NN):
    return lax.dot_general(a, b, dims, preferred_element_type=F32)


def rows_of(i, size):
    return pl.ds(pl.multiple_of(i * size, size), size)


def chunks(size=32):
    return [slice(i, i + size) for i in range(0, TOKENS, size)]


def normalise(source, mod, row, normed, scale, modulated):
    offset = mod[row]
    stretch = 1.0 + mod[row + 1]
    for rows in chunks():
        x = source[rows, :].astype(F32)
        centred = x - jnp.mean(x, axis=-1, keepdims=True)
        spread = jnp.mean(centred * centred, axis=-1, keepdims=True)
        inverse = lax.rsqrt(spread + EPSILON)
        n = centred * inverse
        normed[rows, :] = n
        scale[rows, :] = inverse
        modulated[rows, :] = (n * stretch + offset).astype(BF16)


def project(modulated, weight, packed):
    packed[...] = dot(modulated[...], weight[...], NT).astype(BF16)


def project_out(attended, weight, out):
    out[...] = dot(attended[...], weight[...])


def project_back(right, weight, out):
    total = dot(right[0], weight[: 2 * HE, :]) + dot(right[2, :, :HE], weight[2 * HE :, :])
    out[...] = total.astype(BF16)


def head(ref, h, section=0):
    lane = section * HE + h * HEAD_DIM
    return ref[:, lane : lane + HEAD_DIM]


def probabilities(packed, h, mask):
    scores = dot(head(packed, h, 1), head(packed, h, 0), NT)
    raised = jnp.exp(scores * FACTOR)
    if mask is not None:
        raised = jnp.where(mask, raised, 0.0)
    return raised * (1.0 / jnp.sum(raised, axis=0, keepdims=True))


def head_backward(probs, weights, packed, d_attended, h, right):
    d_head = head(d_attended, h)
    d_weights = dot(head(packed, h, 2), d_head, NT)
    carried = jnp.sum(d_weights * probs, axis=0, keepdims=True)
    d_scores = (probs * (d_weights - carried) * FACTOR).astype(BF16)
    lane = h * HEAD_DIM
    right[0, :, lane : lane + HEAD_DIM] = dot(d_scores, head(packed, h, 1), TN).astype(BF16)
    right[0, :, HE + lane : HE + lane + HEAD_DIM] = dot(d_scores, head(packed, h, 0)).astype(BF16)
    right[2, :, lane : lane + HEAD_DIM] = dot(weights, d_head).astype(BF16)


def attend(weights, packed, h, attended):
    lane = h * HEAD_DIM
    attended[:, lane : lane + HEAD_DIM] = dot(weights, head(packed, h, 2), TN).astype(BF16)


def fold(x):
    return sum(x[8 * i : 8 * i + 8] for i in range(x.shape[0] // 8))


def gated(source, mod, row, out):
    out[...] = (source[...].astype(F32) * mod[row]).astype(BF16)


def gate_sum(upstream, branch):
    total = jnp.zeros((8, D), F32)
    for rows in chunks():
        total = total + fold(upstream[rows, :].astype(F32) * branch[rows, :])
    return jnp.sum(total, axis=0, keepdims=True)


def normalise_back(d_modulated, normed, scale, mod, row, upstream, out):
    stretch = 1.0 + mod[row + 1]
    totals = [jnp.zeros((8, D), F32)] * 2
    for rows in chunks():
        g = d_modulated[rows, :].astype(F32)
        n = normed[rows, :]
        dn = g * stretch
        first = jnp.mean(dn, axis=-1, keepdims=True)
        second = jnp.mean(dn * n, axis=-1, keepdims=True)
        dx = scale[rows, :] * (dn - first - n * second)
        out[rows, :] = (upstream[rows, :].astype(F32) + dx).astype(BF16)
        totals = [total + fold(term) for total, term in zip(totals, (g, g * n))]
    return [jnp.sum(t, axis=0, keepdims=True) for t in totals]


def swap1(i):
    return i + 1 - 2 * lax.rem(i, 2)


class Place:
    def __init__(self):
        self.dp = lax.axis_index("dp")
        self.seq = lax.axis_index("seq")
        self.x = lax.rem(self.dp, 4)
        self.yh = lax.div(self.dp, 4)
        self.yl = lax.div(self.seq, 8)
        self.y = 2 * self.yh + self.yl
        self.z = lax.rem(lax.div(self.seq, 2), 4)
        self.core = lax.rem(self.seq, 2)

    def at(self, x=None, y=None, z=None, core=None):
        x = self.x if x is None else x
        y = self.y if y is None else y
        z = self.z if z is None else z
        core = self.core if core is None else core
        return {
            "dp": 4 * lax.div(y, 2) + x,
            "seq": 8 * lax.rem(y, 2) + 2 * z + core,
        }

    def pair(self, i):
        near, far = swap1(i), 3 - i
        return near + self.core * (far - near), far + self.core * (near - far)


def remote(src, dst, send, recv, device):
    return pltpu.make_async_remote_copy(
        src_ref=src, dst_ref=dst, send_sem=send, recv_sem=recv, device_id=device, device_id_type=MESH
    )


class PairTerms:
    def __init__(self, place, left, right, send, recv):
        self.core = place.core
        other = place.at(core=1 - place.core)
        away = 2 - 2 * place.core
        self.left, self.right = left, right
        self.copies = [
            remote(left.at[0, 0], left.at[0, 1], send.at[0], recv.at[0], other),
            remote(left.at[1, 0], left.at[1, 1], send.at[1], recv.at[1], other),
            remote(right.at[away], right.at[away + 1], send.at[2], recv.at[2], other),
        ]

    def start(self, i):
        if i == 1:
            pl.when(self.core == 0)(self.copies[1].start)
        else:
            self.copies[i].start()

    def wait_recv(self):
        self.copies[0].wait_recv()
        pl.when(self.core == 1)(self.copies[1].wait_recv)
        self.copies[2].wait_recv()

    def wait_send(self):
        self.copies[0].wait_send()
        pl.when(self.core == 0)(self.copies[1].wait_send)
        self.copies[2].wait_send()

    def multiply(self, part, out):
        first = PART * part
        pieces = [(first, first + PART)]
        if part == 1:
            pieces = [(first, HE), (HE, first + PART)]
        for low, high in pieces:
            left = self.left[0 if high <= HE else self.core].reshape(2 * TOKENS, D)
            right = self.right[pl.ds(2 * self.core, 2), :, low:high].reshape(2 * TOKENS, high - low)
            total = dot(left, right, TN)
            for yh in range(2):
                for x in range(4):
                    row = SLAB * (4 * yh + x)
                    out[yh, x, :, low - first : high - first] = total[row : row + SLAB].astype(BF16)


class Reduction:
    def __init__(self, place, names, whole, first, pair, half, second, quarter, third, final, other, send, recv):
        self.place, self.names = place, names
        self.whole, self.first, self.pair, self.half, self.second = whole, first, pair, half, second
        self.quarter, self.third, self.final, self.other = quarter, third, final, other
        self.at = [getattr(place, name) for name in names]
        a = self.at[0]
        a1, self.a2 = place.pair(a)
        to_a1, to_a2 = place.at(**{names[0]: a1}), place.at(**{names[0]: self.a2})
        self.copies = [
            remote(whole.at[:, lax.rem(a + 2, 4)], first.at[1], send.at[0], recv.at[0], to_a1),
            remote(whole.at[:, a1], first.at[0], send.at[1], recv.at[1], to_a1),
            remote(whole.at[:, self.a2], pair, send.at[2], recv.at[2], to_a2),
        ]
        for j in range(1, 4):
            peer = lax.rem(self.at[1] + j, 4)
            self.copies.append(
                remote(half.at[peer], second.at[j - 1], send.at[2 + j], recv.at[2 + j], place.at(**{names[1]: peer}))
            )
        x, y, z = place.x, place.y, place.z
        owner = {n: getattr(place, m) for n, m in zip("xy", names)}
        came = dict(zip(names[:2], (x, y)))
        self.owns = [jnp.logical_and(jnp.logical_and(owner["x"] == x, owner["y"] == y), z == j) for j in range(4)]
        self.took = [
            jnp.logical_and(
                jnp.logical_and(getattr(place, names[0]) == x, getattr(place, names[1]) == y), self.at[2] == k
            )
            for k in range(4)
        ]
        self.out = [
            remote(
                quarter.at[j], third.at[self.at[2]], send.at[6 + j], recv.at[6 + self.at[2]],
                place.at(**owner, z=j),
            )
            for j in range(4)
        ]
        self.back = [
            remote(
                quarter.at[0], third.at[k], send.at[6 + k], recv.at[6 + k],
                place.at(**came, **{names[2]: k}),
            )
            for k in range(4)
        ]
        self.swap = remote(final, other, send.at[10], recv.at[10], place.at(core=1 - place.core))

    def start_out(self):
        for j in range(4):
            pl.when(jnp.logical_not(self.owns[j]))(self.out[j].start)

            @pl.when(self.owns[j])
            def _():
                self.third[self.at[2]] = self.quarter[j]

    def wait_back(self):
        for k in range(4):
            pl.when(jnp.logical_not(self.took[k]))(self.back[k].wait_recv)

    def stage0(self):
        self.copies[0].start()
        self.copies[1].start()

    def stage1(self):
        self.copies[0].wait_recv()
        for yh in range(2):
            kept = self.whole.at[yh, self.a2]
            kept[...] = (kept[...].astype(F32) + self.first[1, yh].astype(F32)).astype(BF16)
        self.copies[2].start()

    def stage2(self):
        self.copies[1].wait_recv()
        self.copies[2].wait_recv()
        for yh in range(2):
            total = self.whole[yh, self.at[0]].astype(F32) + self.first[0, yh].astype(F32)
            total = total + self.pair[yh].astype(F32)
            self.half[2 * yh, :72] = total[:72].astype(BF16)
            self.half[2 * yh + 1, :72] = total[72:].astype(BF16)
        for copy in self.copies[3:]:
            copy.start()

    def stage3(self):
        for copy in self.copies[3:]:
            copy.wait_recv()
        total = self.half[self.at[1]].astype(F32)
        for k in range(3):
            total = total + self.second[k].astype(F32)
        for j in range(4):
            main, rest = total[18 * j : 18 * j + 16], total[18 * j + 16 : 18 * j + 18]
            strips = [rest[:, 128 * i : 128 * i + 128] for i in range(3)]
            strips.append(jnp.zeros((10, 128), F32))
            self.quarter[j] = jnp.concatenate([main, jnp.concatenate(strips, axis=0)], axis=1).astype(BF16)
        self.start_out()

    def stage4(self):
        self.wait_back()
        total = self.third[0].astype(F32)
        for k in range(1, 4):
            total = total + self.third[k].astype(F32)
        total = total * (1.0 / 8)
        strips = [total[2 * i : 2 * i + 2, PART:] for i in range(3)]
        rows = [total[:, :PART], jnp.concatenate(strips, axis=1), jnp.zeros((6, PART), F32)]
        rows, core = jnp.concatenate(rows, axis=0), self.place.core
        self.final[...] = pltpu.roll(rows, lax.rem(24 - 9 * (1 - core), 24), 0)[:16]
        self.swap.start()
        return pltpu.roll(rows, lax.rem(24 - 9 * core, 24), 0)[:16]

    def stage5(self, own):
        self.swap.wait_recv()
        low = self.place.core == 0
        theirs = self.other[...]
        return jnp.where(low, own, theirs)[:9], jnp.where(low, theirs, own)[:9]

    def wait_send(self):
        for copy in self.copies:
            copy.wait_send()
        for j in range(4):
            pl.when(jnp.logical_not(self.owns[j]))(self.out[j].wait_send)
        self.swap.wait_send()


class ClipSum:
    def __init__(self, place, held, arrived, send, recv):
        self.held, self.arrived = held, arrived
        devices = [
            place.at(core=1 - place.core),
            place.at(z=swap1(place.z)),
            place.at(z=3 - place.z),
            place.at(y=swap1(place.y)),
        ]
        self.copies = [
            remote(held.at[i], arrived.at[i], send.at[i], recv.at[i], device)
            for i, device in enumerate(devices)
        ]

    def start(self):
        self.copies[0].start()

    def step(self, i):
        self.copies[i].wait_recv()
        self.held[i + 1] = self.held[i] + self.arrived[i]
        if i < 3:
            self.copies[i + 1].start()

    def wait_send(self):
        for copy in self.copies:
            copy.wait_send()


class Exchange:
    def __init__(self, source, target, send, recv):
        self.source, self.target, self.send, self.recv = source, target, send, recv
        self.me = lax.axis_index("seq")

    def to(self, j):
        peer = lax.rem(self.me + j, SEQ)
        return pltpu.make_async_remote_copy(
            src_ref=self.source.at[rows_of(peer, 16)],
            dst_ref=self.target.at[rows_of(self.me, 16)],
            send_sem=self.send.at[j],
            recv_sem=self.recv.at[j],
            device_id={"seq": peer},
            device_id_type=MESH,
        )

    def start(self, j):
        self.to(j).start()

    def wait_recv(self):
        def body(j, _):
            sender = lax.rem(self.me + SEQ - j, SEQ)
            pltpu.make_async_remote_copy(
                src_ref=self.source.at[rows_of(sender, 16)],
                dst_ref=self.target.at[rows_of(sender, 16)],
                send_sem=self.send.at[j],
                recv_sem=self.recv.at[j],
                device_id={"seq": sender},
                device_id_type=MESH,
            ).wait_recv()
            return 0

        lax.fori_loop(1, SEQ, body, 0)

    def wait_send(self):
        def body(j, _):
            self.to(j).wait_send()
            return 0

        lax.fori_loop(1, SEQ, body, 0)


def kernel(
    lat_hbm, cot_hbm, mod_hbm, wqs_hbm, wos_hbm, wqt_hbm, wot_hbm,
    grad_latents, moments, dqkv_s, dout_s, dqkv_t, dout_t,
    lat, mod, wqs, wos, wqt, wot,
    normed_s, scale_s, packed_s, probs_s, attended_s, branch_s, hidden_out, hidden,
    cot, normed_t, scale_t, packed_t, probs_t, attended_t, branch_t, grad_out, grad_hidden, d_attended_out, d_attended, d_modulated,
    left_s, right_s, left_t, right_t,
    whole, first, pair, half, second, quarter, third, final, other,
    held, arrived,
    load_sem, send_sem, recv_sem, pair_send, pair_recv, sum_send, sum_recv, clip_send, clip_recv,
):
    place = Place()
    me = place.seq
    here = rows_of(me, 16)
    modulated_s, d_branch_s = left_s.at[0, 0], left_s.at[1, 0]
    modulated_t, d_branch_t = left_t.at[0, 0], left_t.at[1, 0]
    loads = [
        pltpu.make_async_copy(src, dst, load_sem.at[i])
        for i, (src, dst) in enumerate(
            [
                (lat_hbm, lat), (mod_hbm, mod), (wqs_hbm, wqs), (wos_hbm, wos), (cot_hbm, grad_out), (wot_hbm, wot),
                (wqt_hbm, wqt), (cot_hbm.at[here], cot.at[here]),
            ]
        )
    ]
    for load in loads:
        load.start()

    barrier = pltpu.get_barrier_semaphore()

    def signal(device):
        pl.semaphore_signal(barrier, inc=1, device_id=device, device_id_type=MESH)

    def greet(j, _):
        signal({"seq": lax.rem(me + j, SEQ)})
        return 0

    lax.fori_loop(1, SEQ, greet, 0)
    for j in range(1, 4):
        for k in range(4):
            signal(place.at(x=lax.rem(place.x + j, 4), z=k))
    signal(place.at(y=lax.rem(place.y + 2, 4)))
    signal(place.at(y=3 - place.y))

    @pl.when(place.x != place.y)
    def _():
        for k in range(4):
            signal(place.at(x=place.y, y=place.x, z=k))

    loads[0].wait()
    loads[1].wait()
    normalise(lat, mod, 0, normed_s, scale_s, modulated_s)
    trips = [
        Exchange(source, target, send_sem.at[i], recv_sem.at[i])
        for i, (source, target) in enumerate(
            [(cot_hbm, cot), (hidden_out, hidden), (grad_out, grad_hidden), (d_attended_out, d_attended)]
        )
    ]
    cot_trip, hidden_trip, grad_trip, attended_trip = trips
    pair_s = PairTerms(place, left_s, right_s, pair_send.at[0], pair_recv.at[0])
    pair_t = PairTerms(place, left_t, right_t, pair_send.at[1], pair_recv.at[1])
    sums_s, sums_t = [
        [
            Reduction(
                place, names[p], whole.at[l, p], first.at[l, p], pair.at[l, p], half.at[l, p], second.at[l, p],
                quarter.at[l, p], third.at[l, p], final.at[l, p], other.at[l, p],
                sum_send.at[l, p], sum_recv.at[l, p],
            )
            for p in range(3)
        ]
        for l, names in enumerate((("xyz", "yxz", "zyx"), ("xyz", "yxz", "zyx")))
    ]
    clip = ClipSum(place, held, arrived, clip_send, clip_recv)

    def send_all(trip):
        for j in range(1, SEQ):
            trip.start(j)

    loads[2].wait()
    project(modulated_s, wqs, packed_s)
    for h in range(HEADS):
        probs = probabilities(packed_s, h, None)
        probs_s[h] = probs
        attend(probs.astype(BF16), packed_s, h, attended_s)
    loads[3].wait()
    project_out(attended_s, wos, branch_s)
    for rows in chunks():
        hidden_out[rows, :] = (lat[rows, :].astype(F32) + mod[2] * branch_s[rows, :]).astype(BF16)
    loads[4].wait()
    loads[5].wait()
    gated(grad_out, mod, 5, d_modulated)
    d_attended_out[...] = dot(d_modulated[...], wot[...], NT).astype(BF16)
    pl.semaphore_wait(barrier, SEQ + 13 + jnp.where(place.x == place.y, 0, 4))
    send_all(hidden_trip)
    send_all(attended_trip)
    send_all(cot_trip)
    d_attended[here, :] = d_attended_out[here, :]
    hidden[here, :] = hidden_out[here, :]
    right_s[2, :, HE:] = attended_s[...]
    pair_s.start(0)

    hidden_trip.wait_recv()
    normalise(hidden, mod, 3, normed_t, scale_t, modulated_t)
    pair_t.start(0)
    loads[6].wait()
    project(modulated_t, wqt, packed_t)
    patch_row = lax.rem(lax.broadcasted_iota(jnp.int32, (TOKENS, TOKENS), 0), 16)
    patch_col = lax.rem(lax.broadcasted_iota(jnp.int32, (TOKENS, TOKENS), 1), 16)
    mask = patch_row == patch_col
    for h in range(HEADS):
        probs = probabilities(packed_t, h, mask)
        probs_t[h] = probs
        attend(probs.astype(BF16), packed_t, h, attended_t)
    project_out(attended_t, wot, branch_t)
    attended_trip.wait_recv()
    for h in range(HEADS):
        probs = probs_t[h]
        head_backward(probs, probs.astype(BF16), packed_t, d_attended, h, right_t)
    right_t[2, :, HE:] = attended_t[...]
    pair_t.start(2)
    project_back(right_t, wqt, d_modulated)
    loads[7].wait()
    cot_trip.wait_recv()
    d_offset, d_stretch = normalise_back(
        d_modulated, normed_t, scale_t, mod, 3, cot, grad_out
    )
    send_all(grad_trip)
    gated(cot, mod, 5, d_branch_t)
    pair_t.start(1)
    clip_first = held.at[0]
    clip_first[3:4, :] = d_offset
    clip_first[4:5, :] = d_stretch
    clip_first[5:6, :] = gate_sum(cot, branch_t)
    grad_hidden[here, :] = grad_out[here, :]
    pair_t.wait_recv()
    for p in range(3):
        pair_t.multiply(p, whole.at[1, p])
        sums_t[p].stage0()
    sums_t[0].stage1()

    grad_trip.wait_recv()
    gated(grad_hidden, mod, 2, d_branch_s)
    pair_s.start(1)
    d_attended[...] = dot(d_branch_s[...], wos[...], NT).astype(BF16)
    for h in range(HEADS):
        probs = probs_s[h]
        head_backward(probs, probs.astype(BF16), packed_s, d_attended, h, right_s)
    pair_s.start(2)
    project_back(right_s, wqs, d_modulated)
    sums_t[1].stage1()
    sums_t[2].stage1()
    pair_s.wait_recv()
    for p in (2, 1, 0):
        pair_s.multiply(p, whole.at[0, p])
        sums_s[p].stage0()
    sums_t[0].stage2()
    sums_t[1].stage2()
    sums_t[2].stage2()
    d_offset, d_stretch = normalise_back(
        d_modulated, normed_s, scale_s, mod, 0, grad_hidden, grad_latents
    )
    clip_first[0:1, :] = d_offset
    clip_first[1:2, :] = d_stretch
    clip_first[2:3, :] = gate_sum(grad_hidden, branch_s)
    clip_first[6:8, :] = jnp.zeros((2, D), F32)
    clip.start()
    for p in range(3):
        sums_t[p].stage3()
    for p in (2, 1, 0):
        sums_s[p].stage1()
    clip.step(0)
    for p in (2, 1, 0):
        sums_s[p].stage2()
    owned = [sums.stage4() for sums in sums_t]
    clip.step(1)
    for p in (2, 1, 0):
        sums_s[p].stage3()
    clip.step(2)
    owned_s = [sums.stage4() for sums in sums_s]
    clip.step(3)
    for i in range(6):
        moments[i] = held[4, i : i + 1, :]
    write_rows([sums.stage5(own) for sums, own in zip(sums_t, owned)], dqkv_t, dout_t)
    for part in (*trips, pair_s, pair_t, *sums_t, clip):
        part.wait_send()
    results_s = [sums.stage5(own) for sums, own in zip(sums_s, owned_s)]
    write_rows(results_s, dqkv_s, dout_s)
    for part in sums_s:
        part.wait_send()


def write_rows(results, dqkv, dout):
    for p, (low, high) in enumerate(results):
        dqkv[:, PART * p : PART * p + PART] = low
        start = 2 * HE + PART * p
        if p == 0:
            dqkv[:, start : start + PART] = high
        elif p == 1:
            dqkv[:, start:] = high[:, : PACKED - start]
            dout[:, : PART - (PACKED - start)] = high[:, PACKED - start :]
        else:
            dout[:, start - PACKED :] = high


def copy_out(*refs):
    for source, target in zip(refs[:6], refs[6:]):
        target[...] = source[...]


def local(latents, cotangent, modulation, spatial_qkv, spatial_out, temporal_qkv, temporal_out):
    vm = pl.BlockSpec(memory_space=pltpu.VMEM)
    hbm = pl.BlockSpec(memory_space=pl.ANY)
    sds = jax.ShapeDtypeStruct

    def bf16(*shape):
        return pltpu.VMEM(shape, BF16)

    def f32(*shape):
        return pltpu.VMEM(shape, F32)

    wide, wide32, column, narrow = bf16(TOKENS, D), f32(TOKENS, D), f32(TOKENS, 1), bf16(TOKENS, HE)
    three, wq, wo = bf16(TOKENS, PACKED), bf16(PACKED, D), bf16(HE, D)
    left, right = bf16(2, 2, TOKENS, D), bf16(4, TOKENS, 2 * HE)
    dma = pltpu.SemaphoreType.DMA
    shapes = [
        sds((TOKENS, D), BF16),
        sds((6, 1, D), F32),
        sds((9, PACKED), F32),
        sds((9, HE), F32),
        sds((9, PACKED), F32),
        sds((9, HE), F32),
    ]
    outs = pl.pallas_call(
        kernel,
        out_shape=shapes,
        in_specs=[hbm] * 7,
        out_specs=[vm] * 6,
        scratch_shapes=[
            wide, f32(6, 1, D), wq, wo, wq, wo,
            wide32, column, three, f32(HEADS, TOKENS, TOKENS), narrow, wide32, wide, wide,
            wide, wide32, column, three, f32(HEADS, TOKENS, TOKENS), narrow, wide32, wide, wide, narrow, narrow, wide,
            left, right, left, right,
            bf16(2, 3, 2, 4, SLAB, PART), bf16(2, 3, 2, 2, SLAB, PART), bf16(2, 3, 2, SLAB, PART),
            bf16(2, 3, 4, BLOCK, PART), bf16(2, 3, 3, BLOCK, PART), bf16(2, 3, 4, 16, PART + 128),
            bf16(2, 3, 4, 16, PART + 128), f32(2, 3, 16, PART), f32(2, 3, 16, PART),
            f32(5, 8, D), f32(4, 8, D),
            dma((8,)), dma((4, SEQ)), dma((4, SEQ)), dma((2, 3)), dma((2, 3)),
            dma((2, 3, 11)), dma((2, 3, 11)), dma((4,)), dma((4,)),
        ],
        compiler_params=pltpu.CompilerParams(
            collective_id=0, has_side_effects=True, vmem_limit_bytes=62 * 2**20
        ),
    )(
        latents.reshape(TOKENS, D), cotangent.reshape(TOKENS, D), modulation.transpose(1, 0, 2),
        spatial_qkv.T, spatial_out.T, temporal_qkv.T, temporal_out.T,
    )
    grad, moments, *grads = pl.pallas_call(
        copy_out,
        out_shape=shapes,
        in_specs=[vm] * 6,
        out_specs=[vm] * 6,
    )(*outs)
    return (grad.reshape(latents.shape), moments.transpose(1, 0, 2), *grads)


def solution(mesh):
    in_specs = (
        P("dp", "seq", None, None),
        P("dp", "seq", None, None),
        P("dp", None, None),
        P(),
        P(),
        P(),
        P(),
    )
    out_specs = (
        P("dp", "seq", None, None),
        P("dp", None, None),
        P(("dp", "seq"), None),
        P(("dp", "seq"), None),
        P(("dp", "seq"), None),
        P(("dp", "seq"), None),
    )
    return jax.shard_map(local, mesh=mesh, in_specs=in_specs, out_specs=out_specs, check_vma=False)
```

```python
import functools

import jax
import jax.numpy as jnp
from jax import lax
from jax.experimental import pallas as pl
from jax.experimental.pallas import tpu as pltpu
from jax.sharding import PartitionSpec as P

HEADS = 8
HEAD_DIM = 72
HE = HEADS * HEAD_DIM
PACKED = 3 * HE
D = 1152
TOKENS = 256
SEQ = 16
EPSILON = 1e-06
FACTOR = HEAD_DIM**-0.5
SLAB = 144
BLOCK = 80
PART = 384
MESH = pl.DeviceIdType.MESH
F32 = jnp.float32
BF16 = jnp.bfloat16

NN = (((1,), (0,)), ((), ()))
NT = (((1,), (1,)), ((), ()))
TN = (((0,), (0,)), ((), ()))


def dot(a, b, dims=NN):
    return lax.dot_general(a, b, dims, preferred_element_type=F32)


def rows_of(i, size):
    return pl.ds(pl.multiple_of(i * size, size), size)


def chunks(size=32):
    return [slice(i, i + size) for i in range(0, TOKENS, size)]


def normalise(source, mod, row, normed, scale, modulated):
    offset = mod[row]
    stretch = 1.0 + mod[row + 1]
    for rows in chunks():
        x = source[rows, :].astype(F32)
        centred = x - jnp.mean(x, axis=-1, keepdims=True)
        spread = jnp.mean(centred * centred, axis=-1, keepdims=True)
        inverse = lax.rsqrt(spread + EPSILON)
        n = centred * inverse
        normed[rows, :] = n
        scale[rows, :] = inverse
        modulated[rows, :] = (n * stretch + offset).astype(BF16)


def project(modulated, weight, packed):
    packed[...] = dot(modulated[...], weight[...], NT).astype(BF16)


def project_out(attended, weight, out):
    out[...] = dot(attended[...], weight[...])


def project_back(right, weight, out):
    total = dot(right[0], weight[: 2 * HE, :]) + dot(right[2, :, :HE], weight[2 * HE :, :])
    out[...] = total.astype(BF16)


def head(ref, h, section=0):
    lane = section * HE + h * HEAD_DIM
    return ref[:, lane : lane + HEAD_DIM]


def probabilities(packed, h, mask):
    scores = dot(head(packed, h, 1), head(packed, h, 0), NT)
    raised = jnp.exp(scores * FACTOR)
    if mask is not None:
        raised = jnp.where(mask, raised, 0.0)
    return raised * (1.0 / jnp.sum(raised, axis=0, keepdims=True))


def head_backward(probs, weights, packed, d_attended, h, right):
    d_head = head(d_attended, h)
    d_weights = dot(head(packed, h, 2), d_head, NT)
    carried = jnp.sum(d_weights * probs, axis=0, keepdims=True)
    d_scores = (probs * (d_weights - carried) * FACTOR).astype(BF16)
    lane = h * HEAD_DIM
    right[0, :, lane : lane + HEAD_DIM] = dot(d_scores, head(packed, h, 1), TN).astype(BF16)
    right[0, :, HE + lane : HE + lane + HEAD_DIM] = dot(d_scores, head(packed, h, 0)).astype(BF16)
    right[2, :, lane : lane + HEAD_DIM] = dot(weights, d_head).astype(BF16)


def attend(weights, packed, h, attended):
    lane = h * HEAD_DIM
    attended[:, lane : lane + HEAD_DIM] = dot(weights, head(packed, h, 2), TN).astype(BF16)


def fold(x):
    return sum(x[8 * i : 8 * i + 8] for i in range(x.shape[0] // 8))


def gated(source, mod, row, out):
    out[...] = (source[...].astype(F32) * mod[row]).astype(BF16)


def gate_sum(upstream, branch):
    total = jnp.zeros((8, D), F32)
    for rows in chunks():
        total = total + fold(upstream[rows, :].astype(F32) * branch[rows, :])
    return jnp.sum(total, axis=0, keepdims=True)


def normalise_back(d_modulated, normed, scale, mod, row, upstream, out):
    stretch = 1.0 + mod[row + 1]
    totals = [jnp.zeros((8, D), F32)] * 2
    for rows in chunks():
        g = d_modulated[rows, :].astype(F32)
        n = normed[rows, :]
        dn = g * stretch
        first = jnp.mean(dn, axis=-1, keepdims=True)
        second = jnp.mean(dn * n, axis=-1, keepdims=True)
        dx = scale[rows, :] * (dn - first - n * second)
        out[rows, :] = (upstream[rows, :].astype(F32) + dx).astype(BF16)
        totals = [total + fold(term) for total, term in zip(totals, (g, g * n))]
    return [jnp.sum(t, axis=0, keepdims=True) for t in totals]


def swap1(i):
    return i + 1 - 2 * lax.rem(i, 2)


class Place:
    def __init__(self):
        self.dp = lax.axis_index("dp")
        self.seq = lax.axis_index("seq")
        self.x = lax.rem(self.dp, 4)
        self.yh = lax.div(self.dp, 4)
        self.yl = lax.div(self.seq, 8)
        self.y = 2 * self.yh + self.yl
        self.z = lax.rem(lax.div(self.seq, 2), 4)
        self.core = lax.rem(self.seq, 2)

    def at(self, x=None, y=None, z=None, core=None):
        x = self.x if x is None else x
        y = self.y if y is None else y
        z = self.z if z is None else z
        core = self.core if core is None else core
        return {
            "dp": 4 * lax.div(y, 2) + x,
            "seq": 8 * lax.rem(y, 2) + 2 * z + core,
        }

    def pair(self, i):
        near, far = swap1(i), 3 - i
        return near + self.core * (far - near), far + self.core * (near - far)


def remote(src, dst, send, recv, device):
    return pltpu.make_async_remote_copy(
        src_ref=src, dst_ref=dst, send_sem=send, recv_sem=recv, device_id=device, device_id_type=MESH
    )


class PairTerms:
    def __init__(self, place, left, right, send, recv):
        self.core = place.core
        other = place.at(core=1 - place.core)
        away = 2 - 2 * place.core
        self.left, self.right = left, right
        self.copies = [
            remote(left.at[0, 0], left.at[0, 1], send.at[0], recv.at[0], other),
            remote(left.at[1, 0], left.at[1, 1], send.at[1], recv.at[1], other),
            remote(right.at[away], right.at[away + 1], send.at[2], recv.at[2], other),
        ]

    def start(self, i):
        if i == 1:
            pl.when(self.core == 0)(self.copies[1].start)
        else:
            self.copies[i].start()

    def wait_recv(self):
        self.copies[0].wait_recv()
        pl.when(self.core == 1)(self.copies[1].wait_recv)
        self.copies[2].wait_recv()

    def wait_send(self):
        self.copies[0].wait_send()
        pl.when(self.core == 0)(self.copies[1].wait_send)
        self.copies[2].wait_send()

    def multiply(self, part, out):
        first = PART * part
        pieces = [(first, first + PART)]
        if part == 1:
            pieces = [(first, HE), (HE, first + PART)]
        for low, high in pieces:
            left = self.left[0 if high <= HE else self.core].reshape(2 * TOKENS, D)
            right = self.right[pl.ds(2 * self.core, 2), :, low:high].reshape(2 * TOKENS, high - low)
            total = dot(left, right, TN)
            for yh in range(2):
                for x in range(4):
                    row = SLAB * (4 * yh + x)
                    out[yh, x, :, low - first : high - first] = total[row : row + SLAB].astype(BF16)


class Reduction:
    def __init__(self, place, names, outer, whole, first, pair, half, second, quarter, third, final, other, send, recv):
        self.place, self.names = place, names
        self.whole, self.first, self.pair, self.half, self.second = whole, first, pair, half, second
        self.quarter, self.third, self.final, self.other = quarter, third, final, other
        self.at = [getattr(place, name) for name in names]
        a = self.at[0]
        a1, self.a2 = (3 - a, swap1(a)) if outer else place.pair(a)
        to_a1, to_a2 = place.at(**{names[0]: a1}), place.at(**{names[0]: self.a2})
        self.copies = [
            remote(whole.at[:, lax.rem(a + 2, 4)], first.at[1], send.at[0], recv.at[0], to_a1),
            remote(whole.at[:, a1], first.at[0], send.at[1], recv.at[1], to_a1),
            remote(whole.at[:, self.a2], pair, send.at[2], recv.at[2], to_a2),
        ]
        for j in range(1, 4):
            peer = lax.rem(self.at[1] + j, 4)
            self.copies.append(
                remote(half.at[peer], second.at[j - 1], send.at[2 + j], recv.at[2 + j], place.at(**{names[1]: peer}))
            )
        x, y, z = place.x, place.y, place.z
        owner = {n: getattr(place, m) for n, m in zip("xy", names)}
        came = dict(zip(names[:2], (x, y)))
        self.owns = [jnp.logical_and(jnp.logical_and(owner["x"] == x, owner["y"] == y), z == j) for j in range(4)]
        self.took = [
            jnp.logical_and(
                jnp.logical_and(getattr(place, names[0]) == x, getattr(place, names[1]) == y), self.at[2] == k
            )
            for k in range(4)
        ]
        self.out = [
            remote(
                quarter.at[j], third.at[self.at[2]], send.at[6 + j], recv.at[6 + self.at[2]],
                place.at(**owner, z=j),
            )
            for j in range(4)
        ]
        self.back = [
            remote(
                quarter.at[0], third.at[k], send.at[6 + k], recv.at[6 + k],
                place.at(**came, **{names[2]: k}),
            )
            for k in range(4)
        ]
        self.swap = remote(final, other, send.at[10], recv.at[10], place.at(core=1 - place.core))

    def start_out(self):
        for j in range(4):
            pl.when(jnp.logical_not(self.owns[j]))(self.out[j].start)

            @pl.when(self.owns[j])
            def _():
                self.third[self.at[2]] = self.quarter[j]

    def wait_back(self):
        for k in range(4):
            pl.when(jnp.logical_not(self.took[k]))(self.back[k].wait_recv)

    def stage0(self):
        self.copies[0].start()
        self.copies[1].start()

    def stage1(self):
        self.copies[0].wait_recv()
        for yh in range(2):
            kept = self.whole.at[yh, self.a2]
            kept[...] = (kept[...].astype(F32) + self.first[1, yh].astype(F32)).astype(BF16)
        self.copies[2].start()

    def stage2(self):
        self.copies[1].wait_recv()
        self.copies[2].wait_recv()
        for yh in range(2):
            total = self.whole[yh, self.at[0]].astype(F32) + self.first[0, yh].astype(F32)
            total = total + self.pair[yh].astype(F32)
            self.half[2 * yh, :72] = total[:72].astype(BF16)
            self.half[2 * yh + 1, :72] = total[72:].astype(BF16)
        for copy in self.copies[3:]:
            copy.start()

    def stage3(self):
        for copy in self.copies[3:]:
            copy.wait_recv()
        total = self.half[self.at[1]].astype(F32)
        for k in range(3):
            total = total + self.second[k].astype(F32)
        for j in range(4):
            main, rest = total[18 * j : 18 * j + 16], total[18 * j + 16 : 18 * j + 18]
            strips = [rest[:, 128 * i : 128 * i + 128] for i in range(3)]
            strips.append(jnp.zeros((10, 128), F32))
            self.quarter[j] = jnp.concatenate([main, jnp.concatenate(strips, axis=0)], axis=1).astype(BF16)
        self.start_out()

    def stage4(self):
        self.wait_back()
        total = self.third[0].astype(F32)
        for k in range(1, 4):
            total = total + self.third[k].astype(F32)
        total = total * (1.0 / 8)
        strips = [total[2 * i : 2 * i + 2, PART:] for i in range(3)]
        rows = [total[:, :PART], jnp.concatenate(strips, axis=1), jnp.zeros((6, PART), F32)]
        rows, core = jnp.concatenate(rows, axis=0), self.place.core
        self.final[...] = pltpu.roll(rows, lax.rem(24 - 9 * (1 - core), 24), 0)[:16]
        self.swap.start()
        return pltpu.roll(rows, lax.rem(24 - 9 * core, 24), 0)[:16]

    def stage5(self, own):
        self.swap.wait_recv()
        low = self.place.core == 0
        theirs = self.other[...]
        return jnp.where(low, own, theirs)[:9], jnp.where(low, theirs, own)[:9]

    def wait_send(self):
        for copy in self.copies:
            copy.wait_send()
        for j in range(4):
            pl.when(jnp.logical_not(self.owns[j]))(self.out[j].wait_send)
        self.swap.wait_send()


class ClipSum:
    def __init__(self, place, held, arrived, send, recv):
        self.held, self.arrived = held, arrived
        devices = [
            place.at(core=1 - place.core),
            place.at(z=swap1(place.z)),
            place.at(z=3 - place.z),
            place.at(y=swap1(place.y)),
        ]
        self.copies = [
            remote(held.at[i], arrived.at[i], send.at[i], recv.at[i], device)
            for i, device in enumerate(devices)
        ]

    def start(self):
        self.copies[0].start()

    def step(self, i):
        self.copies[i].wait_recv()
        self.held[i + 1] = self.held[i] + self.arrived[i]
        if i < 3:
            self.copies[i + 1].start()

    def wait_send(self):
        for copy in self.copies:
            copy.wait_send()


class Exchange:
    def __init__(self, source, target, send, recv):
        self.source, self.target, self.send, self.recv = source, target, send, recv
        self.me = lax.axis_index("seq")

    def to(self, j):
        peer = lax.rem(self.me + j, SEQ)
        return pltpu.make_async_remote_copy(
            src_ref=self.source.at[rows_of(peer, 16)],
            dst_ref=self.target.at[rows_of(self.me, 16)],
            send_sem=self.send.at[j],
            recv_sem=self.recv.at[j],
            device_id={"seq": peer},
            device_id_type=MESH,
        )

    def start(self, j):
        self.to(j).start()

    def wait_recv(self):
        def body(j, _):
            sender = lax.rem(self.me + SEQ - j, SEQ)
            pltpu.make_async_remote_copy(
                src_ref=self.source.at[rows_of(sender, 16)],
                dst_ref=self.target.at[rows_of(sender, 16)],
                send_sem=self.send.at[j],
                recv_sem=self.recv.at[j],
                device_id={"seq": sender},
                device_id_type=MESH,
            ).wait_recv()
            return 0

        lax.fori_loop(1, SEQ, body, 0)

    def wait_send(self):
        def body(j, _):
            self.to(j).wait_send()
            return 0

        lax.fori_loop(1, SEQ, body, 0)


def kernel(
    lat_hbm, cot_hbm, mod_hbm, wqs_hbm, wos_hbm, wqt_hbm, wot_hbm,
    grad_latents, moments, dqkv_s, dout_s, dqkv_t, dout_t,
    lat, mod, wqs, wos, wqt, wot,
    normed_s, scale_s, packed_s, probs_s, attended_s, branch_s, hidden_out, hidden,
    cot, normed_t, scale_t, packed_t, probs_t, attended_t, branch_t, grad_out, grad_hidden, d_attended_out, d_attended, d_modulated,
    left_s, right_s, left_t, right_t,
    whole, first, pair, half, second, quarter, third, final, other,
    held, arrived,
    load_sem, send_sem, recv_sem, pair_send, pair_recv, sum_send, sum_recv, clip_send, clip_recv,
):
    place = Place()
    me = place.seq
    here = rows_of(me, 16)
    modulated_s, d_branch_s = left_s.at[0, 0], left_s.at[1, 0]
    modulated_t, d_branch_t = left_t.at[0, 0], left_t.at[1, 0]
    loads = [
        pltpu.make_async_copy(src, dst, load_sem.at[i])
        for i, (src, dst) in enumerate(
            [
                (lat_hbm, lat), (mod_hbm, mod), (wqs_hbm, wqs), (wos_hbm, wos), (cot_hbm, grad_out), (wot_hbm, wot),
                (wqt_hbm, wqt), (cot_hbm.at[here], cot.at[here]),
            ]
        )
    ]
    for load in loads:
        load.start()

    barrier = pltpu.get_barrier_semaphore()

    def signal(device):
        pl.semaphore_signal(barrier, inc=1, device_id=device, device_id_type=MESH)

    def greet(j, _):
        signal({"seq": lax.rem(me + j, SEQ)})
        return 0

    lax.fori_loop(1, SEQ, greet, 0)
    for j in range(1, 4):
        for k in range(4):
            signal(place.at(x=lax.rem(place.x + j, 4), z=k))
    for k in range(4):
        signal(place.at(y=lax.rem(place.y + 2, 4), z=k))
        signal(place.at(y=3 - place.y, z=k))

    @pl.when(place.x != place.y)
    def _():
        for k in range(4):
            signal(place.at(x=place.y, y=place.x, z=k))

    loads[0].wait()
    loads[1].wait()
    normalise(lat, mod, 0, normed_s, scale_s, modulated_s)
    trips = [
        Exchange(source, target, send_sem.at[i], recv_sem.at[i])
        for i, (source, target) in enumerate(
            [(cot_hbm, cot), (hidden_out, hidden), (grad_out, grad_hidden), (d_attended_out, d_attended)]
        )
    ]
    cot_trip, hidden_trip, grad_trip, attended_trip = trips
    pair_s = PairTerms(place, left_s, right_s, pair_send.at[0], pair_recv.at[0])
    pair_t = PairTerms(place, left_t, right_t, pair_send.at[1], pair_recv.at[1])
    sums_s, sums_t = [
        [
            Reduction(
                place, names[p], l == 1 and p == 2, whole.at[l, p], first.at[l, p], pair.at[l, p], half.at[l, p], second.at[l, p],
                quarter.at[l, p], third.at[l, p], final.at[l, p], other.at[l, p],
                sum_send.at[l, p], sum_recv.at[l, p],
            )
            for p in range(3)
        ]
        for l, names in enumerate((("xzy", "yxz", "zyx"), ("xzy", "xzy", "yxz")))
    ]
    clip = ClipSum(place, held, arrived, clip_send, clip_recv)

    def send_all(trip):
        for j in range(1, SEQ):
            trip.start(j)

    loads[2].wait()
    project(modulated_s, wqs, packed_s)
    for h in range(HEADS):
        probs = probabilities(packed_s, h, None)
        probs_s[h] = probs
        attend(probs.astype(BF16), packed_s, h, attended_s)
    loads[3].wait()
    project_out(attended_s, wos, branch_s)
    for rows in chunks():
        hidden_out[rows, :] = (lat[rows, :].astype(F32) + mod[2] * branch_s[rows, :]).astype(BF16)
    loads[4].wait()
    loads[5].wait()
    gated(grad_out, mod, 5, d_modulated)
    d_attended_out[...] = dot(d_modulated[...], wot[...], NT).astype(BF16)
    pl.semaphore_wait(barrier, SEQ + 19 + jnp.where(place.x == place.y, 0, 4))
    send_all(hidden_trip)
    send_all(attended_trip)
    send_all(cot_trip)
    d_attended[here, :] = d_attended_out[here, :]
    hidden[here, :] = hidden_out[here, :]
    right_s[2, :, HE:] = attended_s[...]
    pair_s.start(0)

    hidden_trip.wait_recv()
    normalise(hidden, mod, 3, normed_t, scale_t, modulated_t)
    pair_t.start(0)
    loads[6].wait()
    project(modulated_t, wqt, packed_t)
    patch_row = lax.rem(lax.broadcasted_iota(jnp.int32, (TOKENS, TOKENS), 0), 16)
    patch_col = lax.rem(lax.broadcasted_iota(jnp.int32, (TOKENS, TOKENS), 1), 16)
    mask = patch_row == patch_col
    for h in range(HEADS):
        probs = probabilities(packed_t, h, mask)
        probs_t[h] = probs
        attend(probs.astype(BF16), packed_t, h, attended_t)
    project_out(attended_t, wot, branch_t)
    attended_trip.wait_recv()
    for h in range(HEADS):
        probs = probs_t[h]
        head_backward(probs, probs.astype(BF16), packed_t, d_attended, h, right_t)
    right_t[2, :, HE:] = attended_t[...]
    pair_t.start(2)
    project_back(right_t, wqt, d_modulated)
    loads[7].wait()
    cot_trip.wait_recv()
    d_offset, d_stretch = normalise_back(
        d_modulated, normed_t, scale_t, mod, 3, cot, grad_out
    )
    send_all(grad_trip)
    gated(cot, mod, 5, d_branch_t)
    pair_t.start(1)
    clip_first = held.at[0]
    clip_first[3:4, :] = d_offset
    clip_first[4:5, :] = d_stretch
    clip_first[5:6, :] = gate_sum(cot, branch_t)
    grad_hidden[here, :] = grad_out[here, :]
    pair_t.wait_recv()
    for p in range(3):
        pair_t.multiply(p, whole.at[1, p])
        sums_t[p].stage0()
    sums_t[0].stage1()

    grad_trip.wait_recv()
    gated(grad_hidden, mod, 2, d_branch_s)
    pair_s.start(1)
    d_attended[...] = dot(d_branch_s[...], wos[...], NT).astype(BF16)
    for h in range(HEADS):
        probs = probs_s[h]
        head_backward(probs, probs.astype(BF16), packed_s, d_attended, h, right_s)
    pair_s.start(2)
    project_back(right_s, wqs, d_modulated)
    sums_t[1].stage1()
    sums_t[2].stage1()
    sums_t[0].stage2()
    pair_s.wait_recv()
    for p in (2, 1, 0):
        pair_s.multiply(p, whole.at[0, p])
        sums_s[p].stage0()
    d_offset, d_stretch = normalise_back(
        d_modulated, normed_s, scale_s, mod, 0, grad_hidden, lat
    )
    leave = pltpu.make_async_copy(lat, grad_latents, load_sem.at[8])
    leave.start()
    clip_first[0:1, :] = d_offset
    clip_first[1:2, :] = d_stretch
    clip_first[2:3, :] = gate_sum(grad_hidden, branch_s)
    clip_first[6:8, :] = jnp.zeros((2, D), F32)
    clip.start()
    sums_t[1].stage2()
    sums_t[0].stage3()
    sums_t[2].stage2()
    for p in (2, 1, 0):
        sums_s[p].stage1()
    clip.step(0)
    sums_t[1].stage3()
    sums_t[2].stage3()
    for p in (2, 1, 0):
        sums_s[p].stage2()
    owned = [sums_t[0].stage4(), sums_t[1].stage4()]
    clip.step(1)
    for p in (2, 1, 0):
        sums_s[p].stage3()
    owned.append(sums_t[2].stage4())
    clip.step(2)
    owned_s = [sums.stage4() for sums in sums_s]
    clip.step(3)
    for i in range(6):
        moments[i] = held[4, i : i + 1, :]
    write_rows([sums.stage5(own) for sums, own in zip(sums_t, owned)], dqkv_t, dout_t)
    for part in (*trips, pair_s, pair_t, *sums_t, clip):
        part.wait_send()
    results_s = [sums.stage5(own) for sums, own in zip(sums_s, owned_s)]
    write_rows(results_s, dqkv_s, dout_s)
    for part in sums_s:
        part.wait_send()
    leave.wait()


def write_rows(results, dqkv, dout):
    for p, (low, high) in enumerate(results):
        dqkv[:, PART * p : PART * p + PART] = low
        start = 2 * HE + PART * p
        if p == 0:
            dqkv[:, start : start + PART] = high
        elif p == 1:
            dqkv[:, start:] = high[:, : PACKED - start]
            dout[:, : PART - (PACKED - start)] = high[:, PACKED - start :]
        else:
            dout[:, start - PACKED :] = high


def copy_out(*refs):
    for source, target in zip(refs[:6], refs[6:]):
        target[...] = source[...]


def local(latents, cotangent, modulation, spatial_qkv, spatial_out, temporal_qkv, temporal_out):
    vm = pl.BlockSpec(memory_space=pltpu.VMEM)
    hbm = pl.BlockSpec(memory_space=pl.ANY)
    sds = jax.ShapeDtypeStruct

    def bf16(*shape):
        return pltpu.VMEM(shape, BF16)

    def f32(*shape):
        return pltpu.VMEM(shape, F32)

    wide, wide32, column, narrow = bf16(TOKENS, D), f32(TOKENS, D), f32(TOKENS, 1), bf16(TOKENS, HE)
    three, wq, wo = bf16(TOKENS, PACKED), bf16(PACKED, D), bf16(HE, D)
    left, right = bf16(2, 2, TOKENS, D), bf16(4, TOKENS, 2 * HE)
    dma = pltpu.SemaphoreType.DMA
    shapes = [
        sds((TOKENS, D), BF16),
        sds((6, 1, D), F32),
        sds((9, PACKED), F32),
        sds((9, HE), F32),
        sds((9, PACKED), F32),
        sds((9, HE), F32),
    ]
    outs = pl.pallas_call(
        kernel,
        out_shape=shapes,
        in_specs=[hbm] * 7,
        out_specs=[hbm] + [vm] * 5,
        scratch_shapes=[
            wide, f32(6, 1, D), wq, wo, wq, wo,
            wide32, column, three, f32(HEADS, TOKENS, TOKENS), narrow, wide32, wide, wide,
            wide, wide32, column, three, f32(HEADS, TOKENS, TOKENS), narrow, wide32, wide, wide, narrow, narrow, wide,
            left, right, left, right,
            bf16(2, 3, 2, 4, SLAB, PART), bf16(2, 3, 2, 2, SLAB, PART), bf16(2, 3, 2, SLAB, PART),
            bf16(2, 3, 4, BLOCK, PART), bf16(2, 3, 3, BLOCK, PART), bf16(2, 3, 4, 16, PART + 128),
            bf16(2, 3, 4, 16, PART + 128), f32(2, 3, 16, PART), f32(2, 3, 16, PART),
            f32(5, 8, D), f32(4, 8, D),
            dma((9,)), dma((4, SEQ)), dma((4, SEQ)), dma((2, 3)), dma((2, 3)),
            dma((2, 3, 11)), dma((2, 3, 11)), dma((4,)), dma((4,)),
        ],
        compiler_params=pltpu.CompilerParams(
            collective_id=0, has_side_effects=True, vmem_limit_bytes=62 * 2**20
        ),
    )(
        latents.reshape(TOKENS, D), cotangent.reshape(TOKENS, D), modulation.transpose(1, 0, 2),
        spatial_qkv.T, spatial_out.T, temporal_qkv.T, temporal_out.T,
    )
    grad, moments, *grads = pl.pallas_call(
        copy_out,
        out_shape=shapes,
        in_specs=[vm] * 6,
        out_specs=[vm] * 6,
    )(*outs)
    return (grad.reshape(latents.shape), moments.transpose(1, 0, 2), *grads)


def solution(mesh):
    in_specs = (
        P("dp", "seq", None, None),
        P("dp", "seq", None, None),
        P("dp", None, None),
        P(),
        P(),
        P(),
        P(),
    )
    out_specs = (
        P("dp", "seq", None, None),
        P("dp", None, None),
        P(("dp", "seq"), None),
        P(("dp", "seq"), None),
        P(("dp", "seq"), None),
        P(("dp", "seq"), None),
    )
    return jax.shard_map(local, mesh=mesh, in_specs=in_specs, out_specs=out_specs, check_vma=False)
```

```python
import functools

import jax
import jax.numpy as jnp
from jax import lax
from jax.experimental import pallas as pl
from jax.experimental.pallas import tpu as pltpu
from jax.sharding import PartitionSpec as P

HEADS = 8
HEAD_DIM = 72
HE = HEADS * HEAD_DIM
PACKED = 3 * HE
D = 1152
TOKENS = 256
SEQ = 16
EPSILON = 1e-06
FACTOR = HEAD_DIM**-0.5
SLAB = 144
BLOCK = 80
PART = 384
MESH = pl.DeviceIdType.MESH
F32 = jnp.float32
BF16 = jnp.bfloat16

NN = (((1,), (0,)), ((), ()))
NT = (((1,), (1,)), ((), ()))
TN = (((0,), (0,)), ((), ()))


def dot(a, b, dims=NN):
    return lax.dot_general(a, b, dims, preferred_element_type=F32)


def rows_of(i, size):
    return pl.ds(pl.multiple_of(i * size, size), size)


def chunks(size=32):
    return [slice(i, i + size) for i in range(0, TOKENS, size)]


def normalise(source, mod, row, normed, scale, modulated):
    offset = mod[row]
    stretch = 1.0 + mod[row + 1]
    for rows in chunks():
        x = source[rows, :].astype(F32)
        centred = x - jnp.mean(x, axis=-1, keepdims=True)
        spread = jnp.mean(centred * centred, axis=-1, keepdims=True)
        inverse = lax.rsqrt(spread + EPSILON)
        n = centred * inverse
        normed[rows, :] = n
        scale[rows, :] = inverse
        modulated[rows, :] = (n * stretch + offset).astype(BF16)


def project(modulated, weight, packed):
    packed[...] = dot(modulated[...], weight[...], NT).astype(BF16)


def project_out(attended, weight, out):
    out[...] = dot(attended[...], weight[...])


def project_back(right, weight, out):
    total = dot(right[0], weight[: 2 * HE, :]) + dot(right[2, :, :HE], weight[2 * HE :, :])
    out[...] = total.astype(BF16)


def head(ref, h, section=0):
    lane = section * HE + h * HEAD_DIM
    return ref[:, lane : lane + HEAD_DIM]


def probabilities(packed, h, mask):
    scores = dot(head(packed, h, 1), head(packed, h, 0), NT)
    raised = jnp.exp(scores * FACTOR)
    if mask is not None:
        raised = jnp.where(mask, raised, 0.0)
    return raised * (1.0 / jnp.sum(raised, axis=0, keepdims=True))


def head_backward(probs, weights, packed, d_attended, h, right):
    d_head = head(d_attended, h)
    d_weights = dot(head(packed, h, 2), d_head, NT)
    carried = jnp.sum(d_weights * probs, axis=0, keepdims=True)
    d_scores = (probs * (d_weights - carried) * FACTOR).astype(BF16)
    lane = h * HEAD_DIM
    right[0, :, lane : lane + HEAD_DIM] = dot(d_scores, head(packed, h, 1), TN).astype(BF16)
    right[0, :, HE + lane : HE + lane + HEAD_DIM] = dot(d_scores, head(packed, h, 0)).astype(BF16)
    right[2, :, lane : lane + HEAD_DIM] = dot(weights, d_head).astype(BF16)


def attend(weights, packed, h, attended):
    lane = h * HEAD_DIM
    attended[:, lane : lane + HEAD_DIM] = dot(weights, head(packed, h, 2), TN).astype(BF16)


def fold(x):
    return sum(x[8 * i : 8 * i + 8] for i in range(x.shape[0] // 8))


def gated(source, mod, row, out):
    out[...] = (source[...].astype(F32) * mod[row]).astype(BF16)


def gate_sum(upstream, branch):
    total = jnp.zeros((8, D), F32)
    for rows in chunks():
        total = total + fold(upstream[rows, :].astype(F32) * branch[rows, :])
    return jnp.sum(total, axis=0, keepdims=True)


def normalise_back(d_modulated, normed, scale, mod, row, upstream, out):
    stretch = 1.0 + mod[row + 1]
    totals = [jnp.zeros((8, D), F32)] * 2
    for rows in chunks():
        g = d_modulated[rows, :].astype(F32)
        n = normed[rows, :]
        dn = g * stretch
        first = jnp.mean(dn, axis=-1, keepdims=True)
        second = jnp.mean(dn * n, axis=-1, keepdims=True)
        dx = scale[rows, :] * (dn - first - n * second)
        out[rows, :] = (upstream[rows, :].astype(F32) + dx).astype(BF16)
        totals = [total + fold(term) for total, term in zip(totals, (g, g * n))]
    return [jnp.sum(t, axis=0, keepdims=True) for t in totals]


def swap1(i):
    return i + 1 - 2 * lax.rem(i, 2)


class Place:
    def __init__(self):
        self.dp = lax.axis_index("dp")
        self.seq = lax.axis_index("seq")
        self.x = lax.rem(self.dp, 4)
        self.yh = lax.div(self.dp, 4)
        self.yl = lax.div(self.seq, 8)
        self.y = 2 * self.yh + self.yl
        self.z = lax.rem(lax.div(self.seq, 2), 4)
        self.core = lax.rem(self.seq, 2)

    def at(self, x=None, y=None, z=None, core=None):
        x = self.x if x is None else x
        y = self.y if y is None else y
        z = self.z if z is None else z
        core = self.core if core is None else core
        return {
            "dp": 4 * lax.div(y, 2) + x,
            "seq": 8 * lax.rem(y, 2) + 2 * z + core,
        }

    def pair(self, i):
        near, far = swap1(i), 3 - i
        return near + self.core * (far - near), far + self.core * (near - far)


def remote(src, dst, send, recv, device):
    return pltpu.make_async_remote_copy(
        src_ref=src, dst_ref=dst, send_sem=send, recv_sem=recv, device_id=device, device_id_type=MESH
    )


class PairTerms:
    def __init__(self, place, left, right, send, recv):
        self.core = place.core
        other = place.at(core=1 - place.core)
        away = 2 - 2 * place.core
        self.left, self.right = left, right
        self.copies = [
            remote(left.at[0, 0], left.at[0, 1], send.at[0], recv.at[0], other),
            remote(left.at[1, 0], left.at[1, 1], send.at[1], recv.at[1], other),
            remote(right.at[away], right.at[away + 1], send.at[2], recv.at[2], other),
        ]

    def start(self, i):
        if i == 1:
            pl.when(self.core == 0)(self.copies[1].start)
        else:
            self.copies[i].start()

    def wait_recv(self, part):
        if part == 0:
            self.copies[0].wait_recv()
            self.copies[2].wait_recv()
        elif part == 1:
            pl.when(self.core == 1)(self.copies[1].wait_recv)

    def wait_send(self):
        self.copies[0].wait_send()
        pl.when(self.core == 0)(self.copies[1].wait_send)
        self.copies[2].wait_send()

    def multiply(self, part, out):
        first = PART * part
        pieces = [(first, first + PART)]
        if part == 1:
            pieces = [(first, HE), (HE, first + PART)]
        for low, high in pieces:
            left = self.left[0 if high <= HE else self.core].reshape(2 * TOKENS, D)
            right = self.right[pl.ds(2 * self.core, 2), :, low:high].reshape(2 * TOKENS, high - low)
            total = dot(left, right, TN)
            for yh in range(2):
                for x in range(4):
                    row = SLAB * (4 * yh + x)
                    out[yh, x, :, low - first : high - first] = total[row : row + SLAB].astype(BF16)


class Reduction:
    def __init__(self, place, names, outer, whole, first, pair, half, second, quarter, third, final, other, send, recv):
        self.place, self.names = place, names
        self.whole, self.first, self.pair, self.half, self.second = whole, first, pair, half, second
        self.quarter, self.third, self.final, self.other = quarter, third, final, other
        self.at = [getattr(place, name) for name in names]
        a = self.at[0]
        a1, self.a2 = (3 - a, swap1(a)) if outer else place.pair(a)
        to_a1, to_a2 = place.at(**{names[0]: a1}), place.at(**{names[0]: self.a2})
        self.copies = [
            remote(whole.at[:, lax.rem(a + 2, 4)], first.at[1], send.at[0], recv.at[0], to_a1),
            remote(whole.at[:, a1], first.at[0], send.at[1], recv.at[1], to_a1),
            remote(whole.at[:, self.a2], pair, send.at[2], recv.at[2], to_a2),
        ]
        for j in range(1, 4):
            peer = lax.rem(self.at[1] + j, 4)
            self.copies.append(
                remote(half.at[peer], second.at[j - 1], send.at[2 + j], recv.at[2 + j], place.at(**{names[1]: peer}))
            )
        x, y, z = place.x, place.y, place.z
        owner = {n: getattr(place, m) for n, m in zip("xy", names)}
        came = dict(zip(names[:2], (x, y)))
        self.owns = [jnp.logical_and(jnp.logical_and(owner["x"] == x, owner["y"] == y), z == j) for j in range(4)]
        self.took = [
            jnp.logical_and(
                jnp.logical_and(getattr(place, names[0]) == x, getattr(place, names[1]) == y), self.at[2] == k
            )
            for k in range(4)
        ]
        self.out = [
            remote(
                quarter.at[j], third.at[self.at[2]], send.at[6 + j], recv.at[6 + self.at[2]],
                place.at(**owner, z=j),
            )
            for j in range(4)
        ]
        self.back = [
            remote(
                quarter.at[0], third.at[k], send.at[6 + k], recv.at[6 + k],
                place.at(**came, **{names[2]: k}),
            )
            for k in range(4)
        ]
        self.swap = remote(final, other, send.at[10], recv.at[10], place.at(core=1 - place.core))

    def start_out(self):
        for j in range(4):
            pl.when(jnp.logical_not(self.owns[j]))(self.out[j].start)

            @pl.when(self.owns[j])
            def _():
                self.third[self.at[2]] = self.quarter[j]

    def wait_back(self):
        for k in range(4):
            pl.when(jnp.logical_not(self.took[k]))(self.back[k].wait_recv)

    def stage0(self):
        self.copies[0].start()
        self.copies[1].start()

    def stage1(self):
        self.copies[0].wait_recv()
        for yh in range(2):
            kept = self.whole.at[yh, self.a2]
            kept[...] = (kept[...].astype(F32) + self.first[1, yh].astype(F32)).astype(BF16)
        self.copies[2].start()

    def stage2(self):
        self.copies[1].wait_recv()
        self.copies[2].wait_recv()
        for yh in range(2):
            total = self.whole[yh, self.at[0]].astype(F32) + self.first[0, yh].astype(F32)
            total = total + self.pair[yh].astype(F32)
            self.half[2 * yh, :72] = total[:72].astype(BF16)
            self.half[2 * yh + 1, :72] = total[72:].astype(BF16)
        for copy in self.copies[3:]:
            copy.start()

    def stage3(self):
        for copy in self.copies[3:]:
            copy.wait_recv()
        total = self.half[self.at[1]].astype(F32)
        for k in range(3):
            total = total + self.second[k].astype(F32)
        for j in range(4):
            main, rest = total[18 * j : 18 * j + 16], total[18 * j + 16 : 18 * j + 18]
            strips = [rest[:, 128 * i : 128 * i + 128] for i in range(3)]
            strips.append(jnp.zeros((10, 128), F32))
            self.quarter[j] = jnp.concatenate([main, jnp.concatenate(strips, axis=0)], axis=1).astype(BF16)
        self.start_out()

    def stage4(self):
        self.wait_back()
        total = self.third[0].astype(F32)
        for k in range(1, 4):
            total = total + self.third[k].astype(F32)
        total = total * (1.0 / 8)
        strips = [total[2 * i : 2 * i + 2, PART:] for i in range(3)]
        rows = [total[:, :PART], jnp.concatenate(strips, axis=1), jnp.zeros((6, PART), F32)]
        rows, core = jnp.concatenate(rows, axis=0), self.place.core
        self.final[...] = pltpu.roll(rows, lax.rem(24 - 9 * (1 - core), 24), 0)[:16]
        self.swap.start()
        return pltpu.roll(rows, lax.rem(24 - 9 * core, 24), 0)[:16]

    def stage5(self, own):
        self.swap.wait_recv()
        low = self.place.core == 0
        theirs = self.other[...]
        return jnp.where(low, own, theirs)[:9], jnp.where(low, theirs, own)[:9]

    def wait_send(self):
        for copy in self.copies:
            copy.wait_send()

    def wait_send_last(self):
        for j in range(4):
            pl.when(jnp.logical_not(self.owns[j]))(self.out[j].wait_send)
        self.swap.wait_send()


class ClipSum:
    def __init__(self, place, held, arrived, send, recv):
        self.held, self.arrived = held, arrived
        devices = [
            place.at(core=1 - place.core),
            place.at(z=swap1(place.z)),
            place.at(z=3 - place.z),
            place.at(y=swap1(place.y)),
        ]
        self.copies = [
            remote(held.at[i], arrived.at[i], send.at[i], recv.at[i], device)
            for i, device in enumerate(devices)
        ]

    def start(self):
        self.copies[0].start()

    def step(self, i):
        self.copies[i].wait_recv()
        self.held[i + 1] = self.held[i] + self.arrived[i]
        if i < 3:
            self.copies[i + 1].start()

    def wait_send(self):
        for copy in self.copies:
            copy.wait_send()


class Exchange:
    def __init__(self, source, target, send, recv):
        self.source, self.target, self.send, self.recv = source, target, send, recv
        self.me = lax.axis_index("seq")

    def to(self, j):
        peer = lax.rem(self.me + j, SEQ)
        return pltpu.make_async_remote_copy(
            src_ref=self.source.at[rows_of(peer, 16)],
            dst_ref=self.target.at[rows_of(self.me, 16)],
            send_sem=self.send.at[j],
            recv_sem=self.recv.at[j],
            device_id={"seq": peer},
            device_id_type=MESH,
        )

    def start(self, j):
        self.to(j).start()

    def wait_recv(self):
        for j in range(1, SEQ):
            sender = lax.rem(self.me + SEQ - j, SEQ)
            pltpu.make_async_remote_copy(
                src_ref=self.source.at[rows_of(sender, 16)],
                dst_ref=self.target.at[rows_of(sender, 16)],
                send_sem=self.send.at[j],
                recv_sem=self.recv.at[j],
                device_id={"seq": sender},
                device_id_type=MESH,
            ).wait_recv()

    def wait_send(self):
        for j in range(1, SEQ):
            self.to(j).wait_send()


def kernel(
    lat_hbm, cot_hbm, mod_hbm, wqs_hbm, wos_hbm, wqt_hbm, wot_hbm,
    grad_latents, moments, dqkv_s, dout_s, dqkv_t, dout_t,
    lat, mod, wqs, wos, wqt, wot,
    normed_s, scale_s, packed_s, probs_s, attended_s, branch_s, hidden_out, hidden,
    cot, normed_t, scale_t, packed_t, probs_t, attended_t, branch_t, grad_out, grad_hidden, d_attended_out, d_attended, d_modulated,
    left_s, right_s, left_t, right_t,
    whole, first, pair, half, second, quarter, third, final, other,
    held, arrived,
    load_sem, send_sem, recv_sem, pair_send, pair_recv, sum_send, sum_recv, clip_send, clip_recv,
):
    place = Place()
    me = place.seq
    here = rows_of(me, 16)
    modulated_s, d_branch_s = left_s.at[0, 0], left_s.at[1, 0]
    modulated_t, d_branch_t = left_t.at[0, 0], left_t.at[1, 0]
    loads = [
        pltpu.make_async_copy(src, dst, load_sem.at[i])
        for i, (src, dst) in enumerate(
            [
                (lat_hbm, lat), (mod_hbm, mod), (wqs_hbm, wqs), (wos_hbm, wos), (cot_hbm, grad_out), (wot_hbm, wot),
                (wqt_hbm, wqt), (cot_hbm.at[here], cot.at[here]),
            ]
        )
    ]
    for load in loads:
        load.start()

    barrier = pltpu.get_barrier_semaphore()

    def signal(device):
        pl.semaphore_signal(barrier, inc=1, device_id=device, device_id_type=MESH)

    def greet(j, _):
        signal({"seq": lax.rem(me + j, SEQ)})
        return 0

    lax.fori_loop(1, SEQ, greet, 0)
    for j in range(1, 4):
        for k in range(4):
            signal(place.at(x=lax.rem(place.x + j, 4), z=k))
    for k in range(4):
        signal(place.at(y=lax.rem(place.y + 2, 4), z=k))
        signal(place.at(y=3 - place.y, z=k))

    @pl.when(place.x != place.y)
    def _():
        for k in range(4):
            signal(place.at(x=place.y, y=place.x, z=k))

    loads[0].wait()
    loads[1].wait()
    normalise(lat, mod, 0, normed_s, scale_s, modulated_s)
    trips = [
        Exchange(source, target, send_sem.at[i], recv_sem.at[i])
        for i, (source, target) in enumerate(
            [(cot_hbm, cot), (hidden_out, hidden), (grad_out, grad_hidden), (d_attended_out, d_attended)]
        )
    ]
    cot_trip, hidden_trip, grad_trip, attended_trip = trips
    pair_s = PairTerms(place, left_s, right_s, pair_send.at[0], pair_recv.at[0])
    pair_t = PairTerms(place, left_t, right_t, pair_send.at[1], pair_recv.at[1])
    sums_s, sums_t = [
        [
            Reduction(
                place, names[p], l == 1 and p == 2, whole.at[l, p], first.at[l, p], pair.at[l, p], half.at[l, p], second.at[l, p],
                quarter.at[l, p], third.at[l, p], final.at[l, p], other.at[l, p],
                sum_send.at[l, p], sum_recv.at[l, p],
            )
            for p in range(3)
        ]
        for l, names in enumerate((("xzy", "yxz", "zyx"), ("xzy", "xzy", "yxz")))
    ]
    clip = ClipSum(place, held, arrived, clip_send, clip_recv)

    def send_all(trip):
        for j in range(1, SEQ):
            trip.start(j)

    loads[2].wait()
    project(modulated_s, wqs, packed_s)
    for h in range(HEADS):
        probs = probabilities(packed_s, h, None)
        probs_s[h] = probs
        attend(probs.astype(BF16), packed_s, h, attended_s)
    loads[3].wait()
    project_out(attended_s, wos, branch_s)
    for rows in chunks():
        hidden_out[rows, :] = (lat[rows, :].astype(F32) + mod[2] * branch_s[rows, :]).astype(BF16)
    loads[4].wait()
    loads[5].wait()
    gated(grad_out, mod, 5, d_modulated)
    d_attended_out[...] = dot(d_modulated[...], wot[...], NT).astype(BF16)
    pl.semaphore_wait(barrier, SEQ + 19 + jnp.where(place.x == place.y, 0, 4))
    send_all(hidden_trip)
    send_all(attended_trip)
    send_all(cot_trip)
    d_attended[here, :] = d_attended_out[here, :]
    hidden[here, :] = hidden_out[here, :]
    right_s[2, :, HE:] = attended_s[...]
    pair_s.start(0)

    hidden_trip.wait_recv()
    normalise(hidden, mod, 3, normed_t, scale_t, modulated_t)
    pair_t.start(0)
    loads[6].wait()
    project(modulated_t, wqt, packed_t)
    patch_row = lax.rem(lax.broadcasted_iota(jnp.int32, (TOKENS, TOKENS), 0), 16)
    patch_col = lax.rem(lax.broadcasted_iota(jnp.int32, (TOKENS, TOKENS), 1), 16)
    mask = patch_row == patch_col
    for h in range(HEADS):
        probs = probabilities(packed_t, h, mask)
        probs_t[h] = probs
        attend(probs.astype(BF16), packed_t, h, attended_t)
    project_out(attended_t, wot, branch_t)
    attended_trip.wait_recv()
    for h in range(HEADS):
        probs = probs_t[h]
        head_backward(probs, probs.astype(BF16), packed_t, d_attended, h, right_t)
    right_t[2, :, HE:] = attended_t[...]
    pair_t.start(2)
    project_back(right_t, wqt, d_modulated)
    loads[7].wait()
    cot_trip.wait_recv()
    d_offset, d_stretch = normalise_back(
        d_modulated, normed_t, scale_t, mod, 3, cot, grad_out
    )
    send_all(grad_trip)
    gated(cot, mod, 5, d_branch_t)
    pair_t.start(1)
    clip_first = held.at[0]
    clip_first[3:4, :] = d_offset
    clip_first[4:5, :] = d_stretch
    clip_first[5:6, :] = gate_sum(cot, branch_t)
    grad_hidden[here, :] = grad_out[here, :]
    for p in range(3):
        pair_t.wait_recv(p)
        pair_t.multiply(p, whole.at[1, p])
        sums_t[p].stage0()
    sums_t[0].stage1()

    grad_trip.wait_recv()
    gated(grad_hidden, mod, 2, d_branch_s)
    pair_s.start(1)
    d_attended[...] = dot(d_branch_s[...], wos[...], NT).astype(BF16)
    for h in range(HEADS):
        probs = probs_s[h]
        head_backward(probs, probs.astype(BF16), packed_s, d_attended, h, right_s)
    pair_s.start(2)
    project_back(right_s, wqs, d_modulated)
    sums_t[1].stage1()
    sums_t[2].stage1()
    sums_t[0].stage2()
    pair_s.wait_recv(0)
    pair_s.wait_recv(1)
    for p in (2, 1, 0):
        pair_s.multiply(p, whole.at[0, p])
        sums_s[p].stage0()
    d_offset, d_stretch = normalise_back(
        d_modulated, normed_s, scale_s, mod, 0, grad_hidden, lat
    )
    leave = pltpu.make_async_copy(lat, grad_latents, load_sem.at[8])
    leave.start()
    clip_first[0:1, :] = d_offset
    clip_first[1:2, :] = d_stretch
    clip_first[2:3, :] = gate_sum(grad_hidden, branch_s)
    clip_first[6:8, :] = jnp.zeros((2, D), F32)
    clip.start()
    sums_t[1].stage2()
    sums_t[0].stage3()
    for part in (*trips, pair_s, pair_t):
        part.wait_send()
    sums_t[2].stage2()
    for p in (2, 1, 0):
        sums_s[p].stage1()
    clip.step(0)
    sums_t[1].stage3()
    sums_t[2].stage3()
    for p in (2, 1, 0):
        sums_s[p].stage2()
    owned = [sums_t[0].stage4(), sums_t[1].stage4()]
    clip.step(1)
    for p in (2, 1, 0):
        sums_s[p].stage3()
    owned.append(sums_t[2].stage4())
    clip.step(2)
    for part in (*sums_s, *sums_t):
        part.wait_send()
    write_rows([sums.stage5(own) for sums, own in zip(sums_t, owned)], dqkv_t, dout_t)
    for part in sums_t:
        part.wait_send_last()
    clip.step(3)
    for i in range(6):
        moments[i] = held[4, i : i + 1, :]
    clip.wait_send()
    owned_s = [sums.stage4() for sums in sums_s]
    results_s = [sums.stage5(own) for sums, own in zip(sums_s, owned_s)]
    write_rows(results_s, dqkv_s, dout_s)
    for sums in sums_s:
        sums.wait_send_last()
    leave.wait()


def write_rows(results, dqkv, dout):
    for p, (low, high) in enumerate(results):
        dqkv[:, PART * p : PART * p + PART] = low
        start = 2 * HE + PART * p
        if p == 0:
            dqkv[:, start : start + PART] = high
        elif p == 1:
            dqkv[:, start:] = high[:, : PACKED - start]
            dout[:, : PART - (PACKED - start)] = high[:, PACKED - start :]
        else:
            dout[:, start - PACKED :] = high


def copy_out(*refs):
    for source, target in zip(refs[:6], refs[6:]):
        target[...] = source[...]


def local(latents, cotangent, modulation, spatial_qkv, spatial_out, temporal_qkv, temporal_out):
    vm = pl.BlockSpec(memory_space=pltpu.VMEM)
    hbm = pl.BlockSpec(memory_space=pl.ANY)
    sds = jax.ShapeDtypeStruct

    def bf16(*shape):
        return pltpu.VMEM(shape, BF16)

    def f32(*shape):
        return pltpu.VMEM(shape, F32)

    wide, wide32, column, narrow = bf16(TOKENS, D), f32(TOKENS, D), f32(TOKENS, 1), bf16(TOKENS, HE)
    three, wq, wo = bf16(TOKENS, PACKED), bf16(PACKED, D), bf16(HE, D)
    left, right = bf16(2, 2, TOKENS, D), bf16(4, TOKENS, 2 * HE)
    dma = pltpu.SemaphoreType.DMA
    shapes = [
        sds((TOKENS, D), BF16),
        sds((6, 1, D), F32),
        sds((9, PACKED), F32),
        sds((9, HE), F32),
        sds((9, PACKED), F32),
        sds((9, HE), F32),
    ]
    outs = pl.pallas_call(
        kernel,
        out_shape=shapes,
        in_specs=[hbm] * 7,
        out_specs=[hbm] + [vm] * 5,
        scratch_shapes=[
            wide, f32(6, 1, D), wq, wo, wq, wo,
            wide32, column, three, f32(HEADS, TOKENS, TOKENS), narrow, wide32, wide, wide,
            wide, wide32, column, three, f32(HEADS, TOKENS, TOKENS), narrow, wide32, wide, wide, narrow, narrow, wide,
            left, right, left, right,
            bf16(2, 3, 2, 4, SLAB, PART), bf16(2, 3, 2, 2, SLAB, PART), bf16(2, 3, 2, SLAB, PART),
            bf16(2, 3, 4, BLOCK, PART), bf16(2, 3, 3, BLOCK, PART), bf16(2, 3, 4, 16, PART + 128),
            bf16(2, 3, 4, 16, PART + 128), f32(2, 3, 16, PART), f32(2, 3, 16, PART),
            f32(5, 8, D), f32(4, 8, D),
            dma((9,)), dma((4, SEQ)), dma((4, SEQ)), dma((2, 3)), dma((2, 3)),
            dma((2, 3, 11)), dma((2, 3, 11)), dma((4,)), dma((4,)),
        ],
        compiler_params=pltpu.CompilerParams(
            collective_id=0, has_side_effects=True, vmem_limit_bytes=62 * 2**20
        ),
    )(
        latents.reshape(TOKENS, D), cotangent.reshape(TOKENS, D), modulation.transpose(1, 0, 2),
        spatial_qkv.T, spatial_out.T, temporal_qkv.T, temporal_out.T,
    )
    grad, moments, *grads = pl.pallas_call(
        copy_out,
        out_shape=shapes,
        in_specs=[vm] * 6,
        out_specs=[vm] * 6,
    )(*outs)
    return (grad.reshape(latents.shape), moments.transpose(1, 0, 2), *grads)


def solution(mesh):
    in_specs = (
        P("dp", "seq", None, None),
        P("dp", "seq", None, None),
        P("dp", None, None),
        P(),
        P(),
        P(),
        P(),
    )
    out_specs = (
        P("dp", "seq", None, None),
        P("dp", None, None),
        P(("dp", "seq"), None),
        P(("dp", "seq"), None),
        P(("dp", "seq"), None),
        P(("dp", "seq"), None),
    )
    return jax.shard_map(local, mesh=mesh, in_specs=in_specs, out_specs=out_specs, check_vma=False)
```

```python
import functools

import jax
import jax.numpy as jnp
from jax import lax
from jax.experimental import pallas as pl
from jax.experimental.pallas import tpu as pltpu
from jax.sharding import PartitionSpec as P

HEADS = 8
HEAD_DIM = 72
HE = HEADS * HEAD_DIM
PACKED = 3 * HE
D = 1152
TOKENS = 256
SEQ = 16
EPSILON = 1e-06
FACTOR = HEAD_DIM**-0.5
SLAB = 144
BLOCK = 80
PART = 384
MESH = pl.DeviceIdType.MESH
F32 = jnp.float32
BF16 = jnp.bfloat16

NN = (((1,), (0,)), ((), ()))
NT = (((1,), (1,)), ((), ()))
TN = (((0,), (0,)), ((), ()))


def dot(a, b, dims=NN):
    return lax.dot_general(a, b, dims, preferred_element_type=F32)


def rows_of(i, size):
    return pl.ds(pl.multiple_of(i * size, size), size)


def chunks(size=32):
    return [slice(i, i + size) for i in range(0, TOKENS, size)]


def normalise(source, mod, row, normed, scale, modulated):
    offset = mod[row]
    stretch = 1.0 + mod[row + 1]
    for rows in chunks():
        x = source[rows, :].astype(F32)
        centred = x - jnp.mean(x, axis=-1, keepdims=True)
        spread = jnp.mean(centred * centred, axis=-1, keepdims=True)
        inverse = lax.rsqrt(spread + EPSILON)
        n = centred * inverse
        normed[rows, :] = n
        scale[rows, :] = inverse
        modulated[rows, :] = (n * stretch + offset).astype(BF16)


def project(modulated, weight, packed):
    packed[...] = dot(modulated[...], weight[...], NT).astype(BF16)


def project_out(attended, weight, out):
    out[...] = dot(attended[...], weight[...])


def project_back(right, weight, out):
    total = dot(right[0], weight[: 2 * HE, :]) + dot(right[2, :, :HE], weight[2 * HE :, :])
    out[...] = total.astype(BF16)


def head(ref, h, section=0):
    lane = section * HE + h * HEAD_DIM
    return ref[:, lane : lane + HEAD_DIM]


def probabilities(packed, h, mask):
    scores = dot(head(packed, h, 1), head(packed, h, 0), NT)
    raised = jnp.exp(scores * FACTOR)
    if mask is not None:
        raised = jnp.where(mask, raised, 0.0)
    return raised * (1.0 / jnp.sum(raised, axis=0, keepdims=True))


def head_backward(probs, weights, packed, d_attended, h, right):
    d_head = head(d_attended, h)
    d_weights = dot(head(packed, h, 2), d_head, NT)
    carried = jnp.sum(d_weights * probs, axis=0, keepdims=True)
    d_scores = (probs * (d_weights - carried) * FACTOR).astype(BF16)
    lane = h * HEAD_DIM
    right[0, :, lane : lane + HEAD_DIM] = dot(d_scores, head(packed, h, 1), TN).astype(BF16)
    right[0, :, HE + lane : HE + lane + HEAD_DIM] = dot(d_scores, head(packed, h, 0)).astype(BF16)
    right[2, :, lane : lane + HEAD_DIM] = dot(weights, d_head).astype(BF16)


def attend(weights, packed, h, attended):
    lane = h * HEAD_DIM
    attended[:, lane : lane + HEAD_DIM] = dot(weights, head(packed, h, 2), TN).astype(BF16)


def fold(x):
    return sum(x[8 * i : 8 * i + 8] for i in range(x.shape[0] // 8))


def gated(source, mod, row, out):
    out[...] = (source[...].astype(F32) * mod[row]).astype(BF16)


def gate_sum(upstream, branch):
    total = jnp.zeros((8, D), F32)
    for rows in chunks():
        total = total + fold(upstream[rows, :].astype(F32) * branch[rows, :])
    return jnp.sum(total, axis=0, keepdims=True)


def normalise_back(d_modulated, normed, scale, mod, row, upstream, out):
    stretch = 1.0 + mod[row + 1]
    totals = [jnp.zeros((8, D), F32)] * 2
    for rows in chunks():
        g = d_modulated[rows, :].astype(F32)
        n = normed[rows, :]
        dn = g * stretch
        first = jnp.mean(dn, axis=-1, keepdims=True)
        second = jnp.mean(dn * n, axis=-1, keepdims=True)
        dx = scale[rows, :] * (dn - first - n * second)
        out[rows, :] = (upstream[rows, :].astype(F32) + dx).astype(BF16)
        totals = [total + fold(term) for total, term in zip(totals, (g, g * n))]
    return [jnp.sum(t, axis=0, keepdims=True) for t in totals]


def swap1(i):
    return i + 1 - 2 * lax.rem(i, 2)


class Place:
    def __init__(self):
        self.dp = lax.axis_index("dp")
        self.seq = lax.axis_index("seq")
        self.x = lax.rem(self.dp, 4)
        self.yh = lax.div(self.dp, 4)
        self.yl = lax.div(self.seq, 8)
        self.y = 2 * self.yh + self.yl
        self.z = lax.rem(lax.div(self.seq, 2), 4)
        self.core = lax.rem(self.seq, 2)

    def at(self, x=None, y=None, z=None, core=None):
        x = self.x if x is None else x
        y = self.y if y is None else y
        z = self.z if z is None else z
        core = self.core if core is None else core
        return {
            "dp": 4 * lax.div(y, 2) + x,
            "seq": 8 * lax.rem(y, 2) + 2 * z + core,
        }

    def pair(self, i):
        near, far = swap1(i), 3 - i
        return near + self.core * (far - near), far + self.core * (near - far)


def remote(src, dst, send, recv, device):
    return pltpu.make_async_remote_copy(
        src_ref=src, dst_ref=dst, send_sem=send, recv_sem=recv, device_id=device, device_id_type=MESH
    )


class PairTerms:
    def __init__(self, place, left, right, send, recv):
        self.core = place.core
        other = place.at(core=1 - place.core)
        away = 2 - 2 * place.core
        self.left, self.right = left, right
        self.copies = [
            remote(left.at[0, 0], left.at[0, 1], send.at[0], recv.at[0], other),
            remote(left.at[1, 0], left.at[1, 1], send.at[1], recv.at[1], other),
            remote(right.at[away], right.at[away + 1], send.at[2], recv.at[2], other),
        ]

    def start(self, i):
        if i == 1:
            pl.when(self.core == 0)(self.copies[1].start)
        else:
            self.copies[i].start()

    def wait_recv(self, part):
        if part == 0:
            self.copies[0].wait_recv()
            self.copies[2].wait_recv()
        elif part == 1:
            pl.when(self.core == 1)(self.copies[1].wait_recv)

    def wait_send(self):
        self.copies[0].wait_send()
        pl.when(self.core == 0)(self.copies[1].wait_send)
        self.copies[2].wait_send()

    def multiply(self, part, out):
        first = PART * part
        pieces = [(first, first + PART)]
        if part == 1:
            pieces = [(first, HE), (HE, first + PART)]
        for low, high in pieces:
            left = self.left[0 if high <= HE else self.core].reshape(2 * TOKENS, D)
            right = self.right[pl.ds(2 * self.core, 2), :, low:high].reshape(2 * TOKENS, high - low)
            total = dot(left, right, TN)
            for yh in range(2):
                for x in range(4):
                    row = SLAB * (4 * yh + x)
                    out[yh, x, :, low - first : high - first] = total[row : row + SLAB].astype(BF16)


class Reduction:
    def __init__(self, place, names, outer, whole, first, pair, half, second, quarter, third, final, other, send, recv):
        self.place, self.names = place, names
        self.whole, self.first, self.pair, self.half, self.second = whole, first, pair, half, second
        self.quarter, self.third, self.final, self.other = quarter, third, final, other
        self.at = [getattr(place, name) for name in names]
        a = self.at[0]
        a1, self.a2 = (3 - a, swap1(a)) if outer else place.pair(a)
        to_a1, to_a2 = place.at(**{names[0]: a1}), place.at(**{names[0]: self.a2})
        self.copies = [
            remote(whole.at[:, lax.rem(a + 2, 4)], first.at[1], send.at[0], recv.at[0], to_a1),
            remote(whole.at[:, a1], first.at[0], send.at[1], recv.at[1], to_a1),
            remote(whole.at[:, self.a2], pair, send.at[2], recv.at[2], to_a2),
        ]
        for j in range(1, 4):
            peer = lax.rem(self.at[1] + j, 4)
            self.copies.append(
                remote(half.at[peer], second.at[j - 1], send.at[2 + j], recv.at[2 + j], place.at(**{names[1]: peer}))
            )
        x, y, z = place.x, place.y, place.z
        owner = {n: getattr(place, m) for n, m in zip("xy", names)}
        came = dict(zip(names[:2], (x, y)))
        self.owns = [jnp.logical_and(jnp.logical_and(owner["x"] == x, owner["y"] == y), z == j) for j in range(4)]
        self.took = [
            jnp.logical_and(
                jnp.logical_and(getattr(place, names[0]) == x, getattr(place, names[1]) == y), self.at[2] == k
            )
            for k in range(4)
        ]
        self.out = [
            remote(
                quarter.at[j], third.at[self.at[2]], send.at[6 + j], recv.at[6 + self.at[2]],
                place.at(**owner, z=j),
            )
            for j in range(4)
        ]
        self.back = [
            remote(
                quarter.at[0], third.at[k], send.at[6 + k], recv.at[6 + k],
                place.at(**came, **{names[2]: k}),
            )
            for k in range(4)
        ]
        self.swap = remote(final, other, send.at[10], recv.at[10], place.at(core=1 - place.core))

    def start_out(self):
        for j in range(4):
            pl.when(jnp.logical_not(self.owns[j]))(self.out[j].start)

            @pl.when(self.owns[j])
            def _():
                self.third[self.at[2]] = self.quarter[j]

    def wait_back(self):
        for k in range(4):
            pl.when(jnp.logical_not(self.took[k]))(self.back[k].wait_recv)

    def stage0(self):
        self.copies[0].start()
        self.copies[1].start()

    def stage1(self):
        self.copies[0].wait_recv()
        for yh in range(2):
            kept = self.whole.at[yh, self.a2]
            kept[...] = (kept[...].astype(F32) + self.first[1, yh].astype(F32)).astype(BF16)
        self.copies[2].start()

    def stage2(self):
        self.copies[1].wait_recv()
        self.copies[2].wait_recv()
        for yh in range(2):
            total = self.whole[yh, self.at[0]].astype(F32) + self.first[0, yh].astype(F32)
            total = total + self.pair[yh].astype(F32)
            self.half[2 * yh, :72] = total[:72].astype(BF16)
            self.half[2 * yh + 1, :72] = total[72:].astype(BF16)
        for copy in self.copies[3:]:
            copy.start()

    def stage3(self):
        for copy in self.copies[3:]:
            copy.wait_recv()
        total = self.half[self.at[1]].astype(F32)
        for k in range(3):
            total = total + self.second[k].astype(F32)
        for j in range(4):
            main, rest = total[18 * j : 18 * j + 16], total[18 * j + 16 : 18 * j + 18]
            strips = [rest[:, 128 * i : 128 * i + 128] for i in range(3)]
            strips.append(jnp.zeros((10, 128), F32))
            self.quarter[j] = jnp.concatenate([main, jnp.concatenate(strips, axis=0)], axis=1).astype(BF16)
        self.start_out()

    def stage4(self):
        self.wait_back()
        total = self.third[0].astype(F32)
        for k in range(1, 4):
            total = total + self.third[k].astype(F32)
        total = total * (1.0 / 8)
        strips = [total[2 * i : 2 * i + 2, PART:] for i in range(3)]
        rows = [total[:, :PART], jnp.concatenate(strips, axis=1), jnp.zeros((6, PART), F32)]
        rows, core = jnp.concatenate(rows, axis=0), self.place.core
        self.final[...] = pltpu.roll(rows, lax.rem(24 - 9 * (1 - core), 24), 0)[:16]
        self.swap.start()
        return pltpu.roll(rows, lax.rem(24 - 9 * core, 24), 0)[:16]

    def stage5(self, own):
        self.swap.wait_recv()
        low = self.place.core == 0
        theirs = self.other[...]
        return jnp.where(low, own, theirs)[:9], jnp.where(low, theirs, own)[:9]

    def wait_send(self):
        for copy in self.copies:
            copy.wait_send()

    def wait_send_last(self):
        for j in range(4):
            pl.when(jnp.logical_not(self.owns[j]))(self.out[j].wait_send)
        self.swap.wait_send()


class ClipSum:
    def __init__(self, place, held, arrived, send, recv):
        self.held, self.arrived = held, arrived
        devices = [
            place.at(core=1 - place.core),
            place.at(z=swap1(place.z)),
            place.at(z=3 - place.z),
            place.at(y=swap1(place.y)),
        ]
        self.copies = [
            remote(held.at[i], arrived.at[i], send.at[i], recv.at[i], device)
            for i, device in enumerate(devices)
        ]

    def start(self):
        self.copies[0].start()

    def step(self, i):
        self.copies[i].wait_recv()
        self.held[i + 1] = self.held[i] + self.arrived[i]
        if i < 3:
            self.copies[i + 1].start()

    def wait_send(self):
        for copy in self.copies:
            copy.wait_send()


class Exchange:
    def __init__(self, source, target, send, recv):
        self.source, self.target, self.send, self.recv = source, target, send, recv
        self.me = lax.axis_index("seq")

    def to(self, j):
        peer = lax.rem(self.me + j, SEQ)
        return pltpu.make_async_remote_copy(
            src_ref=self.source.at[rows_of(peer, 16)],
            dst_ref=self.target.at[rows_of(self.me, 16)],
            send_sem=self.send.at[j],
            recv_sem=self.recv.at[j],
            device_id={"seq": peer},
            device_id_type=MESH,
        )

    def start(self, j):
        self.to(j).start()

    def wait_recv(self):
        for j in range(1, SEQ):
            sender = lax.rem(self.me + SEQ - j, SEQ)
            pltpu.make_async_remote_copy(
                src_ref=self.source.at[rows_of(sender, 16)],
                dst_ref=self.target.at[rows_of(sender, 16)],
                send_sem=self.send.at[j],
                recv_sem=self.recv.at[j],
                device_id={"seq": sender},
                device_id_type=MESH,
            ).wait_recv()

    def wait_send(self):
        for j in range(1, SEQ):
            self.to(j).wait_send()


def kernel(
    lat_hbm, cot_hbm, mod_hbm, wqs_hbm, wos_hbm, wqt_hbm, wot_hbm,
    grad_latents, moments, dqkv_s, dout_s, dqkv_t, dout_t,
    lat, mod, wqs, wos, wqt, wot,
    normed_s, scale_s, packed_s, probs_s, attended_s, branch_s, hidden_out, hidden,
    cot, normed_t, scale_t, packed_t, probs_t, attended_t, branch_t, grad_out, grad_hidden, d_attended_out, d_attended, d_modulated,
    left_s, right_s, left_t, right_t,
    whole, first, pair, half, second, quarter, third, final, other,
    held, arrived,
    load_sem, send_sem, recv_sem, pair_send, pair_recv, sum_send, sum_recv, clip_send, clip_recv,
):
    place = Place()
    me = place.seq
    here = rows_of(me, 16)
    modulated_s, d_branch_s = left_s.at[0, 0], left_s.at[1, 0]
    modulated_t, d_branch_t = left_t.at[0, 0], left_t.at[1, 0]
    loads = [
        pltpu.make_async_copy(src, dst, load_sem.at[i])
        for i, (src, dst) in enumerate(
            [
                (lat_hbm, lat), (mod_hbm, mod), (wqs_hbm, wqs), (wos_hbm, wos), (cot_hbm, grad_out), (wot_hbm, wot),
                (wqt_hbm, wqt), (cot_hbm.at[here], cot.at[here]),
            ]
        )
    ]
    for load in loads[:3]:
        load.start()

    barrier = pltpu.get_barrier_semaphore()

    def signal(device):
        pl.semaphore_signal(barrier, inc=1, device_id=device, device_id_type=MESH)

    def greet(j, _):
        signal({"seq": lax.rem(me + j, SEQ)})
        return 0

    lax.fori_loop(1, SEQ, greet, 0)
    for j in range(1, 4):
        for k in range(4):
            signal(place.at(x=lax.rem(place.x + j, 4), z=k))
    for k in range(4):
        signal(place.at(y=lax.rem(place.y + 2, 4), z=k))
        signal(place.at(y=3 - place.y, z=k))

    @pl.when(place.x != place.y)
    def _():
        for k in range(4):
            signal(place.at(x=place.y, y=place.x, z=k))

    loads[0].wait()
    loads[1].wait()
    normalise(lat, mod, 0, normed_s, scale_s, modulated_s)
    trips = [
        Exchange(source, target, send_sem.at[i], recv_sem.at[i])
        for i, (source, target) in enumerate(
            [(cot_hbm, cot), (hidden_out, hidden), (grad_out, grad_hidden), (d_attended_out, d_attended)]
        )
    ]
    cot_trip, hidden_trip, grad_trip, attended_trip = trips
    pair_s = PairTerms(place, left_s, right_s, pair_send.at[0], pair_recv.at[0])
    pair_t = PairTerms(place, left_t, right_t, pair_send.at[1], pair_recv.at[1])
    sums_s, sums_t = [
        [
            Reduction(
                place, names[p], l == 1 and p == 2, whole.at[l, p], first.at[l, p], pair.at[l, p], half.at[l, p], second.at[l, p],
                quarter.at[l, p], third.at[l, p], final.at[l, p], other.at[l, p],
                sum_send.at[l, p], sum_recv.at[l, p],
            )
            for p in range(3)
        ]
        for l, names in enumerate((("xzy", "yxz", "zyx"), ("xzy", "xzy", "yxz")))
    ]
    clip = ClipSum(place, held, arrived, clip_send, clip_recv)

    def send_all(trip):
        for j in range(1, SEQ):
            trip.start(j)

    loads[2].wait()
    for load in loads[3:]:
        load.start()
    project(modulated_s, wqs, packed_s)
    for h in range(HEADS):
        probs = probabilities(packed_s, h, None)
        probs_s[h] = probs
        attend(probs.astype(BF16), packed_s, h, attended_s)
    loads[3].wait()
    project_out(attended_s, wos, branch_s)
    for rows in chunks():
        hidden_out[rows, :] = (lat[rows, :].astype(F32) + mod[2] * branch_s[rows, :]).astype(BF16)
    pl.semaphore_wait(barrier, SEQ + 19 + jnp.where(place.x == place.y, 0, 4))
    send_all(hidden_trip)
    loads[4].wait()
    loads[5].wait()
    gated(grad_out, mod, 5, d_modulated)
    d_attended_out[...] = dot(d_modulated[...], wot[...], NT).astype(BF16)
    send_all(attended_trip)
    send_all(cot_trip)
    d_attended[here, :] = d_attended_out[here, :]
    hidden[here, :] = hidden_out[here, :]
    right_s[2, :, HE:] = attended_s[...]
    pair_s.start(0)

    hidden_trip.wait_recv()
    normalise(hidden, mod, 3, normed_t, scale_t, modulated_t)
    pair_t.start(0)
    loads[6].wait()
    project(modulated_t, wqt, packed_t)
    patch_row = lax.rem(lax.broadcasted_iota(jnp.int32, (TOKENS, TOKENS), 0), 16)
    patch_col = lax.rem(lax.broadcasted_iota(jnp.int32, (TOKENS, TOKENS), 1), 16)
    mask = patch_row == patch_col
    for h in range(HEADS):
        probs = probabilities(packed_t, h, mask)
        probs_t[h] = probs
        attend(probs.astype(BF16), packed_t, h, attended_t)
    project_out(attended_t, wot, branch_t)
    attended_trip.wait_recv()
    for h in range(HEADS):
        probs = probs_t[h]
        head_backward(probs, probs.astype(BF16), packed_t, d_attended, h, right_t)
    right_t[2, :, HE:] = attended_t[...]
    pair_t.start(2)
    project_back(right_t, wqt, d_modulated)
    loads[7].wait()
    cot_trip.wait_recv()
    d_offset, d_stretch = normalise_back(
        d_modulated, normed_t, scale_t, mod, 3, cot, grad_out
    )
    send_all(grad_trip)
    gated(cot, mod, 5, d_branch_t)
    pair_t.start(1)
    clip_first = held.at[0]
    clip_first[3:4, :] = d_offset
    clip_first[4:5, :] = d_stretch
    clip_first[5:6, :] = gate_sum(cot, branch_t)
    grad_hidden[here, :] = grad_out[here, :]
    for p in range(3):
        pair_t.wait_recv(p)
        pair_t.multiply(p, whole.at[1, p])
        sums_t[p].stage0()
    sums_t[0].stage1()

    grad_trip.wait_recv()
    gated(grad_hidden, mod, 2, d_branch_s)
    pair_s.start(1)
    d_attended[...] = dot(d_branch_s[...], wos[...], NT).astype(BF16)
    for h in range(HEADS):
        probs = probs_s[h]
        head_backward(probs, probs.astype(BF16), packed_s, d_attended, h, right_s)
    pair_s.start(2)
    project_back(right_s, wqs, d_modulated)
    sums_t[1].stage1()
    sums_t[2].stage1()
    sums_t[0].stage2()
    pair_s.wait_recv(0)
    pair_s.wait_recv(1)
    for p in (2, 1, 0):
        pair_s.multiply(p, whole.at[0, p])
        sums_s[p].stage0()
    d_offset, d_stretch = normalise_back(
        d_modulated, normed_s, scale_s, mod, 0, grad_hidden, lat
    )
    leave = pltpu.make_async_copy(lat, grad_latents, load_sem.at[8])
    leave.start()
    clip_first[0:1, :] = d_offset
    clip_first[1:2, :] = d_stretch
    clip_first[2:3, :] = gate_sum(grad_hidden, branch_s)
    clip_first[6:8, :] = jnp.zeros((2, D), F32)
    clip.start()
    sums_t[1].stage2()
    sums_t[0].stage3()
    for part in (*trips, pair_s, pair_t):
        part.wait_send()
    sums_t[2].stage2()
    for p in (2, 1, 0):
        sums_s[p].stage1()
    clip.step(0)
    sums_t[1].stage3()
    sums_t[2].stage3()
    for p in (2, 1, 0):
        sums_s[p].stage2()
    owned = [sums_t[0].stage4(), sums_t[1].stage4()]
    clip.step(1)
    for p in (2, 1, 0):
        sums_s[p].stage3()
    owned.append(sums_t[2].stage4())
    clip.step(2)
    for part in (*sums_s, *sums_t):
        part.wait_send()
    write_rows([sums.stage5(own) for sums, own in zip(sums_t, owned)], dqkv_t, dout_t)
    for part in sums_t:
        part.wait_send_last()
    clip.step(3)
    for i in range(6):
        moments[i] = held[4, i : i + 1, :]
    clip.wait_send()
    owned_s = [sums.stage4() for sums in sums_s]
    results_s = [sums.stage5(own) for sums, own in zip(sums_s, owned_s)]
    write_rows(results_s, dqkv_s, dout_s)
    for sums in sums_s:
        sums.wait_send_last()
    leave.wait()


def write_rows(results, dqkv, dout):
    for p, (low, high) in enumerate(results):
        dqkv[:, PART * p : PART * p + PART] = low
        start = 2 * HE + PART * p
        if p == 0:
            dqkv[:, start : start + PART] = high
        elif p == 1:
            dqkv[:, start:] = high[:, : PACKED - start]
            dout[:, : PART - (PACKED - start)] = high[:, PACKED - start :]
        else:
            dout[:, start - PACKED :] = high


def copy_out(*refs):
    for source, target in zip(refs[:6], refs[6:]):
        target[...] = source[...]


def local(latents, cotangent, modulation, spatial_qkv, spatial_out, temporal_qkv, temporal_out):
    vm = pl.BlockSpec(memory_space=pltpu.VMEM)
    hbm = pl.BlockSpec(memory_space=pl.ANY)
    sds = jax.ShapeDtypeStruct

    def bf16(*shape):
        return pltpu.VMEM(shape, BF16)

    def f32(*shape):
        return pltpu.VMEM(shape, F32)

    wide, wide32, column, narrow = bf16(TOKENS, D), f32(TOKENS, D), f32(TOKENS, 1), bf16(TOKENS, HE)
    three, wq, wo = bf16(TOKENS, PACKED), bf16(PACKED, D), bf16(HE, D)
    left, right = bf16(2, 2, TOKENS, D), bf16(4, TOKENS, 2 * HE)
    dma = pltpu.SemaphoreType.DMA
    shapes = [
        sds((TOKENS, D), BF16),
        sds((6, 1, D), F32),
        sds((9, PACKED), F32),
        sds((9, HE), F32),
        sds((9, PACKED), F32),
        sds((9, HE), F32),
    ]
    outs = pl.pallas_call(
        kernel,
        out_shape=shapes,
        in_specs=[hbm] * 7,
        out_specs=[hbm] + [vm] * 5,
        scratch_shapes=[
            wide, f32(6, 1, D), wq, wo, wq, wo,
            wide32, column, three, f32(HEADS, TOKENS, TOKENS), narrow, wide32, wide, wide,
            wide, wide32, column, three, f32(HEADS, TOKENS, TOKENS), narrow, wide32, wide, wide, narrow, narrow, wide,
            left, right, left, right,
            bf16(2, 3, 2, 4, SLAB, PART), bf16(2, 3, 2, 2, SLAB, PART), bf16(2, 3, 2, SLAB, PART),
            bf16(2, 3, 4, BLOCK, PART), bf16(2, 3, 3, BLOCK, PART), bf16(2, 3, 4, 16, PART + 128),
            bf16(2, 3, 4, 16, PART + 128), f32(2, 3, 16, PART), f32(2, 3, 16, PART),
            f32(5, 8, D), f32(4, 8, D),
            dma((9,)), dma((4, SEQ)), dma((4, SEQ)), dma((2, 3)), dma((2, 3)),
            dma((2, 3, 11)), dma((2, 3, 11)), dma((4,)), dma((4,)),
        ],
        compiler_params=pltpu.CompilerParams(
            collective_id=0, has_side_effects=True, vmem_limit_bytes=62 * 2**20
        ),
    )(
        latents.reshape(TOKENS, D), cotangent.reshape(TOKENS, D), modulation.transpose(1, 0, 2),
        spatial_qkv.T, spatial_out.T, temporal_qkv.T, temporal_out.T,
    )
    grad, moments, *grads = pl.pallas_call(
        copy_out,
        out_shape=shapes,
        in_specs=[vm] * 6,
        out_specs=[vm] * 6,
    )(*outs)
    return (grad.reshape(latents.shape), moments.transpose(1, 0, 2), *grads)


def solution(mesh):
    in_specs = (
        P("dp", "seq", None, None),
        P("dp", "seq", None, None),
        P("dp", None, None),
        P(),
        P(),
        P(),
        P(),
    )
    out_specs = (
        P("dp", "seq", None, None),
        P("dp", None, None),
        P(("dp", "seq"), None),
        P(("dp", "seq"), None),
        P(("dp", "seq"), None),
        P(("dp", "seq"), None),
    )
    return jax.shard_map(local, mesh=mesh, in_specs=in_specs, out_specs=out_specs, check_vma=False)
```
